32 devices in a mesh: gx: 8 (over y, x, core), gy: 4 (over z).
Axes of the slice: x: 2, y: 2, z: 4, core: 2. Of those that a mesh axis runs over, the one named last changes fastest.
Arguments:
- fields: float32 [4, 128, 64, 128], P(None, 'gx', 'gy'), may hold values from -6 to 6
- factor_x: float32 [128, 32], P('gx'), may hold values from -0.75 to 0.75
- factor_y: float32 [64, 32], P('gy'), may hold values from -1 to 1
Outputs:
- advanced: float32 [4, 128, 64, 128], P(None, 'gx', 'gy')
- core_tensor: float32 [4, 32, 32, 128], P(None, 'gx', 'gy')
- rebuilt: float32 [4, 128, 64, 128], P(None, 'gx', 'gy')
The draws below stay inside these ranges and needn't reach their ends.
All inputs are finite; a program needn't handle non-finite values.
Results may differ from the reference program's by a relative error of at most 0.000082.
Values sent between devices are 32-bit elements; how exact they have to be, the bound alone decides.
No kernel may reach another device: no remote copies, remote signals or barrier semaphores. Data moves between devices by JAX's collectives and lax.ppermute only.
A program may use at most 64 MiB of HBM per device.

```python
import jax
import jax.numpy as jnp
from jax import lax

NZ = 128
RANK = 32
FIELDS = 4
NX = 128
NY = 64


def strengthened(result, own_key, source, target, shards_of, factor):
    def block_of(position):
        return (jnp.arange(result.shape[position]) // (result.shape[position] // shards_of)).reshape((-1,) + (1,) * (result.ndim - 1 - position))

    one_side = jax.random.permutation(own_key, shards_of)[block_of(target)]
    second = (block_of(target) + shards_of // 2) % shards_of
    return jnp.where((block_of(source) == one_side) | (block_of(source) == second), factor * result, result)


def levels(rng, extent, shards, least, top_value):
    gain = 1.0
    for dim, shards_of in shards:
        steps = jax.random.uniform(jax.random.fold_in(jax.random.fold_in(rng, 6), dim), (shards_of,), jnp.float32, least / len(shards), top_value / len(shards))
        gain = gain * jnp.repeat(jnp.exp(steps), extent[dim] // shards_of).reshape((-1,) + (1,) * (len(extent) - 1 - dim))
    return gain


def noise(key, shape, spread, bound, pieces=(), dtype=jnp.bfloat16):
    entries = spread * jax.random.normal(key, shape, jnp.float32)
    if pieces:
        entries = entries * levels(key, shape, pieces, -0.22, 0.18)
    return jnp.clip(entries, -bound, bound).astype(dtype)


def heavy_noise(key, extent, width, most, cuts, heavy, dtype=jnp.bfloat16):
    drawn = width * jax.random.normal(key, extent, jnp.float32)
    if cuts:
        drawn = drawn * levels(key, extent, cuts, -0.22, 0.18)
    return jnp.clip(strengthened(drawn, jax.random.fold_in(key, 3), *heavy), -most, most).astype(dtype)


def setup_inputs(seed: int = 0) -> dict:
    splits = jax.random.split(jax.random.key(seed), 4)
    return {
        "fields": noise(splits[0], (FIELDS, NX, NY, NZ), 1.0, 6.0, ((1, 8), (2, 4)), jnp.float32),
        "factor_x": heavy_noise(splits[1], (NX, RANK), NX ** -0.5, 0.75, ((0, 8),), (0, 1, 8, 2.0), jnp.float32),
        "factor_y": heavy_noise(splits[2], (NY, RANK), NY ** -0.5, 1.0, ((0, 4),), (0, 1, 4, 2.0), jnp.float32),
    }


TIME_STEP = 0.2
REACT_RATE = 0.5
HEAT_RELEASE = 1.0


def derivative(flux_field, axis):
    def pair(shift):
        return jnp.roll(flux_field, -shift, axis) - jnp.roll(flux_field, shift, axis)
    return (45.0 * pair(1) - 9.0 * pair(2) + pair(3)) / 60.0


def tendency(state):
    pressure = 0.5 * state[3]
    flux_x = state[0][None] * state
    flux_x = flux_x.at[0].add(pressure)
    flux_y = state[1][None] * state
    flux_y = flux_y.at[1].add(pressure)
    react = REACT_RATE * state[2] * (1.0 + jnp.tanh(state[3]))
    zeros = jnp.zeros_like(react)
    source = jnp.stack([zeros, zeros, -react, HEAT_RELEASE * react])
    return source - derivative(flux_x, 1) - derivative(flux_y, 2)


def reference(fields, factor_x, factor_y):
    high = lax.Precision.HIGHEST
    z_width = min(NZ, 16)
    n_blocks = NZ // z_width
    rescale = (float(NX) * float(NY)) ** 0.5 / RANK

    def one_block(state):
        section_one = state + TIME_STEP * tendency(state)
        section_two = 0.75 * state + 0.25 * (section_one + TIME_STEP * tendency(section_one))
        advanced = (1.0 / 3.0) * state + (2.0 / 3.0) * (section_two + TIME_STEP * tendency(section_two))
        partial_value = jnp.einsum("fxyz,xa->fayz", advanced, factor_x, precision=high)
        core_tensor = jnp.einsum("fayz,yb->fabz", partial_value, factor_y, precision=high)
        columns = jnp.einsum("fabz,yb->fayz", core_tensor, factor_y, precision=high)
        rebuilt = rescale * jnp.einsum("fayz,xa->fxyz", columns, factor_x, precision=high)
        return advanced, core_tensor, rebuilt

    blocks = jnp.moveaxis(fields.reshape(FIELDS, NX, NY, n_blocks, z_width), 3, 0)
    adv_blocks, core_blocks, rebuilt_blocks = lax.map(one_block, blocks)

    def joined(stacked):
        shape = stacked.shape
        return jnp.moveaxis(stacked, 0, 3).reshape(shape[1], shape[2], shape[3], NZ)

    return joined(adv_blocks), joined(core_blocks), joined(rebuilt_blocks)
```

```python
import functools
import math

import jax
import jax.numpy as jnp
from jax import lax
from jax.experimental import pallas as pl
from jax.experimental.pallas import tpu as pltpu
from jax.sharding import PartitionSpec as P

TIME_STEP = 0.2
REACT_RATE = 0.5
HEAT_RELEASE = 1.0
SUBLANES = 8
LANES = 128


def fits(mesh, fields, factor_x, factor_y):
    n_f, n_x, n_y, n_z = fields.shape
    count_x, count_y = mesh.shape["gx"], mesh.shape["gy"]
    devices = count_x * count_y
    rank = factor_x.shape[1]
    if n_x % count_x or n_y % count_y or n_z % devices:
        return False
    block_x, block_y, block_z = n_x // count_x, n_y // count_y, n_z // devices
    return (
        n_x == LANES
        and n_z == LANES
        and block_x * SUBLANES == LANES
        and block_x == 2 * SUBLANES
        and block_y == 2 * SUBLANES
        and 2 * block_z == SUBLANES
        and count_x == SUBLANES
        and factor_y.shape[1] == rank
        and 4 * rank == LANES
        and rank == count_y * SUBLANES
        and rank % count_x == 0
        and 2 * (rank // count_x) * n_f * block_z == LANES
    )


def exchange(blocks, stride):
    blocks = list(blocks)
    lane = lax.broadcasted_iota(jnp.int32, (SUBLANES, LANES), 1)
    step = 1
    while step < len(blocks):
        width = stride * step
        upper = (lane & width) != 0
        for i in range(len(blocks)):
            if i & step:
                continue
            low, high = blocks[i], blocks[i + step]
            blocks[i] = jnp.where(upper, pltpu.roll(high, width, 1), low)
            blocks[i + step] = jnp.where(upper, high, pltpu.roll(low, LANES - width, 1))
        step *= 2
    return blocks


def pack_kernel(block_x, block_y, fields_ref, factor_x_ref, factor_y_ref, out_ref):
    n_f = fields_ref.shape[0]
    tiles = LANES // SUBLANES
    sub = lax.broadcasted_iota(jnp.int32, (tiles, SUBLANES, LANES), 1)
    lower = sub < SUBLANES // 2
    half = SUBLANES // 2
    for f in range(n_f):
        turned = []
        for octet in range(2):
            rows = [
                fields_ref[f, pl.ds(octet * SUBLANES + y, block_x, stride=block_y), :]
                for y in range(SUBLANES)
            ]
            matrix = jnp.concatenate(rows, axis=0)
            turned.append(matrix.T.reshape(tiles, SUBLANES, LANES))
        first, second = turned
        at = pl.ds(f * SUBLANES, SUBLANES)
        out_ref[:, 0, at, :] = jnp.where(lower, first, pltpu.roll(second, half, 1))
        out_ref[:, 1, at, :] = jnp.where(lower, pltpu.roll(first, half, 1), second)
    factors = jnp.concatenate(
        [
            factor_x_ref[0:SUBLANES, :],
            factor_x_ref[SUBLANES:, :],
            factor_y_ref[0:SUBLANES, :],
            factor_y_ref[SUBLANES:, :],
        ],
        axis=1,
    )
    out_ref[:, :, n_f * SUBLANES :, :] = jnp.broadcast_to(
        factors[None, None], (tiles, 2, SUBLANES, LANES)
    )


def split(value):
    high = value.astype(jnp.bfloat16)
    low = (value - high.astype(jnp.float32)).astype(jnp.bfloat16)
    return high, low


def mul(a, b):
    return jnp.dot(a, b, preferred_element_type=jnp.float32)


def mul_split(a, b):
    return mul(a[0], b[0]) + (mul(a[0], b[1]) + mul(a[1], b[0]))


def main_kernel(n_f, count_x, count_y, rank, rescale, in_ref, out_ref, ext_a, ext_b, ext_c, adv):
    half = SUBLANES // 2
    margin = 3
    inner = pl.ds(margin, SUBLANES)
    lower = lax.broadcasted_iota(jnp.int32, (margin, SUBLANES, LANES), 1) < half

    def fill_margins(ext):
        for f in range(n_f):
            head = [pltpu.roll(ext[f, s, margin : 2 * margin], half, 1) for s in range(count_y)]
            tail = [pltpu.roll(ext[f, s, SUBLANES : SUBLANES + margin], half, 1) for s in range(count_y)]
            for s in range(count_y):
                ext[f, s, 0:margin] = jnp.where(lower, tail[s - 1], tail[s])
                ext[f, s, SUBLANES + margin :] = jnp.where(lower, head[s], head[(s + 1) % count_y])

    def section(ext, store):
        def one(s, carry):
            padded = [ext[f, s] for f in range(n_f)]
            center = [p[margin : margin + SUBLANES] for p in padded]
            react = REACT_RATE * center[2] * (1.0 + jnp.tanh(center[3]))
            for f in range(n_f):
                flux_y = padded[1] * padded[f]
                if f == 1:
                    flux_y = flux_y + 0.5 * padded[3]
                flux_x = center[0] * center[f]
                if f == 0:
                    flux_x = flux_x + 0.5 * center[3]

                def along_y(k):
                    ahead = flux_y[margin + k : margin + k + SUBLANES]
                    return ahead - flux_y[margin - k : margin - k + SUBLANES]

                def along_x(k):
                    return pltpu.roll(flux_x, LANES - k, 2) - pltpu.roll(flux_x, k, 2)

                change = (
                    45.0 * (along_x(1) + along_y(1))
                    - 9.0 * (along_x(2) + along_y(2))
                    + (along_x(3) + along_y(3))
                ) * (-1.0 / 60.0)
                if f == 2:
                    change = change - react
                if f == 3:
                    change = change + HEAT_RELEASE * react
                store(f, s, center[f], change)
            return carry

        lax.fori_loop(0, count_y, one, 0)

    for s in range(count_y):
        for f in range(n_f):
            got = [in_ref[i, s, f * SUBLANES : (f + 1) * SUBLANES, :] for i in range(count_x)]
            for y, block in enumerate(exchange(got, LANES // SUBLANES)):
                ext_a[f, s, margin + y] = block
    fill_margins(ext_a)

    def first(f, s, center, change):
        ext_b[f, s, inner] = center + TIME_STEP * change

    def second(f, s, center, change):
        ext_c[f, s, inner] = 0.75 * ext_a[f, s, inner] + 0.25 * (center + TIME_STEP * change)

    def third(f, s, center, change):
        adv[f, s] = (1.0 / 3.0) * ext_a[f, s, inner] + (2.0 / 3.0) * (center + TIME_STEP * change)

    section(ext_a, first)
    fill_margins(ext_b)
    section(ext_b, second)
    fill_margins(ext_c)
    section(ext_c, third)

    at = pl.ds(n_f * SUBLANES, SUBLANES)
    group = n_f * half
    wide = rank * group
    held_x = split(jnp.concatenate([in_ref[i, 0, at, :] for i in range(count_x)], axis=0))
    row = lax.broadcasted_iota(jnp.int32, (LANES, wide), 0)
    col = lax.broadcasted_iota(jnp.int32, (LANES, wide), 1)

    def spread(part):
        pieces = []
        for octet in range(2):
            picks = (row - octet * rank == col // group).astype(jnp.bfloat16)
            pieces.append(mul(part, picks).reshape(count_x, 1, SUBLANES, wide))
        return jnp.concatenate(pieces, axis=1).reshape(LANES, wide)

    spread_x = [spread(part) for part in held_x]
    turned_x = [part.T for part in spread_x]
    plane = count_y * SUBLANES * SUBLANES
    total = None
    lane_f = (lax.broadcasted_iota(jnp.int32, (LANES, wide), 1) // half) % n_f
    for f in range(n_f):
        weights = [jnp.where(lane_f == f, part, 0.0).astype(jnp.bfloat16) for part in spread_x]
        term = mul_split(split(adv[f].reshape(plane, LANES)), weights)
        total = term if total is None else total + term
    row_z = lax.broadcasted_iota(jnp.int32, (plane, wide), 0) % half
    col_z = lax.broadcasted_iota(jnp.int32, (plane, wide), 1) % half
    same_z = row_z == col_z
    partial = split(jnp.where(same_z, total, 0.0))

    held_y = split(jnp.concatenate([in_ref[0, s, at, :] for s in range(count_y)], axis=0))
    rows_y = count_y * SUBLANES
    picks = lax.broadcasted_iota(jnp.int32, (plane, rows_y), 0) // SUBLANES
    picks = (picks == lax.broadcasted_iota(jnp.int32, (plane, rows_y), 1)).astype(jnp.bfloat16)
    row_octet = (lax.broadcasted_iota(jnp.int32, (plane, LANES), 0) // half) % 2
    col_octet = lax.broadcasted_iota(jnp.int32, (plane, LANES), 1) // rank - 2
    spread_y = [jnp.where(row_octet == col_octet, mul(picks, part), 0.0) for part in held_y]
    weights_y = [part.astype(jnp.bfloat16) for part in spread_y]
    turned_y = [part.T.astype(jnp.bfloat16) for part in spread_y]
    halves = mul_split(turned_y, partial)
    core = halves[2 * rank : 3 * rank] + halves[3 * rank :]

    for s in range(count_y):
        for i in range(count_x):
            place = i * (LANES // 2)
            block = core[s * SUBLANES : (s + 1) * SUBLANES, place // LANES * LANES : place // LANES * LANES + LANES]
            if place % LANES:
                block = pltpu.roll(block, LANES // 2, 1)
            out_ref[i, s, 2 * n_f * SUBLANES :, :] = block

    doubled = jnp.concatenate([jnp.zeros((2 * rank, wide), jnp.float32), core, core], axis=0)
    columns = mul_split(weights_y, split(doubled))
    columns = split(jnp.where(same_z, rescale * columns, 0.0))
    row_f = (lax.broadcasted_iota(jnp.int32, (wide, LANES), 0) // half) % n_f

    def send(block, f, s, first_row):
        parts = exchange([block[y] for y in range(SUBLANES)], LANES // SUBLANES)
        for i in range(count_x):
            out_ref[i, s, first_row + f * SUBLANES : first_row + (f + 1) * SUBLANES, :] = parts[i]

    for f in range(n_f):
        weights = [jnp.where(row_f == f, part, 0.0).astype(jnp.bfloat16) for part in turned_x]
        rebuilt = mul_split(columns, weights).reshape(count_y, SUBLANES, SUBLANES, LANES)
        for s in range(count_y):
            send(adv[f, s], f, s, 0)
            send(rebuilt[s], f, s, n_f * SUBLANES)


def unpack_kernel(n_f, block_x, block_y, in_ref, advanced_ref, core_ref, rebuilt_ref):
    half = SUBLANES // 2
    tiles = LANES // SUBLANES
    lower = lax.broadcasted_iota(jnp.int32, (tiles, SUBLANES, LANES), 1) < half
    for target, first_row in ((advanced_ref, 0), (rebuilt_ref, n_f * SUBLANES)):
        for f in range(n_f):
            at = pl.ds(first_row + f * SUBLANES, SUBLANES)
            even, odd = in_ref[:, 0, at, :], in_ref[:, 1, at, :]
            first = jnp.where(lower, even, pltpu.roll(odd, half, 1))
            second = jnp.where(lower, pltpu.roll(even, half, 1), odd)
            for octet, part in enumerate((first, second)):
                turned = part.reshape(LANES, LANES).T
                for y in range(SUBLANES):
                    rows = pl.ds(octet * SUBLANES + y, block_x, stride=block_y)
                    target[f, rows, :] = turned[y * block_x : (y + 1) * block_x]
    at = pl.ds(2 * n_f * SUBLANES, SUBLANES)
    count = 2 * tiles
    lane = lax.broadcasted_iota(jnp.int32, (SUBLANES, LANES), 1)
    upper = lane >= LANES // 2
    got = [in_ref[d // 2, d % 2, at, :] for d in range(count)]
    kept = [
        jnp.where(upper, pltpu.roll(got[d + tiles], LANES // 2, 1), got[d]) for d in range(tiles)
    ]
    for place, block in enumerate(exchange(kept, half)):
        core_ref[place % n_f, place // n_f] = block


def z_plan(fields, factor_x, factor_y):
    n_f, block_x, block_y, n_z = fields.shape
    rank = factor_x.shape[1]
    count_x = lax.axis_size("gx")
    count_y = lax.axis_size("gy")
    devices = count_x * count_y
    pairs = devices // 2
    rows_in = (n_f + 1) * SUBLANES
    rows_out = (2 * n_f + 1) * SUBLANES
    rescale = math.sqrt(float(block_x * count_x) * float(block_y * count_y)) / rank
    params = pltpu.CompilerParams(vmem_limit_bytes=48 * 1024 * 1024)
    vmem = pl.BlockSpec(memory_space=pltpu.VMEM)
    f32 = jnp.float32

    packed = pl.pallas_call(
        functools.partial(pack_kernel, block_x, block_y),
        out_shape=jax.ShapeDtypeStruct((pairs, 2, rows_in, n_z), f32),
        in_specs=[vmem] * 3,
        out_specs=vmem,
        compiler_params=params,
        name="pack",
    )(fields.reshape(n_f, block_x * block_y, n_z), factor_x, factor_y)
    planes = lax.all_to_all(
        packed.reshape(devices, rows_in, n_z), ("gx", "gy"), 0, 0, tiled=True
    )
    extended = pltpu.VMEM((n_f, count_y, SUBLANES + 6, SUBLANES, LANES), f32)
    results = pl.pallas_call(
        functools.partial(main_kernel, n_f, count_x, count_y, rank, rescale),
        out_shape=jax.ShapeDtypeStruct((count_x, count_y, rows_out, n_z), f32),
        in_specs=[vmem],
        out_specs=vmem,
        scratch_shapes=[
            extended,
            extended,
            extended,
            pltpu.VMEM((n_f, count_y, SUBLANES, SUBLANES, LANES), f32),
        ],
        compiler_params=params,
        name="sections",
    )(planes.reshape(count_x, count_y, rows_in, n_z))
    back = lax.all_to_all(
        results.reshape(devices, rows_out, n_z), ("gx", "gy"), 0, 0, tiled=True
    )
    flat = jax.ShapeDtypeStruct((n_f, block_x * block_y, n_z), f32)
    core = jax.ShapeDtypeStruct((n_f, rank // count_x, rank // count_y, n_z), f32)
    advanced, core_tensor, rebuilt = pl.pallas_call(
        functools.partial(unpack_kernel, n_f, block_x, block_y),
        out_shape=(flat, core, flat),
        in_specs=[vmem],
        out_specs=(vmem, vmem, vmem),
        compiler_params=params,
        name="unpack",
    )(back.reshape(pairs, 2, rows_out, n_z))
    return advanced.reshape(fields.shape), core_tensor, rebuilt.reshape(fields.shape)


def extended(block, sides, width):
    for axis, dim in sides:
        count = lax.axis_size(axis)
        forward = [(i, i + 1) for i in range(count - 1)]
        forward.append((count - 1, 0))
        backward = [(target, source) for source, target in forward]
        low = lax.ppermute(
            lax.slice_in_dim(block, block.shape[dim] - width, None, axis=dim), axis, forward
        )
        high = lax.ppermute(lax.slice_in_dim(block, 0, width, axis=dim), axis, backward)
        block = jnp.concatenate([low, block, high], axis=dim)
    return block


def inner_part(array, margin):
    return array[:, margin : array.shape[1] - margin, margin : array.shape[2] - margin]


def tendency(padded):
    n_x = padded.shape[1]
    n_y = padded.shape[2]
    pressure = 0.5 * padded[3]
    flux_x = padded[0][None] * padded
    flux_x = flux_x.at[0].add(pressure)
    flux_y = padded[1][None] * padded
    flux_y = flux_y.at[1].add(pressure)

    def along_x(shift):
        return (
            flux_x[:, 3 + shift : n_x - 3 + shift, 3 : n_y - 3]
            - flux_x[:, 3 - shift : n_x - 3 - shift, 3 : n_y - 3]
        )

    def along_y(shift):
        return (
            flux_y[:, 3 : n_x - 3, 3 + shift : n_y - 3 + shift]
            - flux_y[:, 3 : n_x - 3, 3 - shift : n_y - 3 - shift]
        )

    deriv_x = (45.0 * along_x(1) - 9.0 * along_x(2) + along_x(3)) / 60.0
    deriv_y = (45.0 * along_y(1) - 9.0 * along_y(2) + along_y(3)) / 60.0
    center = inner_part(padded, 3)
    react = REACT_RATE * center[2] * (1.0 + jnp.tanh(center[3]))
    zeros = jnp.zeros_like(react)
    source = jnp.stack([zeros, zeros, -react, HEAT_RELEASE * react])
    return source - deriv_x - deriv_y


def section_tendency(state):
    padded = extended(state, (("gx", 1), ("gy", 2)), 3)
    return tendency(padded)


def per_device(fields, factor_x, factor_y):
    high = lax.Precision.HIGHEST
    section_one = fields + TIME_STEP * section_tendency(fields)
    section_two = 0.75 * fields + 0.25 * (section_one + TIME_STEP * section_tendency(section_one))
    advanced = 1.0 / 3.0 * fields + 2.0 / 3.0 * (
        section_two + TIME_STEP * section_tendency(section_two)
    )
    rank_full = factor_x.shape[1]
    count_x = lax.axis_size("gx")
    count_y = lax.axis_size("gy")
    partial_x = jnp.einsum("fxyz,xa->fayz", advanced, factor_x, precision=high)
    partial_value = lax.psum_scatter(partial_x, "gx", scatter_dimension=1, tiled=True)
    local_core = jnp.einsum("fayz,yb->fabz", partial_value, factor_y, precision=high)
    core_tensor = lax.psum_scatter(local_core, "gy", scatter_dimension=2, tiled=True)
    weights = factor_y
    columns = jnp.einsum(
        "fabz,yb->fayz",
        lax.all_gather(core_tensor, "gy", axis=2, tiled=True),
        weights,
        precision=high,
    )
    weights = factor_x
    expanded = jnp.einsum(
        "fayz,xa->fxyz", lax.all_gather(columns, "gx", axis=1, tiled=True), weights, precision=high
    )
    total_x = factor_x.shape[0] * count_x
    total_y = factor_y.shape[0] * count_y
    rescale = math.sqrt(float(total_x) * float(total_y)) / rank_full
    rebuilt = rescale * expanded
    return (advanced, core_tensor, rebuilt)


def solution(mesh):
    placed = (P(None, "gx", "gy", None), P("gx", None), P("gy", None))
    out = P(None, "gx", "gy", None)

    def whole(fields, factor_x, factor_y):
        plan = z_plan if fits(mesh, fields, factor_x, factor_y) else per_device
        return jax.shard_map(
            plan, mesh=mesh, in_specs=placed, out_specs=(out, out, out), check_vma=False
        )(fields, factor_x, factor_y)

    return whole
```

```python
import functools
import math

import jax
import jax.numpy as jnp
from jax import lax
from jax.experimental import pallas as pl
from jax.experimental.pallas import tpu as pltpu
from jax.sharding import PartitionSpec as P

TIME_STEP = 0.2
REACT_RATE = 0.5
HEAT_RELEASE = 1.0
SUBLANES = 8
LANES = 128
HALF = SUBLANES // 2


def fits(mesh, fields, factor_x, factor_y):
    n_f, n_x, n_y, n_z = fields.shape
    count_x, count_y = mesh.shape["gx"], mesh.shape["gy"]
    devices = count_x * count_y
    rank = factor_x.shape[1]
    if n_x % count_x or n_y % count_y or n_z % devices:
        return False
    block_x, block_y, block_z = n_x // count_x, n_y // count_y, n_z // devices
    return (
        n_x == LANES
        and n_z == LANES
        and n_f == HALF
        and block_z == HALF
        and block_x == 2 * SUBLANES
        and block_y == 2 * SUBLANES
        and count_x == SUBLANES
        and count_y == HALF
        and rank == count_y * SUBLANES
        and factor_y.shape[1] == rank
        and n_f * rank == LANES
    )


def exchange(blocks, stride):
    blocks = list(blocks)
    lane = lax.broadcasted_iota(jnp.int32, (SUBLANES, LANES), 1)
    step = 1
    while step < len(blocks):
        width = stride * step
        upper = (lane & width) != 0
        for i in range(len(blocks)):
            if i & step:
                continue
            low, high = blocks[i], blocks[i + step]
            blocks[i] = jnp.where(upper, pltpu.roll(high, width, 1), low)
            blocks[i + step] = jnp.where(upper, high, pltpu.roll(low, LANES - width, 1))
        step *= 2
    return blocks


def pack_kernel(fields_hbm, factor_x_hbm, factor_y_hbm, out_ref, fields_ref, x_ref, y_ref, sems):
    n_f, rows, _ = fields_ref.shape
    block_x = x_ref.shape[0]
    block_y = rows // block_x
    tiles = LANES // SUBLANES
    copies = [
        pltpu.make_async_copy(fields_hbm.at[f], fields_ref.at[f], sems.at[f]) for f in range(n_f)
    ]
    copies.append(pltpu.make_async_copy(factor_x_hbm, x_ref, sems.at[n_f]))
    copies.append(pltpu.make_async_copy(factor_y_hbm, y_ref, sems.at[n_f + 1]))
    for copy in copies:
        copy.start()
    for f in range(n_f):
        copies[f].wait()
        for octet in range(2):
            matrix = jnp.concatenate(
                [
                    fields_ref[f, pl.ds(octet * SUBLANES + y, block_x, stride=block_y), :]
                    for y in range(SUBLANES)
                ],
                axis=0,
            )
            turned = matrix.T.reshape(tiles, SUBLANES, LANES)
            out_ref[:, 0, 2 * f + octet] = turned[:, :HALF]
            out_ref[:, 1, 2 * f + octet] = turned[:, HALF:]
    copies[n_f].wait()
    copies[n_f + 1].wait()
    part_x = lax.axis_index("gy")
    part_y = lax.rem(lax.axis_index("gx"), block_y // HALF)
    own_x = x_ref[pl.ds(part_x * HALF, HALF), :]
    own_y = y_ref[pl.ds(part_y * HALF, HALF), :]
    factors = jnp.concatenate([own_x, own_y, own_y, own_y], axis=1)
    out_ref[:, :, 2 * n_f] = jnp.broadcast_to(factors[None, None], (tiles, 2, HALF, LANES))


def split(value):
    high = value.astype(jnp.bfloat16)
    low = (value - high.astype(jnp.float32)).astype(jnp.bfloat16)
    return high, low


def mul(a, b, dims=((1,), (0,))):
    return lax.dot_general(a, b, (dims, ((), ())), preferred_element_type=jnp.float32)


def mul_split(a, b, dims=((1,), (0,))):
    return mul(a[0], b[0], dims) + (mul(a[0], b[1], dims) + mul(a[1], b[0], dims))


def main_kernel(n_f, count_x, count_y, rank, rescale, in_ref, out_ref, ext_a, ext_b, ext_c, adv):
    margin = 3
    inner = pl.ds(margin, SUBLANES)
    lower = lax.broadcasted_iota(jnp.int32, (margin, SUBLANES, LANES), 1) < HALF

    def each(body):
        def step(s, carry):
            body(s)
            return carry

        lax.fori_loop(0, count_y, step, 0)

    def fill_margins(ext):
        def one(s):
            before = lax.rem(s + count_y - 1, count_y)
            after = lax.rem(s + 1, count_y)
            for f in range(n_f):
                old = ext[before, f, pl.ds(SUBLANES, margin)]
                own = ext[s, f, pl.ds(SUBLANES, margin)]
                ext[s, f, 0:margin] = pltpu.roll(jnp.where(lower, own, old), HALF, 1)
                own = ext[s, f, pl.ds(margin, margin)]
                new = ext[after, f, pl.ds(margin, margin)]
                ext[s, f, pl.ds(SUBLANES + margin, margin)] = pltpu.roll(
                    jnp.where(lower, new, own), HALF, 1
                )

        each(one)

    row = lax.broadcasted_iota(jnp.int32, (LANES, LANES), 0)
    col = lax.broadcasted_iota(jnp.int32, (LANES, LANES), 1)
    ahead = (row - col) & (LANES - 1)
    taps = jnp.zeros((LANES, LANES), jnp.float32)
    for shift, weight in ((1, 45.0), (2, -9.0), (3, 1.0)):
        taps = jnp.where(ahead == shift, weight, taps)
        taps = jnp.where(ahead == LANES - shift, -weight, taps)
    taps = taps.astype(jnp.bfloat16)
    taps = jnp.concatenate([taps, taps], axis=0)

    def section(ext, step, store):
        def one(s):
            padded = [ext[s, f] for f in range(n_f)]
            center = [p[margin : margin + SUBLANES] for p in padded]
            flux_x = [center[0] * c for c in center]
            flux_x[0] = flux_x[0] + 0.5 * center[3]
            flat = jnp.concatenate(flux_x, axis=0).reshape(n_f * SUBLANES * SUBLANES, LANES)
            along_x = mul(jnp.concatenate(split(flat), axis=1), taps)
            along_x = along_x.reshape(n_f, SUBLANES, SUBLANES, LANES)
            react = (step * REACT_RATE) * center[2] * (1.0 + jnp.tanh(center[3]))
            for f in range(n_f):
                flux_y = padded[1] * padded[f]
                if f == 1:
                    flux_y = flux_y + 0.5 * padded[3]

                def along_y(k):
                    after = flux_y[margin + k : margin + k + SUBLANES]
                    return after - flux_y[margin - k : margin - k + SUBLANES]

                change = (
                    (-45.0 * step / 60.0) * along_y(1)
                    + (9.0 * step / 60.0) * along_y(2)
                    + (-step / 60.0) * (along_y(3) + along_x[f])
                )
                if f == 2:
                    change = change - react
                if f == 3:
                    change = change + HEAT_RELEASE * react
                store(s, f, center[f], change)

        each(one)

    def arrive(s):
        for f in range(n_f):
            got = [
                in_ref[i, s, 2 * f : 2 * f + 2].reshape(SUBLANES, LANES) for i in range(count_x)
            ]
            for y, block in enumerate(exchange(got, LANES // SUBLANES)):
                ext_a[s, f, margin + y] = block

    def send(block, s, f, base):
        parts = exchange([block[y] for y in range(SUBLANES)], LANES // SUBLANES)
        for i, part in enumerate(parts):
            out_ref[i, s, base + 2 * f : base + 2 * f + 2] = part.reshape(2, HALF, LANES)

    def first(s, f, center, change):
        ext_b[s, f, inner] = center + change

    def second(s, f, center, change):
        ext_c[s, f, inner] = 0.75 * ext_a[s, f, inner] + (0.25 * center + change)

    def third(s, f, center, change):
        done = (1.0 / 3.0) * ext_a[s, f, inner] + ((2.0 / 3.0) * center + change)
        adv[f, s] = done
        send(done, s, f, 0)

    each(arrive)
    fill_margins(ext_a)
    section(ext_a, TIME_STEP, first)
    fill_margins(ext_b)
    section(ext_b, 0.25 * TIME_STEP, second)
    fill_margins(ext_c)
    section(ext_c, 2.0 / 3.0 * TIME_STEP, third)

    plane = count_y * SUBLANES * SUBLANES
    held = in_ref[:, :, 2 * n_f].reshape(LANES, LANES)
    held_x = split(held)
    held_y = split(jnp.where(col < rank, pltpu.roll(held, LANES - rank, 1), held))
    picks = (row == col // n_f).astype(jnp.bfloat16)
    spread_x = [mul(part, picks) for part in held_x]
    weights_x = [
        jnp.concatenate(
            [jnp.where(col % n_f == f, part, 0.0).astype(jnp.bfloat16) for f in range(n_f)], axis=0
        )
        for part in spread_x
    ]
    r = lax.broadcasted_iota(jnp.int32, (plane, LANES), 0)
    c = lax.broadcasted_iota(jnp.int32, (plane, LANES), 1)
    from_s, from_y = r // (SUBLANES * SUBLANES), (r // HALF) % 2 * SUBLANES + (r // SUBLANES) % SUBLANES
    block_x = LANES // count_x
    held_at = from_y // HALF * block_x + from_s * HALF + from_y % HALF
    picks = (held_at == c).astype(jnp.bfloat16)
    same_z = r % HALF == c // rank
    weights_y = [jnp.where(same_z, mul(picks, part), 0.0).astype(jnp.bfloat16) for part in held_y]

    def by_x(value):
        return jnp.concatenate([value[f].reshape(plane, LANES) for f in range(n_f)], axis=1)

    partial = mul_split(split(by_x(adv)), weights_x)
    core = mul_split(weights_y, split(partial), ((0,), (0,)))
    columns = split(rescale * mul_split(weights_y, split(core)))

    left = lax.broadcasted_iota(jnp.int32, (SUBLANES, LANES), 1) < LANES // 2
    for s in range(count_y):
        tiles = [core[z * rank + s * SUBLANES : z * rank + (s + 1) * SUBLANES] for z in range(HALF)]
        tiles = exchange(exchange(tiles, 1), LANES // SUBLANES)
        for i in range(count_x):
            tile = tiles[i % HALF]
            turned = pltpu.roll(tile, LANES // 2, 1)
            if i >= HALF:
                tile, turned = turned, tile
            out_ref[i, s, 4 * n_f] = jnp.where(left[:HALF], tile[:HALF], turned[HALF:])

    for f in range(n_f):
        weights = [part[f * LANES : (f + 1) * LANES] for part in weights_x]
        adv[f] = mul_split(columns, weights, ((1,), (1,))).reshape(adv.shape[1:])

    def depart(s):
        for f in range(n_f):
            send(adv[f, s], s, f, 2 * n_f)

    each(depart)


def unpack_kernel(block_x, block_y, in_ref, advanced_ref, core_ref, rebuilt_ref):
    n_f = advanced_ref.shape[0]
    tiles = LANES // SUBLANES
    for target, base in ((advanced_ref, 0), (rebuilt_ref, 2 * n_f)):
        for f in range(n_f):
            for octet in range(2):
                place = base + 2 * f + octet
                matrix = jnp.concatenate([in_ref[:, 0, place], in_ref[:, 1, place]], axis=1)
                turned = matrix.reshape(LANES, LANES).T
                for y in range(SUBLANES):
                    rows = pl.ds(octet * SUBLANES + y, block_x, stride=block_y)
                    target[f, rows, :] = turned[y * block_x : (y + 1) * block_x]
    upper = lax.broadcasted_iota(jnp.int32, (SUBLANES, LANES), 1) >= LANES // 2
    got = []
    for d in range(2 * tiles):
        block = in_ref[d // 2, d % 2, 4 * n_f]
        got.append(jnp.concatenate([block, pltpu.roll(block, LANES // 2, 1)], axis=0))
    kept = [
        jnp.where(upper, pltpu.roll(got[d + tiles], LANES // 2, 1), got[d]) for d in range(tiles)
    ]
    a_count = core_ref.shape[1]
    for place, block in enumerate(exchange(kept, HALF)):
        core_ref[place // a_count, place % a_count] = block


def z_plan(fields, factor_x, factor_y):
    n_f, block_x, block_y, n_z = fields.shape
    rank = factor_x.shape[1]
    count_x = lax.axis_size("gx")
    count_y = lax.axis_size("gy")
    devices = count_x * count_y
    pairs = devices // 2
    tiles_in = 2 * n_f + 1
    tiles_out = 4 * n_f + 1
    rescale = math.sqrt(float(block_x * count_x) * float(block_y * count_y)) / rank
    params = pltpu.CompilerParams(vmem_limit_bytes=48 * 1024 * 1024)
    vmem = pl.BlockSpec(memory_space=pltpu.VMEM)
    hbm = pl.BlockSpec(memory_space=pl.ANY)
    f32 = jnp.float32

    packed = pl.pallas_call(
        pack_kernel,
        out_shape=jax.ShapeDtypeStruct((pairs, 2, tiles_in, HALF, n_z), f32),
        in_specs=[hbm] * 3,
        out_specs=vmem,
        scratch_shapes=[
            pltpu.VMEM((n_f, block_x * block_y, n_z), f32),
            pltpu.VMEM(factor_x.shape, f32),
            pltpu.VMEM(factor_y.shape, f32),
            pltpu.SemaphoreType.DMA((n_f + 2,)),
        ],
        compiler_params=params,
        name="pack",
    )(fields.reshape(n_f, block_x * block_y, n_z), factor_x, factor_y)
    planes = lax.all_to_all(
        packed.reshape(devices, tiles_in, HALF, n_z), ("gx", "gy"), 0, 0, tiled=True
    )
    extended = pltpu.VMEM((count_y, n_f, SUBLANES + 6, SUBLANES, LANES), f32)
    results = pl.pallas_call(
        functools.partial(main_kernel, n_f, count_x, count_y, rank, rescale),
        out_shape=jax.ShapeDtypeStruct((count_x, count_y, tiles_out, HALF, n_z), f32),
        in_specs=[vmem],
        out_specs=vmem,
        scratch_shapes=[
            extended,
            extended,
            extended,
            pltpu.VMEM((n_f, count_y, SUBLANES, SUBLANES, LANES), f32),
        ],
        compiler_params=params,
        name="sections",
    )(planes.reshape(count_x, count_y, tiles_in, HALF, n_z))
    back = lax.all_to_all(
        results.reshape(devices, tiles_out, HALF, n_z), ("gx", "gy"), 0, 0, tiled=True
    )
    flat = jax.ShapeDtypeStruct((n_f, block_x * block_y, n_z), f32)
    core = jax.ShapeDtypeStruct((n_f, rank // count_x, rank // count_y, n_z), f32)
    advanced, core_tensor, rebuilt = pl.pallas_call(
        functools.partial(unpack_kernel, block_x, block_y),
        out_shape=(flat, core, flat),
        in_specs=[vmem],
        out_specs=(vmem, vmem, vmem),
        compiler_params=params,
        name="unpack",
    )(back.reshape(pairs, 2, tiles_out, HALF, n_z))
    return advanced.reshape(fields.shape), core_tensor, rebuilt.reshape(fields.shape)


def extended(block, sides, width):
    for axis, dim in sides:
        count = lax.axis_size(axis)
        forward = [(i, i + 1) for i in range(count - 1)]
        forward.append((count - 1, 0))
        backward = [(target, source) for source, target in forward]
        low = lax.ppermute(
            lax.slice_in_dim(block, block.shape[dim] - width, None, axis=dim), axis, forward
        )
        high = lax.ppermute(lax.slice_in_dim(block, 0, width, axis=dim), axis, backward)
        block = jnp.concatenate([low, block, high], axis=dim)
    return block


def inner_part(array, margin):
    return array[:, margin : array.shape[1] - margin, margin : array.shape[2] - margin]


def tendency(padded):
    n_x = padded.shape[1]
    n_y = padded.shape[2]
    pressure = 0.5 * padded[3]
    flux_x = padded[0][None] * padded
    flux_x = flux_x.at[0].add(pressure)
    flux_y = padded[1][None] * padded
    flux_y = flux_y.at[1].add(pressure)

    def along_x(shift):
        return (
            flux_x[:, 3 + shift : n_x - 3 + shift, 3 : n_y - 3]
            - flux_x[:, 3 - shift : n_x - 3 - shift, 3 : n_y - 3]
        )

    def along_y(shift):
        return (
            flux_y[:, 3 : n_x - 3, 3 + shift : n_y - 3 + shift]
            - flux_y[:, 3 : n_x - 3, 3 - shift : n_y - 3 - shift]
        )

    deriv_x = (45.0 * along_x(1) - 9.0 * along_x(2) + along_x(3)) / 60.0
    deriv_y = (45.0 * along_y(1) - 9.0 * along_y(2) + along_y(3)) / 60.0
    center = inner_part(padded, 3)
    react = REACT_RATE * center[2] * (1.0 + jnp.tanh(center[3]))
    zeros = jnp.zeros_like(react)
    source = jnp.stack([zeros, zeros, -react, HEAT_RELEASE * react])
    return source - deriv_x - deriv_y


def section_tendency(state):
    padded = extended(state, (("gx", 1), ("gy", 2)), 3)
    return tendency(padded)


def per_device(fields, factor_x, factor_y):
    high = lax.Precision.HIGHEST
    section_one = fields + TIME_STEP * section_tendency(fields)
    section_two = 0.75 * fields + 0.25 * (section_one + TIME_STEP * section_tendency(section_one))
    advanced = 1.0 / 3.0 * fields + 2.0 / 3.0 * (
        section_two + TIME_STEP * section_tendency(section_two)
    )
    rank_full = factor_x.shape[1]
    count_x = lax.axis_size("gx")
    count_y = lax.axis_size("gy")
    partial_x = jnp.einsum("fxyz,xa->fayz", advanced, factor_x, precision=high)
    partial_value = lax.psum_scatter(partial_x, "gx", scatter_dimension=1, tiled=True)
    local_core = jnp.einsum("fayz,yb->fabz", partial_value, factor_y, precision=high)
    core_tensor = lax.psum_scatter(local_core, "gy", scatter_dimension=2, tiled=True)
    weights = factor_y
    columns = jnp.einsum(
        "fabz,yb->fayz",
        lax.all_gather(core_tensor, "gy", axis=2, tiled=True),
        weights,
        precision=high,
    )
    weights = factor_x
    expanded = jnp.einsum(
        "fayz,xa->fxyz", lax.all_gather(columns, "gx", axis=1, tiled=True), weights, precision=high
    )
    total_x = factor_x.shape[0] * count_x
    total_y = factor_y.shape[0] * count_y
    rescale = math.sqrt(float(total_x) * float(total_y)) / rank_full
    rebuilt = rescale * expanded
    return (advanced, core_tensor, rebuilt)


def solution(mesh):
    placed = (P(None, "gx", "gy", None), P("gx", None), P("gy", None))
    out = P(None, "gx", "gy", None)

    def whole(fields, factor_x, factor_y):
        plan = z_plan if fits(mesh, fields, factor_x, factor_y) else per_device
        return jax.shard_map(
            plan, mesh=mesh, in_specs=placed, out_specs=(out, out, out), check_vma=False
        )(fields, factor_x, factor_y)

    return whole
```

```python
import functools
import math

import jax
import jax.numpy as jnp
from jax import lax
from jax.experimental import pallas as pl
from jax.experimental.pallas import tpu as pltpu
from jax.sharding import PartitionSpec as P

TIME_STEP = 0.2
REACT_RATE = 0.5
HEAT_RELEASE = 1.0
SUBLANES = 8
LANES = 128
HALF = SUBLANES // 2


def fits(mesh, fields, factor_x, factor_y):
    n_f, n_x, n_y, n_z = fields.shape
    count_x, count_y = mesh.shape["gx"], mesh.shape["gy"]
    devices = count_x * count_y
    rank = factor_x.shape[1]
    if n_x % count_x or n_y % count_y or n_z % devices:
        return False
    block_x, block_y, block_z = n_x // count_x, n_y // count_y, n_z // devices
    return (
        n_x == LANES
        and n_z == LANES
        and n_f == HALF
        and block_z == HALF
        and block_x == 2 * SUBLANES
        and block_y == 2 * SUBLANES
        and count_x == SUBLANES
        and count_y == HALF
        and rank == count_y * SUBLANES
        and factor_y.shape[1] == rank
        and n_f * rank == LANES
    )


def exchange(blocks, stride):
    count = len(blocks)
    period = stride * count
    group = lax.broadcasted_iota(jnp.int32, (SUBLANES, LANES), 1) // stride % count
    if period == LANES:
        blocks = [pltpu.roll(b, i * stride, 1) if i else b for i, b in enumerate(blocks)]
        step = 1
        while step < count:
            taken = (group & step) != 0
            blocks = [
                jnp.where(taken, blocks[(i + step) % count], blocks[i]) for i in range(count)
            ]
            step *= 2
        blocks = [blocks[-j % count] for j in range(count)]
        return [pltpu.roll(b, LANES - j * stride, 1) if j else b for j, b in enumerate(blocks)]
    blocks = list(blocks)
    step = 1
    while step < count:
        upper = (group & step) != 0
        for i in range(count):
            if i & step:
                continue
            low, high = blocks[i], blocks[i + step]
            blocks[i] = jnp.where(upper, pltpu.roll(high, stride * step, 1), low)
            blocks[i + step] = jnp.where(upper, high, pltpu.roll(low, LANES - stride * step, 1))
        step *= 2
    return blocks


def pack_kernel(fields_hbm, factor_x_hbm, factor_y_hbm, out_ref, fields_ref, x_ref, y_ref, sems):
    n_f, rows, _ = fields_ref.shape
    block_x = x_ref.shape[0]
    block_y = rows // block_x
    tiles = LANES // SUBLANES
    copies = [
        pltpu.make_async_copy(fields_hbm.at[f], fields_ref.at[f], sems.at[f]) for f in range(n_f)
    ]
    copies.append(pltpu.make_async_copy(factor_x_hbm, x_ref, sems.at[n_f]))
    copies.append(pltpu.make_async_copy(factor_y_hbm, y_ref, sems.at[n_f + 1]))
    for copy in copies:
        copy.start()
    for f in range(n_f):
        copies[f].wait()
        for octet in range(2):
            matrix = jnp.concatenate(
                [
                    fields_ref[f, pl.ds(octet * SUBLANES + y, block_x, stride=block_y), :]
                    for y in range(SUBLANES)
                ],
                axis=0,
            )
            turned = matrix.T.reshape(tiles, SUBLANES, LANES)
            out_ref[:, 0, 2 * f + octet] = turned[:, :HALF]
            out_ref[:, 1, 2 * f + octet] = turned[:, HALF:]
    copies[n_f].wait()
    copies[n_f + 1].wait()
    part_x = lax.axis_index("gy")
    part_y = lax.rem(lax.axis_index("gx"), block_y // HALF)
    own_x = x_ref[pl.ds(part_x * HALF, HALF), :]
    own_y = y_ref[pl.ds(part_y * HALF, HALF), :]
    factors = jnp.concatenate([own_x, own_y, own_y, own_y], axis=1)
    out_ref[:, :, 2 * n_f] = jnp.broadcast_to(factors[None, None], (tiles, 2, HALF, LANES))


def split(value):
    high = value.astype(jnp.bfloat16)
    low = (value - high.astype(jnp.float32)).astype(jnp.bfloat16)
    return high, low


def mul(a, b, dims=((1,), (0,))):
    return lax.dot_general(a, b, (dims, ((), ())), preferred_element_type=jnp.float32)


def mul_split(a, b, dims=((1,), (0,))):
    return mul(a[0], b[0], dims) + (mul(a[0], b[1], dims) + mul(a[1], b[0], dims))


def main_kernel(n_f, count_x, count_y, rank, rescale, in_ref, out_ref, ext_a, ext_b, ext_c, adv):
    margin = 3
    inner = pl.ds(margin, SUBLANES)
    lower = lax.broadcasted_iota(jnp.int32, (margin, SUBLANES, LANES), 1) < HALF

    def each(body):
        def step(s, carry):
            body(s)
            return carry

        lax.fori_loop(0, count_y, step, 0, unroll=True)

    def fill_margins(ext):
        def one(s):
            before = lax.rem(s + count_y - 1, count_y)
            after = lax.rem(s + 1, count_y)
            for f in range(n_f):
                old = ext[before, f, pl.ds(SUBLANES, margin)]
                own = ext[s, f, pl.ds(SUBLANES, margin)]
                ext[s, f, 0:margin] = pltpu.roll(jnp.where(lower, own, old), HALF, 1)
                own = ext[s, f, pl.ds(margin, margin)]
                new = ext[after, f, pl.ds(margin, margin)]
                ext[s, f, pl.ds(SUBLANES + margin, margin)] = pltpu.roll(
                    jnp.where(lower, new, own), HALF, 1
                )

        each(one)

    row = lax.broadcasted_iota(jnp.int32, (LANES, LANES), 0)
    col = lax.broadcasted_iota(jnp.int32, (LANES, LANES), 1)
    ahead = (row - col) & (LANES - 1)
    taps = jnp.zeros((LANES, LANES), jnp.float32)
    for shift, weight in ((1, 45.0), (2, -9.0), (3, 1.0)):
        taps = jnp.where(ahead == shift, weight, taps)
        taps = jnp.where(ahead == LANES - shift, -weight, taps)
    taps = taps.astype(jnp.bfloat16)
    taps = jnp.concatenate([taps, taps], axis=0)

    def section(ext, step, store):
        def one(s):
            padded = [ext[s, f] for f in range(n_f)]
            center = [p[margin : margin + SUBLANES] for p in padded]
            flux_x = [center[0] * c for c in center]
            flux_x[0] = flux_x[0] + 0.5 * center[3]
            flat = jnp.concatenate(flux_x, axis=0).reshape(n_f * SUBLANES * SUBLANES, LANES)
            along_x = mul(jnp.concatenate(split(flat), axis=1), taps)
            along_x = along_x.reshape(n_f, SUBLANES, SUBLANES, LANES)
            react = (step * REACT_RATE) * center[2] * (1.0 + jnp.tanh(center[3]))
            for f in range(n_f):
                flux_y = padded[1] * padded[f]
                if f == 1:
                    flux_y = flux_y + 0.5 * padded[3]

                def along_y(k):
                    after = flux_y[margin + k : margin + k + SUBLANES]
                    return after - flux_y[margin - k : margin - k + SUBLANES]

                change = (
                    (-45.0 * step / 60.0) * along_y(1)
                    + (9.0 * step / 60.0) * along_y(2)
                    + (-step / 60.0) * (along_y(3) + along_x[f])
                )
                if f == 2:
                    change = change - react
                if f == 3:
                    change = change + HEAT_RELEASE * react
                store(s, f, center[f], change)

        each(one)

    def arrive(s):
        for f in range(n_f):
            got = [
                in_ref[i, s, 2 * f : 2 * f + 2].reshape(SUBLANES, LANES) for i in range(count_x)
            ]
            for y, block in enumerate(exchange(got, LANES // SUBLANES)):
                ext_a[s, f, margin + y] = block

    def send(block, s, f, base):
        parts = exchange([block[y] for y in range(SUBLANES)], LANES // SUBLANES)
        for i, part in enumerate(parts):
            out_ref[i, s, base + 2 * f : base + 2 * f + 2] = part.reshape(2, HALF, LANES)

    def first(s, f, center, change):
        ext_b[s, f, inner] = center + change

    def second(s, f, center, change):
        ext_c[s, f, inner] = 0.75 * ext_a[s, f, inner] + (0.25 * center + change)

    def third(s, f, center, change):
        done = (1.0 / 3.0) * ext_a[s, f, inner] + ((2.0 / 3.0) * center + change)
        adv[f, s] = done
        send(done, s, f, 0)

    each(arrive)
    fill_margins(ext_a)
    section(ext_a, TIME_STEP, first)
    fill_margins(ext_b)
    section(ext_b, 0.25 * TIME_STEP, second)
    fill_margins(ext_c)
    section(ext_c, 2.0 / 3.0 * TIME_STEP, third)

    plane = count_y * SUBLANES * SUBLANES
    held = in_ref[:, :, 2 * n_f].reshape(LANES, LANES)
    held_x = split(held)
    held_y = split(jnp.where(col < rank, pltpu.roll(held, LANES - rank, 1), held))
    picks = (row == col // n_f).astype(jnp.bfloat16)
    spread_x = [mul(part, picks) for part in held_x]
    weights_x = [
        jnp.concatenate(
            [jnp.where(col % n_f == f, part, 0.0).astype(jnp.bfloat16) for f in range(n_f)], axis=0
        )
        for part in spread_x
    ]
    r = lax.broadcasted_iota(jnp.int32, (plane, LANES), 0)
    c = lax.broadcasted_iota(jnp.int32, (plane, LANES), 1)
    from_s, from_y = r // (SUBLANES * SUBLANES), (r // HALF) % 2 * SUBLANES + (r // SUBLANES) % SUBLANES
    block_x = LANES // count_x
    held_at = from_y // HALF * block_x + from_s * HALF + from_y % HALF
    picks = (held_at == c).astype(jnp.bfloat16)
    same_z = r % HALF == c // rank
    weights_y = [jnp.where(same_z, mul(picks, part), 0.0).astype(jnp.bfloat16) for part in held_y]

    def by_x(value):
        return jnp.concatenate([value[f].reshape(plane, LANES) for f in range(n_f)], axis=1)

    partial = mul_split(split(by_x(adv)), weights_x)
    core = mul_split(weights_y, split(partial), ((0,), (0,)))
    columns = split(rescale * mul_split(weights_y, split(core)))

    left = lax.broadcasted_iota(jnp.int32, (SUBLANES, LANES), 1) < LANES // 2
    for s in range(count_y):
        tiles = [core[z * rank + s * SUBLANES : z * rank + (s + 1) * SUBLANES] for z in range(HALF)]
        tiles = exchange(exchange(tiles, 1), LANES // SUBLANES)
        for i in range(count_x):
            tile = tiles[i % HALF]
            turned = pltpu.roll(tile, LANES // 2, 1)
            if i >= HALF:
                tile, turned = turned, tile
            out_ref[i, s, 4 * n_f] = jnp.where(left[:HALF], tile[:HALF], turned[HALF:])

    for f in range(n_f):
        weights = [part[f * LANES : (f + 1) * LANES] for part in weights_x]
        adv[f] = mul_split(columns, weights, ((1,), (1,))).reshape(adv.shape[1:])

    def depart(s):
        for f in range(n_f):
            send(adv[f, s], s, f, 2 * n_f)

    each(depart)


def unpack_kernel(block_x, block_y, in_ref, advanced_ref, core_ref, rebuilt_ref):
    n_f = advanced_ref.shape[0]
    tiles = LANES // SUBLANES
    for target, base in ((advanced_ref, 0), (rebuilt_ref, 2 * n_f)):
        for f in range(n_f):
            for octet in range(2):
                place = base + 2 * f + octet
                matrix = jnp.concatenate([in_ref[:, 0, place], in_ref[:, 1, place]], axis=1)
                turned = matrix.reshape(LANES, LANES).T
                for y in range(SUBLANES):
                    rows = pl.ds(octet * SUBLANES + y, block_x, stride=block_y)
                    target[f, rows, :] = turned[y * block_x : (y + 1) * block_x]
    upper = lax.broadcasted_iota(jnp.int32, (SUBLANES, LANES), 1) >= LANES // 2
    got = []
    for d in range(2 * tiles):
        block = in_ref[d // 2, d % 2, 4 * n_f]
        got.append(jnp.concatenate([block, pltpu.roll(block, LANES // 2, 1)], axis=0))
    kept = [
        jnp.where(upper, pltpu.roll(got[d + tiles], LANES // 2, 1), got[d]) for d in range(tiles)
    ]
    a_count = core_ref.shape[1]
    for place, block in enumerate(exchange(kept, HALF)):
        core_ref[place // a_count, place % a_count] = block


def z_plan(fields, factor_x, factor_y):
    n_f, block_x, block_y, n_z = fields.shape
    rank = factor_x.shape[1]
    count_x = lax.axis_size("gx")
    count_y = lax.axis_size("gy")
    devices = count_x * count_y
    pairs = devices // 2
    tiles_in = 2 * n_f + 1
    tiles_out = 4 * n_f + 1
    rescale = math.sqrt(float(block_x * count_x) * float(block_y * count_y)) / rank
    params = pltpu.CompilerParams(vmem_limit_bytes=48 * 1024 * 1024)
    vmem = pl.BlockSpec(memory_space=pltpu.VMEM)
    hbm = pl.BlockSpec(memory_space=pltpu.HBM)
    f32 = jnp.float32

    packed = pl.pallas_call(
        pack_kernel,
        out_shape=jax.ShapeDtypeStruct((pairs, 2, tiles_in, HALF, n_z), f32),
        in_specs=[hbm] * 3,
        out_specs=vmem,
        scratch_shapes=[
            pltpu.VMEM((n_f, block_x * block_y, n_z), f32),
            pltpu.VMEM(factor_x.shape, f32),
            pltpu.VMEM(factor_y.shape, f32),
            pltpu.SemaphoreType.DMA((n_f + 2,)),
        ],
        compiler_params=params,
        name="pack",
    )(fields.reshape(n_f, block_x * block_y, n_z), factor_x, factor_y)
    planes = lax.all_to_all(
        packed.reshape(devices, tiles_in, HALF, n_z), ("gx", "gy"), 0, 0, tiled=True
    )
    extended = pltpu.VMEM((count_y, n_f, SUBLANES + 6, SUBLANES, LANES), f32)
    results = pl.pallas_call(
        functools.partial(main_kernel, n_f, count_x, count_y, rank, rescale),
        out_shape=jax.ShapeDtypeStruct((count_x, count_y, tiles_out, HALF, n_z), f32),
        in_specs=[vmem],
        out_specs=vmem,
        scratch_shapes=[
            extended,
            extended,
            extended,
            pltpu.VMEM((n_f, count_y, SUBLANES, SUBLANES, LANES), f32),
        ],
        compiler_params=params,
        name="sections",
    )(planes.reshape(count_x, count_y, tiles_in, HALF, n_z))
    back = lax.all_to_all(
        results.reshape(devices, tiles_out, HALF, n_z), ("gx", "gy"), 0, 0, tiled=True
    )
    flat = jax.ShapeDtypeStruct((n_f, block_x * block_y, n_z), f32)
    core = jax.ShapeDtypeStruct((n_f, rank // count_x, rank // count_y, n_z), f32)
    advanced, core_tensor, rebuilt = pl.pallas_call(
        functools.partial(unpack_kernel, block_x, block_y),
        out_shape=(flat, core, flat),
        in_specs=[vmem],
        out_specs=(vmem, vmem, vmem),
        compiler_params=params,
        name="unpack",
    )(back.reshape(pairs, 2, tiles_out, HALF, n_z))
    return advanced.reshape(fields.shape), core_tensor, rebuilt.reshape(fields.shape)


def extended(block, sides, width):
    for axis, dim in sides:
        count = lax.axis_size(axis)
        forward = [(i, i + 1) for i in range(count - 1)]
        forward.append((count - 1, 0))
        backward = [(target, source) for source, target in forward]
        low = lax.ppermute(
            lax.slice_in_dim(block, block.shape[dim] - width, None, axis=dim), axis, forward
        )
        high = lax.ppermute(lax.slice_in_dim(block, 0, width, axis=dim), axis, backward)
        block = jnp.concatenate([low, block, high], axis=dim)
    return block


def inner_part(array, margin):
    return array[:, margin : array.shape[1] - margin, margin : array.shape[2] - margin]


def tendency(padded):
    n_x = padded.shape[1]
    n_y = padded.shape[2]
    pressure = 0.5 * padded[3]
    flux_x = padded[0][None] * padded
    flux_x = flux_x.at[0].add(pressure)
    flux_y = padded[1][None] * padded
    flux_y = flux_y.at[1].add(pressure)

    def along_x(shift):
        return (
            flux_x[:, 3 + shift : n_x - 3 + shift, 3 : n_y - 3]
            - flux_x[:, 3 - shift : n_x - 3 - shift, 3 : n_y - 3]
        )

    def along_y(shift):
        return (
            flux_y[:, 3 : n_x - 3, 3 + shift : n_y - 3 + shift]
            - flux_y[:, 3 : n_x - 3, 3 - shift : n_y - 3 - shift]
        )

    deriv_x = (45.0 * along_x(1) - 9.0 * along_x(2) + along_x(3)) / 60.0
    deriv_y = (45.0 * along_y(1) - 9.0 * along_y(2) + along_y(3)) / 60.0
    center = inner_part(padded, 3)
    react = REACT_RATE * center[2] * (1.0 + jnp.tanh(center[3]))
    zeros = jnp.zeros_like(react)
    source = jnp.stack([zeros, zeros, -react, HEAT_RELEASE * react])
    return source - deriv_x - deriv_y


def section_tendency(state):
    padded = extended(state, (("gx", 1), ("gy", 2)), 3)
    return tendency(padded)


def per_device(fields, factor_x, factor_y):
    high = lax.Precision.HIGHEST
    section_one = fields + TIME_STEP * section_tendency(fields)
    section_two = 0.75 * fields + 0.25 * (section_one + TIME_STEP * section_tendency(section_one))
    advanced = 1.0 / 3.0 * fields + 2.0 / 3.0 * (
        section_two + TIME_STEP * section_tendency(section_two)
    )
    rank_full = factor_x.shape[1]
    count_x = lax.axis_size("gx")
    count_y = lax.axis_size("gy")
    partial_x = jnp.einsum("fxyz,xa->fayz", advanced, factor_x, precision=high)
    partial_value = lax.psum_scatter(partial_x, "gx", scatter_dimension=1, tiled=True)
    local_core = jnp.einsum("fayz,yb->fabz", partial_value, factor_y, precision=high)
    core_tensor = lax.psum_scatter(local_core, "gy", scatter_dimension=2, tiled=True)
    weights = factor_y
    columns = jnp.einsum(
        "fabz,yb->fayz",
        lax.all_gather(core_tensor, "gy", axis=2, tiled=True),
        weights,
        precision=high,
    )
    weights = factor_x
    expanded = jnp.einsum(
        "fayz,xa->fxyz", lax.all_gather(columns, "gx", axis=1, tiled=True), weights, precision=high
    )
    total_x = factor_x.shape[0] * count_x
    total_y = factor_y.shape[0] * count_y
    rescale = math.sqrt(float(total_x) * float(total_y)) / rank_full
    rebuilt = rescale * expanded
    return (advanced, core_tensor, rebuilt)


def solution(mesh):
    placed = (P(None, "gx", "gy", None), P("gx", None), P("gy", None))
    out = P(None, "gx", "gy", None)

    def whole(fields, factor_x, factor_y):
        plan = z_plan if fits(mesh, fields, factor_x, factor_y) else per_device
        return jax.shard_map(
            plan, mesh=mesh, in_specs=placed, out_specs=(out, out, out), check_vma=False
        )(fields, factor_x, factor_y)

    return whole
```

```python
import functools
import math

import jax
import jax.numpy as jnp
from jax import lax
from jax.experimental import pallas as pl
from jax.experimental.pallas import tpu as pltpu
from jax.sharding import PartitionSpec as P

TIME_STEP = 0.2
REACT_RATE = 0.5
HEAT_RELEASE = 1.0
SUBLANES = 8
LANES = 128
HALF = SUBLANES // 2


def fits(mesh, fields, factor_x, factor_y):
    n_f, n_x, n_y, n_z = fields.shape
    count_x, count_y = mesh.shape["gx"], mesh.shape["gy"]
    devices = count_x * count_y
    rank = factor_x.shape[1]
    if n_x % count_x or n_y % count_y or n_z % devices:
        return False
    block_x, block_y, block_z = n_x // count_x, n_y // count_y, n_z // devices
    return (
        n_x == LANES
        and n_z == LANES
        and n_f == HALF
        and block_z == HALF
        and block_x == 2 * SUBLANES
        and block_y == 2 * SUBLANES
        and count_x == SUBLANES
        and count_y == HALF
        and rank == count_y * SUBLANES
        and factor_y.shape[1] == rank
        and n_f * rank == LANES
    )


def exchange(blocks, stride):
    count = len(blocks)
    period = stride * count
    group = lax.broadcasted_iota(jnp.int32, (SUBLANES, LANES), 1) // stride % count
    if period == LANES:
        blocks = [pltpu.roll(b, i * stride, 1) if i else b for i, b in enumerate(blocks)]
        step = 1
        while step < count:
            taken = (group & step) != 0
            blocks = [
                jnp.where(taken, blocks[(i + step) % count], blocks[i]) for i in range(count)
            ]
            step *= 2
        blocks = [blocks[-j % count] for j in range(count)]
        return [pltpu.roll(b, LANES - j * stride, 1) if j else b for j, b in enumerate(blocks)]
    blocks = list(blocks)
    step = 1
    while step < count:
        upper = (group & step) != 0
        for i in range(count):
            if i & step:
                continue
            low, high = blocks[i], blocks[i + step]
            blocks[i] = jnp.where(upper, pltpu.roll(high, stride * step, 1), low)
            blocks[i + step] = jnp.where(upper, high, pltpu.roll(low, LANES - stride * step, 1))
        step *= 2
    return blocks


def pack_kernel(fields_hbm, factor_x_hbm, factor_y_hbm, out_ref, fields_ref, x_ref, y_ref, sems):
    n_f, rows, _ = fields_ref.shape
    block_x = x_ref.shape[0]
    block_y = rows // block_x
    tiles = LANES // SUBLANES
    copies = [
        pltpu.make_async_copy(fields_hbm.at[f], fields_ref.at[f], sems.at[f]) for f in range(n_f)
    ]
    copies.append(pltpu.make_async_copy(factor_x_hbm, x_ref, sems.at[n_f]))
    copies.append(pltpu.make_async_copy(factor_y_hbm, y_ref, sems.at[n_f + 1]))
    for copy in copies:
        copy.start()
    for f in range(n_f):
        copies[f].wait()
        for octet in range(2):
            matrix = jnp.concatenate(
                [
                    fields_ref[f, pl.ds(octet * SUBLANES + y, block_x, stride=block_y), :]
                    for y in range(SUBLANES)
                ],
                axis=0,
            )
            turned = matrix.T.reshape(tiles, SUBLANES, LANES)
            out_ref[:, 0, 2 * f + octet] = turned[:, :HALF]
            out_ref[:, 1, 2 * f + octet] = turned[:, HALF:]
    copies[n_f].wait()
    copies[n_f + 1].wait()
    part_x = lax.axis_index("gy")
    part_y = lax.rem(lax.axis_index("gx"), block_y // HALF)
    own_x = x_ref[pl.ds(part_x * HALF, HALF), :]
    own_y = y_ref[pl.ds(part_y * HALF, HALF), :]
    factors = jnp.concatenate([own_x, own_y, own_y, own_y], axis=1)
    out_ref[:, :, 2 * n_f] = jnp.broadcast_to(factors[None, None], (tiles, 2, HALF, LANES))


def split(value):
    high = value.astype(jnp.bfloat16)
    low = (value - high.astype(jnp.float32)).astype(jnp.bfloat16)
    return high, low


def mul(a, b, dims=((1,), (0,))):
    return lax.dot_general(a, b, (dims, ((), ())), preferred_element_type=jnp.float32)


def mul_split(a, b, dims=((1,), (0,))):
    return mul(a[0], b[0], dims) + (mul(a[0], b[1], dims) + mul(a[1], b[0], dims))


def main_kernel(
    n_f, count_x, count_y, rank, rescale, in_ref, adv, spread_ref, *refs
):
    column_refs, (ext_a, ext_b, ext_c, staged) = refs[:count_y], refs[count_y:]
    margin = 3
    inner = pl.ds(margin, SUBLANES)
    lower = lax.broadcasted_iota(jnp.int32, (margin, SUBLANES, LANES), 1) < HALF

    def each(body):
        def step(s, carry):
            body(s)
            return carry

        lax.fori_loop(0, count_y, step, 0, unroll=True)

    def fill_margins(ext):
        def one(s):
            before = lax.rem(s + count_y - 1, count_y)
            after = lax.rem(s + 1, count_y)
            for f in range(n_f):
                old = ext[before, f, pl.ds(SUBLANES, margin)]
                own = ext[s, f, pl.ds(SUBLANES, margin)]
                ext[s, f, 0:margin] = pltpu.roll(jnp.where(lower, own, old), HALF, 1)
                own = ext[s, f, pl.ds(margin, margin)]
                new = ext[after, f, pl.ds(margin, margin)]
                ext[s, f, pl.ds(SUBLANES + margin, margin)] = pltpu.roll(
                    jnp.where(lower, new, own), HALF, 1
                )

        each(one)

    row = lax.broadcasted_iota(jnp.int32, (LANES, LANES), 0)
    col = lax.broadcasted_iota(jnp.int32, (LANES, LANES), 1)
    ahead = (row - col) & (LANES - 1)
    taps = jnp.zeros((LANES, LANES), jnp.float32)
    for shift, weight in ((1, 45.0), (2, -9.0), (3, 1.0)):
        taps = jnp.where(ahead == shift, weight, taps)
        taps = jnp.where(ahead == LANES - shift, -weight, taps)
    taps = taps.astype(jnp.bfloat16)
    taps = jnp.concatenate([taps, taps], axis=0)

    def section(ext, step, store):
        def one(s):
            padded = [ext[s, f] for f in range(n_f)]
            center = [p[margin : margin + SUBLANES] for p in padded]
            flux_x = [center[0] * c for c in center]
            flux_x[0] = flux_x[0] + 0.5 * center[3]
            flat = jnp.concatenate(flux_x, axis=0).reshape(n_f * SUBLANES * SUBLANES, LANES)
            along_x = mul(jnp.concatenate(split(flat), axis=1), taps)
            along_x = along_x.reshape(n_f, SUBLANES, SUBLANES, LANES)
            react = (step * REACT_RATE) * center[2] * (1.0 + jnp.tanh(center[3]))
            for f in range(n_f):
                flux_y = padded[1] * padded[f]
                if f == 1:
                    flux_y = flux_y + 0.5 * padded[3]

                def along_y(k):
                    after = flux_y[margin + k : margin + k + SUBLANES]
                    return after - flux_y[margin - k : margin - k + SUBLANES]

                change = (
                    (-45.0 * step / 60.0) * along_y(1)
                    + (9.0 * step / 60.0) * along_y(2)
                    + (-step / 60.0) * (along_y(3) + along_x[f])
                )
                if f == 2:
                    change = change - react
                if f == 3:
                    change = change + HEAT_RELEASE * react
                store(s, f, center[f], change)

        each(one)

    def arrive(s):
        for f in range(n_f):
            got = [
                in_ref[i, s, 2 * f : 2 * f + 2].reshape(SUBLANES, LANES) for i in range(count_x)
            ]
            for y, block in enumerate(exchange(got, LANES // SUBLANES)):
                ext_a[s, f, margin + y] = block

    def first(s, f, center, change):
        ext_b[s, f, inner] = center + change

    def second(s, f, center, change):
        ext_c[s, f, inner] = 0.75 * ext_a[s, f, inner] + (0.25 * center + change)

    def third(s, f, center, change):
        adv[f, s] = (1.0 / 3.0) * ext_a[s, f, inner] + ((2.0 / 3.0) * center + change)

    each(arrive)
    fill_margins(ext_a)
    section(ext_a, TIME_STEP, first)
    fill_margins(ext_b)
    section(ext_b, 0.25 * TIME_STEP, second)
    fill_margins(ext_c)
    section(ext_c, 2.0 / 3.0 * TIME_STEP, third)

    plane = count_y * SUBLANES * SUBLANES
    held = in_ref[:, :, 2 * n_f].reshape(LANES, LANES)
    held_x = split(held)
    held_y = split(jnp.where(col < rank, pltpu.roll(held, LANES - rank, 1), held))
    picks = (row == col // n_f).astype(jnp.bfloat16)
    spread_x = [mul(part, picks) for part in held_x]
    weights_x = [
        jnp.concatenate(
            [jnp.where(col % n_f == f, part, 0.0).astype(jnp.bfloat16) for f in range(n_f)], axis=0
        )
        for part in spread_x
    ]
    r = lax.broadcasted_iota(jnp.int32, (plane, LANES), 0)
    c = lax.broadcasted_iota(jnp.int32, (plane, LANES), 1)
    from_s, from_y = r // (SUBLANES * SUBLANES), (r // HALF) % 2 * SUBLANES + (r // SUBLANES) % SUBLANES
    block_x = LANES // count_x
    held_at = from_y // HALF * block_x + from_s * HALF + from_y % HALF
    picks = (held_at == c).astype(jnp.bfloat16)
    same_z = r % HALF == c // rank
    weights_y = [jnp.where(same_z, mul(picks, part), 0.0).astype(jnp.bfloat16) for part in held_y]

    def by_x(value):
        return jnp.concatenate([value[f].reshape(plane, LANES) for f in range(n_f)], axis=1)

    partial = mul_split(split(by_x(adv)), weights_x)
    core = mul_split(weights_y, split(partial), ((0,), (0,)))
    columns = rescale * mul_split(weights_y, split(core))
    for part in range(2):
        spread_ref[part] = weights_x[part]

    block = plane // count_y
    for s in range(count_y):
        staged[s, 0:block] = columns[s * block : (s + 1) * block]
        for z in range(HALF):
            at = z * rank + s * SUBLANES
            staged[s, block + z * SUBLANES : block + (z + 1) * SUBLANES] = core[at : at + SUBLANES]
    own = lax.axis_index("gy")
    for k, ref in enumerate(column_refs):
        ref[...] = staged[lax.rem(own + k, count_y)]


def send_kernel(count_x, adv, out_ref):
    n_f, count_y = adv.shape[:2]
    for s in range(count_y):
        for f in range(n_f):
            parts = exchange([adv[f, s, y] for y in range(SUBLANES)], LANES // SUBLANES)
            for i, part in enumerate(parts):
                out_ref[i, s, 2 * f : 2 * f + 2] = part.reshape(2, HALF, LANES)


def expand_kernel(n_f, count_x, count_y, spread_ref, *refs):
    in_refs, out_refs = refs[:count_y], refs[count_y : count_y + count_x]
    held, staged = refs[count_y + count_x :]
    own = lax.axis_index("gy")
    for k, ref in enumerate(in_refs):
        held[lax.rem(own + count_y - k, count_y)] = ref[...]
    block = SUBLANES * SUBLANES
    plane = count_y * block
    columns = split(jnp.concatenate([held[s, 0:block] for s in range(count_y)], axis=0))
    for f in range(n_f):
        weights = [spread_ref[part, f * LANES : (f + 1) * LANES] for part in range(2)]
        rebuilt = mul_split(columns, weights, ((1,), (1,)))
        rebuilt = rebuilt.reshape(count_y, SUBLANES, SUBLANES, LANES)
        for s in range(count_y):
            parts = exchange([rebuilt[s, y] for y in range(SUBLANES)], LANES // SUBLANES)
            for i, part in enumerate(parts):
                at = (f * count_y + s) * SUBLANES
                staged[i, at : at + SUBLANES] = part
    by_f = [
        exchange([held[s, block + z * SUBLANES : block + (z + 1) * SUBLANES] for z in range(HALF)], 1)
        for s in range(count_y)
    ]
    left = lax.broadcasted_iota(jnp.int32, (SUBLANES, LANES), 1) < LANES // 2
    by_i = []
    for f in range(n_f):
        tiles = exchange([by_f[s][f] for s in range(count_y)], HALF)
        by_i.append(exchange(tiles, LANES // SUBLANES))
    for i in range(count_x):
        for pair in range(n_f // 2):
            low, high = by_i[2 * pair][i % HALF], by_i[2 * pair + 1][i % HALF]
            if i < HALF:
                tile = jnp.where(left, low, pltpu.roll(high, LANES // 2, 1))
            else:
                tile = jnp.where(left, pltpu.roll(low, LANES // 2, 1), high)
            at = (n_f * count_y + pair) * SUBLANES
            staged[i, at : at + SUBLANES] = tile
    own = lax.axis_index("gx")
    for k, ref in enumerate(out_refs):
        ref[...] = staged[lax.rem(own + k, count_x)]


def scatter_rows(turned, octet, block_x, block_y, target, f):
    for y in range(SUBLANES):
        rows = pl.ds(octet * SUBLANES + y, block_x, stride=block_y)
        target[f, rows, :] = turned[y * block_x : (y + 1) * block_x]


def advanced_kernel(block_x, block_y, in_ref, advanced_ref):
    for f in range(advanced_ref.shape[0]):
        for octet in range(2):
            place = 2 * f + octet
            matrix = jnp.concatenate([in_ref[:, 0, place], in_ref[:, 1, place]], axis=1)
            turned = matrix.reshape(LANES, LANES).T
            scatter_rows(turned, octet, block_x, block_y, advanced_ref, f)


def rebuilt_kernel(block_x, block_y, count_x, count_y, *refs):
    in_refs, (rebuilt_ref, core_ref, held) = refs[:count_x], refs[count_x:]
    n_f = rebuilt_ref.shape[0]
    own = lax.axis_index("gx")
    for k, ref in enumerate(in_refs):
        held[lax.rem(own + count_x - k, count_x)] = ref[...]
    pairs = count_y // 2
    lower = lax.broadcasted_iota(jnp.int32, (count_x, pairs, SUBLANES, LANES), 2) < HALF
    for f in range(n_f):
        at = pl.ds(f * count_y * SUBLANES, count_y * SUBLANES)
        tiles = held[:, at, :].reshape(count_x, pairs, 2, SUBLANES, LANES)
        even, odd = tiles[:, :, 0], tiles[:, :, 1]
        first = jnp.where(lower, even, pltpu.roll(odd, HALF, 2))
        second = jnp.where(lower, pltpu.roll(even, HALF, 2), odd)
        for octet, part in enumerate((first, second)):
            turned = part.reshape(LANES, LANES).T
            scatter_rows(turned, octet, block_x, block_y, rebuilt_ref, f)
    a_count = core_ref.shape[1]
    for pair in range(n_f // 2):
        at = (n_f * count_y + pair) * SUBLANES
        tiles = exchange([held[i, at : at + SUBLANES] for i in range(count_x)], LANES // SUBLANES)
        for place, tile in enumerate(tiles):
            core_ref[2 * pair + place // a_count, place % a_count] = tile


def z_plan(fields, factor_x, factor_y):
    n_f, block_x, block_y, n_z = fields.shape
    rank = factor_x.shape[1]
    count_x = lax.axis_size("gx")
    count_y = lax.axis_size("gy")
    devices = count_x * count_y
    pairs = devices // 2
    rescale = math.sqrt(float(block_x * count_x) * float(block_y * count_y)) / rank
    vmem = pl.BlockSpec(memory_space=pltpu.VMEM)
    hbm = pl.BlockSpec(memory_space=pltpu.HBM)
    f32 = jnp.float32

    def array(shape, dtype=f32):
        return jax.ShapeDtypeStruct(shape, dtype)

    def call(kernel, name, outs, scratch, operands, space=vmem, limit=48 * 1024 * 1024):
        return pl.pallas_call(
            kernel,
            out_shape=tuple(outs),
            in_specs=[space] * len(operands),
            out_specs=(vmem,) * len(outs),
            scratch_shapes=scratch,
            compiler_params=pltpu.CompilerParams(vmem_limit_bytes=limit),
            cost_estimate=pl.CostEstimate(flops=10**9, bytes_accessed=0, transcendentals=0),
            name=name,
        )(*operands)

    def swap(blocks, tiles):
        blocks = blocks.reshape(devices, tiles, HALF, n_z)
        return lax.all_to_all(blocks, ("gx", "gy"), 0, 0, tiled=True)

    def pass_on(blocks, axis):
        count = len(blocks)
        moved = [
            lax.ppermute(block, axis, [(i, (i + k) % count) for i in range(count)])
            for k, block in enumerate(blocks)
            if k
        ]
        return [blocks[0]] + moved

    flat = (n_f, block_x * block_y, n_z)
    (packed,) = call(
        pack_kernel,
        "pack",
        [array((pairs, 2, 2 * n_f + 1, HALF, n_z))],
        [
            pltpu.VMEM(flat, f32),
            pltpu.VMEM(factor_x.shape, f32),
            pltpu.VMEM(factor_y.shape, f32),
            pltpu.SemaphoreType.DMA((n_f + 2,)),
        ],
        (fields.reshape(flat), factor_x, factor_y),
        hbm,
        None,
    )
    planes = swap(packed, 2 * n_f + 1).reshape(count_x, count_y, 2 * n_f + 1, HALF, n_z)
    extended = pltpu.VMEM((count_y, n_f, SUBLANES + 6, SUBLANES, LANES), f32)
    rows = SUBLANES * SUBLANES + HALF * SUBLANES
    held, spread, *columns = call(
        functools.partial(main_kernel, n_f, count_x, count_y, rank, rescale),
        "sections",
        [
            array((n_f, count_y, SUBLANES, SUBLANES, LANES)),
            array((2, n_f * LANES, LANES), jnp.bfloat16),
        ]
        + [array((rows, LANES))] * count_y,
        [extended] * 3 + [pltpu.VMEM((count_y, rows, LANES), f32)],
        (planes,),
    )
    columns = pass_on(columns, "gy")
    (sent,) = call(
        functools.partial(send_kernel, count_x),
        "send",
        [array((count_x, count_y, 2 * n_f, HALF, n_z))],
        [],
        (held,),
    )
    sent, columns = lax.optimization_barrier((sent, columns))
    sent = swap(sent, 2 * n_f).reshape(pairs, 2, 2 * n_f, HALF, n_z)
    rows = (n_f * count_y + n_f // 2) * SUBLANES
    blocks = call(
        functools.partial(expand_kernel, n_f, count_x, count_y),
        "expand",
        [array((rows, LANES))] * count_x,
        [
            pltpu.VMEM((count_y,) + columns[0].shape, f32),
            pltpu.VMEM((count_x, rows, LANES), f32),
        ],
        (spread, *columns),
    )
    blocks = pass_on(blocks, "gx")
    (advanced,) = call(
        functools.partial(advanced_kernel, block_x, block_y), "advanced", [array(flat)], [], (sent,)
    )
    rebuilt, core = call(
        functools.partial(rebuilt_kernel, block_x, block_y, count_x, count_y),
        "rebuilt",
        [array(flat), array((n_f, rank // count_x, rank // count_y, n_z))],
        [pltpu.VMEM((count_x, rows, LANES), f32)],
        tuple(blocks),
    )
    return advanced.reshape(fields.shape), core, rebuilt.reshape(fields.shape)


def extended(block, sides, width):
    for axis, dim in sides:
        count = lax.axis_size(axis)
        forward = [(i, i + 1) for i in range(count - 1)]
        forward.append((count - 1, 0))
        backward = [(target, source) for source, target in forward]
        low = lax.ppermute(
            lax.slice_in_dim(block, block.shape[dim] - width, None, axis=dim), axis, forward
        )
        high = lax.ppermute(lax.slice_in_dim(block, 0, width, axis=dim), axis, backward)
        block = jnp.concatenate([low, block, high], axis=dim)
    return block


def inner_part(array, margin):
    return array[:, margin : array.shape[1] - margin, margin : array.shape[2] - margin]


def tendency(padded):
    n_x = padded.shape[1]
    n_y = padded.shape[2]
    pressure = 0.5 * padded[3]
    flux_x = padded[0][None] * padded
    flux_x = flux_x.at[0].add(pressure)
    flux_y = padded[1][None] * padded
    flux_y = flux_y.at[1].add(pressure)

    def along_x(shift):
        return (
            flux_x[:, 3 + shift : n_x - 3 + shift, 3 : n_y - 3]
            - flux_x[:, 3 - shift : n_x - 3 - shift, 3 : n_y - 3]
        )

    def along_y(shift):
        return (
            flux_y[:, 3 : n_x - 3, 3 + shift : n_y - 3 + shift]
            - flux_y[:, 3 : n_x - 3, 3 - shift : n_y - 3 - shift]
        )

    deriv_x = (45.0 * along_x(1) - 9.0 * along_x(2) + along_x(3)) / 60.0
    deriv_y = (45.0 * along_y(1) - 9.0 * along_y(2) + along_y(3)) / 60.0
    center = inner_part(padded, 3)
    react = REACT_RATE * center[2] * (1.0 + jnp.tanh(center[3]))
    zeros = jnp.zeros_like(react)
    source = jnp.stack([zeros, zeros, -react, HEAT_RELEASE * react])
    return source - deriv_x - deriv_y


def section_tendency(state):
    padded = extended(state, (("gx", 1), ("gy", 2)), 3)
    return tendency(padded)


def per_device(fields, factor_x, factor_y):
    high = lax.Precision.HIGHEST
    section_one = fields + TIME_STEP * section_tendency(fields)
    section_two = 0.75 * fields + 0.25 * (section_one + TIME_STEP * section_tendency(section_one))
    advanced = 1.0 / 3.0 * fields + 2.0 / 3.0 * (
        section_two + TIME_STEP * section_tendency(section_two)
    )
    rank_full = factor_x.shape[1]
    count_x = lax.axis_size("gx")
    count_y = lax.axis_size("gy")
    partial_x = jnp.einsum("fxyz,xa->fayz", advanced, factor_x, precision=high)
    partial_value = lax.psum_scatter(partial_x, "gx", scatter_dimension=1, tiled=True)
    local_core = jnp.einsum("fayz,yb->fabz", partial_value, factor_y, precision=high)
    core_tensor = lax.psum_scatter(local_core, "gy", scatter_dimension=2, tiled=True)
    weights = factor_y
    columns = jnp.einsum(
        "fabz,yb->fayz",
        lax.all_gather(core_tensor, "gy", axis=2, tiled=True),
        weights,
        precision=high,
    )
    weights = factor_x
    expanded = jnp.einsum(
        "fayz,xa->fxyz", lax.all_gather(columns, "gx", axis=1, tiled=True), weights, precision=high
    )
    total_x = factor_x.shape[0] * count_x
    total_y = factor_y.shape[0] * count_y
    rescale = math.sqrt(float(total_x) * float(total_y)) / rank_full
    rebuilt = rescale * expanded
    return (advanced, core_tensor, rebuilt)


def solution(mesh):
    placed = (P(None, "gx", "gy", None), P("gx", None), P("gy", None))
    out = P(None, "gx", "gy", None)

    def whole(fields, factor_x, factor_y):
        plan = z_plan if fits(mesh, fields, factor_x, factor_y) else per_device
        return jax.shard_map(
            plan, mesh=mesh, in_specs=placed, out_specs=(out, out, out), check_vma=False
        )(fields, factor_x, factor_y)

    return whole
```

```python
import functools
import math

import jax
import jax.numpy as jnp
from jax import lax
from jax.experimental import pallas as pl
from jax.experimental.pallas import tpu as pltpu
from jax.sharding import PartitionSpec as P

TIME_STEP = 0.2
REACT_RATE = 0.5
HEAT_RELEASE = 1.0
SUBLANES = 8
LANES = 128
HALF = SUBLANES // 2


def fits(mesh, fields, factor_x, factor_y):
    n_f, n_x, n_y, n_z = fields.shape
    count_x, count_y = mesh.shape["gx"], mesh.shape["gy"]
    devices = count_x * count_y
    rank = factor_x.shape[1]
    if n_x % count_x or n_y % count_y or n_z % devices:
        return False
    block_x, block_y, block_z = n_x // count_x, n_y // count_y, n_z // devices
    return (
        n_x == LANES
        and n_z == LANES
        and n_f == HALF
        and block_z == HALF
        and block_x == 2 * SUBLANES
        and block_y == 2 * SUBLANES
        and count_x == SUBLANES
        and count_y == HALF
        and rank == count_y * SUBLANES
        and factor_y.shape[1] == rank
        and n_f * rank == LANES
    )


def exchange(blocks, stride):
    count = len(blocks)
    period = stride * count
    group = lax.broadcasted_iota(jnp.int32, (SUBLANES, LANES), 1) // stride % count
    if period == LANES:
        blocks = [pltpu.roll(b, i * stride, 1) if i else b for i, b in enumerate(blocks)]
        step = 1
        while step < count:
            taken = (group & step) != 0
            blocks = [
                jnp.where(taken, blocks[(i + step) % count], blocks[i]) for i in range(count)
            ]
            step *= 2
        blocks = [blocks[-j % count] for j in range(count)]
        return [pltpu.roll(b, LANES - j * stride, 1) if j else b for j, b in enumerate(blocks)]
    blocks = list(blocks)
    step = 1
    while step < count:
        upper = (group & step) != 0
        for i in range(count):
            if i & step:
                continue
            low, high = blocks[i], blocks[i + step]
            blocks[i] = jnp.where(upper, pltpu.roll(high, stride * step, 1), low)
            blocks[i + step] = jnp.where(upper, high, pltpu.roll(low, LANES - stride * step, 1))
        step *= 2
    return blocks


def pack_kernel(
    fields_hbm, factor_x_hbm, factor_y_hbm, out_hbm, out_ref, fields_ref, x_ref, y_ref, sems, out_sems
):
    n_f, rows, _ = fields_ref.shape
    block_x = x_ref.shape[0]
    block_y = rows // block_x
    tiles = LANES // SUBLANES
    copies = [
        pltpu.make_async_copy(fields_hbm.at[f], fields_ref.at[f], sems.at[f]) for f in range(n_f)
    ]
    copies.append(pltpu.make_async_copy(factor_x_hbm, x_ref, sems.at[n_f]))
    copies.append(pltpu.make_async_copy(factor_y_hbm, y_ref, sems.at[n_f + 1]))
    for copy in copies:
        copy.start()

    def leave(f, tiles):
        at = (slice(None), slice(None), pl.ds(2 * f, tiles))
        return pltpu.make_async_copy(out_ref.at[at], out_hbm.at[at], out_sems.at[f])

    leaving = [leave(f, 2) for f in range(n_f)] + [leave(n_f, 1)]
    for f in range(n_f):
        copies[f].wait()
        for octet in range(2):
            matrix = jnp.concatenate(
                [
                    fields_ref[f, pl.ds(octet * SUBLANES + y, block_x, stride=block_y), :]
                    for y in range(SUBLANES)
                ],
                axis=0,
            )
            turned = matrix.T.reshape(tiles, SUBLANES, LANES)
            out_ref[:, 0, 2 * f + octet] = turned[:, :HALF]
            out_ref[:, 1, 2 * f + octet] = turned[:, HALF:]
        leaving[f].start()
    copies[n_f].wait()
    copies[n_f + 1].wait()
    part_x = lax.axis_index("gy")
    part_y = lax.rem(lax.axis_index("gx"), block_y // HALF)
    own_x = x_ref[pl.ds(part_x * HALF, HALF), :]
    own_y = y_ref[pl.ds(part_y * HALF, HALF), :]
    factors = jnp.concatenate([own_x, own_y, own_y, own_y], axis=1)
    out_ref[:, :, 2 * n_f] = jnp.broadcast_to(factors[None, None], (tiles, 2, HALF, LANES))
    leaving[n_f].start()
    for copy in leaving:
        copy.wait()


def split(value):
    high = value.astype(jnp.bfloat16)
    low = (value - high.astype(jnp.float32)).astype(jnp.bfloat16)
    return high, low


def mul(a, b, dims=((1,), (0,))):
    return lax.dot_general(a, b, (dims, ((), ())), preferred_element_type=jnp.float32)


def mul_split(a, b, dims=((1,), (0,))):
    return mul(a[0], b[0], dims) + (mul(a[0], b[1], dims) + mul(a[1], b[0], dims))


def main_kernel(
    n_f, count_x, count_y, rank, rescale, in_ref, sent_ref, spread_ref, *refs
):
    column_refs = refs[:count_y]
    ext_a, ext_b, ext_c, adv, staged = refs[count_y:]
    margin = 3
    inner = pl.ds(margin, SUBLANES)
    lower = lax.broadcasted_iota(jnp.int32, (margin, SUBLANES, LANES), 1) < HALF

    def each(body):
        def step(s, carry):
            body(s)
            return carry

        lax.fori_loop(0, count_y, step, 0, unroll=True)

    def fill_margins(ext):
        def one(s):
            before = lax.rem(s + count_y - 1, count_y)
            after = lax.rem(s + 1, count_y)
            for f in range(n_f):
                old = ext[before, f, pl.ds(SUBLANES, margin)]
                own = ext[s, f, pl.ds(SUBLANES, margin)]
                ext[s, f, 0:margin] = pltpu.roll(jnp.where(lower, own, old), HALF, 1)
                own = ext[s, f, pl.ds(margin, margin)]
                new = ext[after, f, pl.ds(margin, margin)]
                ext[s, f, pl.ds(SUBLANES + margin, margin)] = pltpu.roll(
                    jnp.where(lower, new, own), HALF, 1
                )

        each(one)

    row = lax.broadcasted_iota(jnp.int32, (LANES, LANES), 0)
    col = lax.broadcasted_iota(jnp.int32, (LANES, LANES), 1)
    ahead = (row - col) & (LANES - 1)
    taps = jnp.zeros((LANES, LANES), jnp.float32)
    for shift, weight in ((1, 45.0), (2, -9.0), (3, 1.0)):
        taps = jnp.where(ahead == shift, weight, taps)
        taps = jnp.where(ahead == LANES - shift, -weight, taps)
    taps = taps.astype(jnp.bfloat16)
    taps = jnp.concatenate([taps, taps], axis=0)

    def section(ext, step, store):
        def one(s):
            padded = [ext[s, f] for f in range(n_f)]
            center = [p[margin : margin + SUBLANES] for p in padded]
            flux_x = [center[0] * c for c in center]
            flux_x[0] = flux_x[0] + 0.5 * center[3]
            flat = jnp.concatenate(flux_x, axis=0).reshape(n_f * SUBLANES * SUBLANES, LANES)
            along_x = mul(jnp.concatenate(split(flat), axis=1), taps)
            along_x = along_x.reshape(n_f, SUBLANES, SUBLANES, LANES)
            react = (step * REACT_RATE) * center[2] * (1.0 + jnp.tanh(center[3]))
            for f in range(n_f):
                flux_y = padded[1] * padded[f]
                if f == 1:
                    flux_y = flux_y + 0.5 * padded[3]

                def along_y(k):
                    after = flux_y[margin + k : margin + k + SUBLANES]
                    return after - flux_y[margin - k : margin - k + SUBLANES]

                change = (
                    (-45.0 * step / 60.0) * along_y(1)
                    + (9.0 * step / 60.0) * along_y(2)
                    + (-step / 60.0) * (along_y(3) + along_x[f])
                )
                if f == 2:
                    change = change - react
                if f == 3:
                    change = change + HEAT_RELEASE * react
                store(s, f, center[f], change)

        each(one)

    def arrive(s):
        for f in range(n_f):
            got = [
                in_ref[i, s, 2 * f : 2 * f + 2].reshape(SUBLANES, LANES) for i in range(count_x)
            ]
            for y, block in enumerate(exchange(got, LANES // SUBLANES)):
                ext_a[s, f, margin + y] = block

    def first(s, f, center, change):
        ext_b[s, f, inner] = center + change

    def second(s, f, center, change):
        ext_c[s, f, inner] = 0.75 * ext_a[s, f, inner] + (0.25 * center + change)

    def third(s, f, center, change):
        done = (1.0 / 3.0) * ext_a[s, f, inner] + ((2.0 / 3.0) * center + change)
        adv[f, s] = done
        parts = exchange([done[y] for y in range(SUBLANES)], LANES // SUBLANES)
        for i, part in enumerate(parts):
            sent_ref[i, s, 2 * f : 2 * f + 2] = part.reshape(2, HALF, LANES)

    each(arrive)
    fill_margins(ext_a)
    section(ext_a, TIME_STEP, first)
    fill_margins(ext_b)
    section(ext_b, 0.25 * TIME_STEP, second)
    fill_margins(ext_c)
    section(ext_c, 2.0 / 3.0 * TIME_STEP, third)

    plane = count_y * SUBLANES * SUBLANES
    held = in_ref[:, :, 2 * n_f].reshape(LANES, LANES)
    held_x = split(held)
    held_y = split(jnp.where(col < rank, pltpu.roll(held, LANES - rank, 1), held))
    picks = (row == col // n_f).astype(jnp.bfloat16)
    spread_x = [mul(part, picks) for part in held_x]
    weights_x = [
        jnp.concatenate(
            [jnp.where(col % n_f == f, part, 0.0).astype(jnp.bfloat16) for f in range(n_f)], axis=0
        )
        for part in spread_x
    ]
    r = lax.broadcasted_iota(jnp.int32, (plane, LANES), 0)
    c = lax.broadcasted_iota(jnp.int32, (plane, LANES), 1)
    from_s, from_y = r // (SUBLANES * SUBLANES), (r // HALF) % 2 * SUBLANES + (r // SUBLANES) % SUBLANES
    block_x = LANES // count_x
    held_at = from_y // HALF * block_x + from_s * HALF + from_y % HALF
    picks = (held_at == c).astype(jnp.bfloat16)
    same_z = r % HALF == c // rank
    weights_y = [jnp.where(same_z, mul(picks, part), 0.0).astype(jnp.bfloat16) for part in held_y]

    def by_x(value):
        return jnp.concatenate([value[f].reshape(plane, LANES) for f in range(n_f)], axis=1)

    partial = mul_split(split(by_x(adv)), weights_x)
    core = mul_split(weights_y, split(partial), ((0,), (0,)))
    columns = rescale * mul_split(weights_y, split(core))
    for part in range(2):
        spread_ref[part] = weights_x[part]

    block = plane // count_y
    for s in range(count_y):
        staged[s, 0:block] = columns[s * block : (s + 1) * block]
        for z in range(HALF):
            at = z * rank + s * SUBLANES
            staged[s, block + z * SUBLANES : block + (z + 1) * SUBLANES] = core[at : at + SUBLANES]
    own = lax.axis_index("gy")
    for k, ref in enumerate(column_refs):
        ref[...] = staged[lax.rem(own + k, count_y)]


def expand_kernel(n_f, count_x, count_y, spread_ref, *refs):
    in_refs, out_refs = refs[:count_y], refs[count_y : count_y + count_x]
    held, staged = refs[count_y + count_x :]
    own = lax.axis_index("gy")
    for k, ref in enumerate(in_refs):
        held[lax.rem(own + count_y - k, count_y)] = ref[...]
    block = SUBLANES * SUBLANES
    plane = count_y * block
    columns = split(jnp.concatenate([held[s, 0:block] for s in range(count_y)], axis=0))
    for f in range(n_f):
        weights = [spread_ref[part, f * LANES : (f + 1) * LANES] for part in range(2)]
        rebuilt = mul_split(columns, weights, ((1,), (1,)))
        rebuilt = rebuilt.reshape(count_y, SUBLANES, SUBLANES, LANES)
        for s in range(count_y):
            parts = exchange([rebuilt[s, y] for y in range(SUBLANES)], LANES // SUBLANES)
            for i, part in enumerate(parts):
                at = (f * count_y + s) * SUBLANES
                staged[i, at : at + SUBLANES] = part
    by_f = [
        exchange([held[s, block + z * SUBLANES : block + (z + 1) * SUBLANES] for z in range(HALF)], 1)
        for s in range(count_y)
    ]
    left = lax.broadcasted_iota(jnp.int32, (SUBLANES, LANES), 1) < LANES // 2
    by_i = []
    for f in range(n_f):
        tiles = exchange([by_f[s][f] for s in range(count_y)], HALF)
        by_i.append(exchange(tiles, LANES // SUBLANES))
    for i in range(count_x):
        for pair in range(n_f // 2):
            low, high = by_i[2 * pair][i % HALF], by_i[2 * pair + 1][i % HALF]
            if i < HALF:
                tile = jnp.where(left, low, pltpu.roll(high, LANES // 2, 1))
            else:
                tile = jnp.where(left, pltpu.roll(low, LANES // 2, 1), high)
            at = (n_f * count_y + pair) * SUBLANES
            staged[i, at : at + SUBLANES] = tile
    own = lax.axis_index("gx")
    for k, ref in enumerate(out_refs):
        ref[...] = staged[lax.rem(own + k, count_x)]


def leave_fields(ref, hbm, sems):
    return [
        pltpu.make_async_copy(ref.at[f], hbm.at[f], sems.at[f]) for f in range(ref.shape[0])
    ]


def scatter_rows(turned, octet, block_x, block_y, target, f):
    for y in range(SUBLANES):
        rows = pl.ds(octet * SUBLANES + y, block_x, stride=block_y)
        target[f, rows, :] = turned[y * block_x : (y + 1) * block_x]


def advanced_kernel(block_x, block_y, in_ref, advanced_hbm, advanced_ref, sems):
    leaving = leave_fields(advanced_ref, advanced_hbm, sems)
    for f in range(advanced_ref.shape[0]):
        for octet in range(2):
            place = 2 * f + octet
            matrix = jnp.concatenate([in_ref[:, 0, place], in_ref[:, 1, place]], axis=1)
            turned = matrix.reshape(LANES, LANES).T
            scatter_rows(turned, octet, block_x, block_y, advanced_ref, f)
        leaving[f].start()
    for copy in leaving:
        copy.wait()


def rebuilt_kernel(block_x, block_y, count_x, count_y, *refs):
    in_refs, (rebuilt_hbm, core_hbm, held, rebuilt_ref, core_ref, sems) = refs[:count_x], refs[count_x:]
    n_f = rebuilt_ref.shape[0]
    leaving = leave_fields(rebuilt_ref, rebuilt_hbm, sems)
    leaving.append(pltpu.make_async_copy(core_ref, core_hbm, sems.at[n_f]))
    own = lax.axis_index("gx")
    for k, ref in enumerate(in_refs):
        held[lax.rem(own + count_x - k, count_x)] = ref[...]
    a_count = core_ref.shape[1]
    for pair in range(n_f // 2):
        at = (n_f * count_y + pair) * SUBLANES
        tiles = exchange([held[i, at : at + SUBLANES] for i in range(count_x)], LANES // SUBLANES)
        for place, tile in enumerate(tiles):
            core_ref[2 * pair + place // a_count, place % a_count] = tile
    leaving[n_f].start()
    pairs = count_y // 2
    lower = lax.broadcasted_iota(jnp.int32, (count_x, pairs, SUBLANES, LANES), 2) < HALF
    for f in range(n_f):
        at = pl.ds(f * count_y * SUBLANES, count_y * SUBLANES)
        tiles = held[:, at, :].reshape(count_x, pairs, 2, SUBLANES, LANES)
        even, odd = tiles[:, :, 0], tiles[:, :, 1]
        first = jnp.where(lower, even, pltpu.roll(odd, HALF, 2))
        second = jnp.where(lower, pltpu.roll(even, HALF, 2), odd)
        for octet, part in enumerate((first, second)):
            turned = part.reshape(LANES, LANES).T
            scatter_rows(turned, octet, block_x, block_y, rebuilt_ref, f)
        leaving[f].start()
    for copy in leaving:
        copy.wait()


def z_plan(fields, factor_x, factor_y):
    n_f, block_x, block_y, n_z = fields.shape
    rank = factor_x.shape[1]
    count_x = lax.axis_size("gx")
    count_y = lax.axis_size("gy")
    devices = count_x * count_y
    pairs = devices // 2
    rescale = math.sqrt(float(block_x * count_x) * float(block_y * count_y)) / rank
    vmem = pl.BlockSpec(memory_space=pltpu.VMEM)
    hbm = pl.BlockSpec(memory_space=pltpu.HBM)
    f32 = jnp.float32

    def array(shape, dtype=f32):
        return jax.ShapeDtypeStruct(shape, dtype)

    def call(
        kernel, name, outs, scratch, operands, space=vmem, out_spaces=None, limit=32 * 1024 * 1024, cost=10**9
    ):
        return pl.pallas_call(
            kernel,
            out_shape=tuple(outs),
            in_specs=[space] * len(operands),
            out_specs=out_spaces or (vmem,) * len(outs),
            scratch_shapes=scratch,
            compiler_params=pltpu.CompilerParams(vmem_limit_bytes=limit),
            cost_estimate=pl.CostEstimate(flops=cost, bytes_accessed=0, transcendentals=0),
            name=name,
        )(*operands)

    def swap(blocks, tiles):
        blocks = blocks.reshape(devices, tiles, HALF, n_z)
        return lax.all_to_all(blocks, ("gx", "gy"), 0, 0, tiled=True)

    def pass_on(blocks, axis):
        count = len(blocks)
        moved = [
            lax.ppermute(block, axis, [(i, (i + k) % count) for i in range(count)])
            for k, block in enumerate(blocks)
            if k
        ]
        return [blocks[0]] + moved

    flat = (n_f, block_x * block_y, n_z)
    (packed,) = call(
        pack_kernel,
        "pack",
        [array((pairs, 2, 2 * n_f + 1, HALF, n_z))],
        [
            pltpu.VMEM((pairs, 2, 2 * n_f + 1, HALF, n_z), f32),
            pltpu.VMEM(flat, f32),
            pltpu.VMEM(factor_x.shape, f32),
            pltpu.VMEM(factor_y.shape, f32),
            pltpu.SemaphoreType.DMA((n_f + 2,)),
            pltpu.SemaphoreType.DMA((n_f + 1,)),
        ],
        (fields.reshape(flat), factor_x, factor_y),
        space=hbm,
        out_spaces=(hbm,),
        limit=None,
    )
    planes = swap(packed, 2 * n_f + 1).reshape(count_x, count_y, 2 * n_f + 1, HALF, n_z)
    extended = pltpu.VMEM((count_y, n_f, SUBLANES + 6, SUBLANES, LANES), f32)
    rows = SUBLANES * SUBLANES + HALF * SUBLANES
    sent, spread, *columns = call(
        functools.partial(main_kernel, n_f, count_x, count_y, rank, rescale),
        "sections",
        [
            array((count_x, count_y, 2 * n_f, HALF, n_z)),
            array((2, n_f * LANES, LANES), jnp.bfloat16),
        ]
        + [array((rows, LANES))] * count_y,
        [extended] * 3
        + [
            pltpu.VMEM((n_f, count_y, SUBLANES, SUBLANES, LANES), f32),
            pltpu.VMEM((count_y, rows, LANES), f32),
        ],
        (planes,),
    )
    columns = pass_on(columns, "gy")
    sent = swap(sent, 2 * n_f).reshape(pairs, 2, 2 * n_f, HALF, n_z)
    rows = (n_f * count_y + n_f // 2) * SUBLANES
    blocks = call(
        functools.partial(expand_kernel, n_f, count_x, count_y),
        "expand",
        [array((rows, LANES))] * count_x,
        [
            pltpu.VMEM((count_y,) + columns[0].shape, f32),
            pltpu.VMEM((count_x, rows, LANES), f32),
        ],
        (spread, *columns),
        cost=20000000000,
    )
    blocks = pass_on(blocks, "gx")
    (advanced,) = call(
        functools.partial(advanced_kernel, block_x, block_y),
        "advanced",
        [array(flat)],
        [pltpu.VMEM(flat, f32), pltpu.SemaphoreType.DMA((n_f,))],
        (sent,),
        out_spaces=(hbm,),
    )
    rebuilt, core = call(
        functools.partial(rebuilt_kernel, block_x, block_y, count_x, count_y),
        "rebuilt",
        [array(flat), array((n_f, rank // count_x, rank // count_y, n_z))],
        [
            pltpu.VMEM((count_x, rows, LANES), f32),
            pltpu.VMEM(flat, f32),
            pltpu.VMEM((n_f, rank // count_x, rank // count_y, n_z), f32),
            pltpu.SemaphoreType.DMA((n_f + 1,)),
        ],
        tuple(blocks),
        out_spaces=(hbm, hbm),
        cost=1000000000,
    )
    return advanced.reshape(fields.shape), core, rebuilt.reshape(fields.shape)


def extended(block, sides, width):
    for axis, dim in sides:
        count = lax.axis_size(axis)
        forward = [(i, i + 1) for i in range(count - 1)]
        forward.append((count - 1, 0))
        backward = [(target, source) for source, target in forward]
        low = lax.ppermute(
            lax.slice_in_dim(block, block.shape[dim] - width, None, axis=dim), axis, forward
        )
        high = lax.ppermute(lax.slice_in_dim(block, 0, width, axis=dim), axis, backward)
        block = jnp.concatenate([low, block, high], axis=dim)
    return block


def inner_part(array, margin):
    return array[:, margin : array.shape[1] - margin, margin : array.shape[2] - margin]


def tendency(padded):
    n_x = padded.shape[1]
    n_y = padded.shape[2]
    pressure = 0.5 * padded[3]
    flux_x = padded[0][None] * padded
    flux_x = flux_x.at[0].add(pressure)
    flux_y = padded[1][None] * padded
    flux_y = flux_y.at[1].add(pressure)

    def along_x(shift):
        return (
            flux_x[:, 3 + shift : n_x - 3 + shift, 3 : n_y - 3]
            - flux_x[:, 3 - shift : n_x - 3 - shift, 3 : n_y - 3]
        )

    def along_y(shift):
        return (
            flux_y[:, 3 : n_x - 3, 3 + shift : n_y - 3 + shift]
            - flux_y[:, 3 : n_x - 3, 3 - shift : n_y - 3 - shift]
        )

    deriv_x = (45.0 * along_x(1) - 9.0 * along_x(2) + along_x(3)) / 60.0
    deriv_y = (45.0 * along_y(1) - 9.0 * along_y(2) + along_y(3)) / 60.0
    center = inner_part(padded, 3)
    react = REACT_RATE * center[2] * (1.0 + jnp.tanh(center[3]))
    zeros = jnp.zeros_like(react)
    source = jnp.stack([zeros, zeros, -react, HEAT_RELEASE * react])
    return source - deriv_x - deriv_y


def section_tendency(state):
    padded = extended(state, (("gx", 1), ("gy", 2)), 3)
    return tendency(padded)


def per_device(fields, factor_x, factor_y):
    high = lax.Precision.HIGHEST
    section_one = fields + TIME_STEP * section_tendency(fields)
    section_two = 0.75 * fields + 0.25 * (section_one + TIME_STEP * section_tendency(section_one))
    advanced = 1.0 / 3.0 * fields + 2.0 / 3.0 * (
        section_two + TIME_STEP * section_tendency(section_two)
    )
    rank_full = factor_x.shape[1]
    count_x = lax.axis_size("gx")
    count_y = lax.axis_size("gy")
    partial_x = jnp.einsum("fxyz,xa->fayz", advanced, factor_x, precision=high)
    partial_value = lax.psum_scatter(partial_x, "gx", scatter_dimension=1, tiled=True)
    local_core = jnp.einsum("fayz,yb->fabz", partial_value, factor_y, precision=high)
    core_tensor = lax.psum_scatter(local_core, "gy", scatter_dimension=2, tiled=True)
    weights = factor_y
    columns = jnp.einsum(
        "fabz,yb->fayz",
        lax.all_gather(core_tensor, "gy", axis=2, tiled=True),
        weights,
        precision=high,
    )
    weights = factor_x
    expanded = jnp.einsum(
        "fayz,xa->fxyz", lax.all_gather(columns, "gx", axis=1, tiled=True), weights, precision=high
    )
    total_x = factor_x.shape[0] * count_x
    total_y = factor_y.shape[0] * count_y
    rescale = math.sqrt(float(total_x) * float(total_y)) / rank_full
    rebuilt = rescale * expanded
    return (advanced, core_tensor, rebuilt)


def solution(mesh):
    placed = (P(None, "gx", "gy", None), P("gx", None), P("gy", None))
    out = P(None, "gx", "gy", None)

    def whole(fields, factor_x, factor_y):
        plan = z_plan if fits(mesh, fields, factor_x, factor_y) else per_device
        return jax.shard_map(
            plan, mesh=mesh, in_specs=placed, out_specs=(out, out, out), check_vma=False
        )(fields, factor_x, factor_y)

    return whole
```

```python
import functools
import math

import jax
import jax.numpy as jnp
from jax import lax
from jax.experimental import pallas as pl
from jax.experimental.pallas import tpu as pltpu
from jax.sharding import PartitionSpec as P

TIME_STEP = 0.2
REACT_RATE = 0.5
HEAT_RELEASE = 1.0
SUBLANES = 8
LANES = 128
HALF = SUBLANES // 2


def fits(mesh, fields, factor_x, factor_y):
    n_f, n_x, n_y, n_z = fields.shape
    count_x, count_y = mesh.shape["gx"], mesh.shape["gy"]
    devices = count_x * count_y
    rank = factor_x.shape[1]
    if n_x % count_x or n_y % count_y or n_z % devices:
        return False
    block_x, block_y, block_z = n_x // count_x, n_y // count_y, n_z // devices
    return (
        n_x == LANES
        and n_z == LANES
        and n_f == HALF
        and block_z == HALF
        and block_x == 2 * SUBLANES
        and block_y == 2 * SUBLANES
        and count_x == SUBLANES
        and count_y == HALF
        and rank == count_y * SUBLANES
        and factor_y.shape[1] == rank
        and n_f * rank == LANES
    )


def exchange(blocks, stride):
    count = len(blocks)
    period = stride * count
    group = lax.broadcasted_iota(jnp.int32, (SUBLANES, LANES), 1) // stride % count
    if period == LANES:
        blocks = [pltpu.roll(b, i * stride, 1) if i else b for i, b in enumerate(blocks)]
        step = 1
        while step < count:
            taken = (group & step) != 0
            blocks = [
                jnp.where(taken, blocks[(i + step) % count], blocks[i]) for i in range(count)
            ]
            step *= 2
        blocks = [blocks[-j % count] for j in range(count)]
        return [pltpu.roll(b, LANES - j * stride, 1) if j else b for j, b in enumerate(blocks)]
    blocks = list(blocks)
    step = 1
    while step < count:
        upper = (group & step) != 0
        for i in range(count):
            if i & step:
                continue
            low, high = blocks[i], blocks[i + step]
            blocks[i] = jnp.where(upper, pltpu.roll(high, stride * step, 1), low)
            blocks[i + step] = jnp.where(upper, high, pltpu.roll(low, LANES - stride * step, 1))
        step *= 2
    return blocks


def pack_kernel(fields_hbm, factor_x_hbm, factor_y_hbm, out_ref, fields_ref, x_ref, y_ref, sems):
    n_f, rows, _ = fields_ref.shape
    block_x = x_ref.shape[0]
    block_y = rows // block_x
    tiles = LANES // SUBLANES
    copies = [
        pltpu.make_async_copy(fields_hbm.at[f], fields_ref.at[f], sems.at[f]) for f in range(n_f)
    ]
    copies.append(pltpu.make_async_copy(factor_x_hbm, x_ref, sems.at[n_f]))
    copies.append(pltpu.make_async_copy(factor_y_hbm, y_ref, sems.at[n_f + 1]))
    for copy in copies:
        copy.start()
    for f in range(n_f):
        copies[f].wait()
        for octet in range(2):
            matrix = jnp.concatenate(
                [
                    fields_ref[f, pl.ds(octet * SUBLANES + y, block_x, stride=block_y), :]
                    for y in range(SUBLANES)
                ],
                axis=0,
            )
            turned = matrix.T.reshape(tiles, SUBLANES, LANES)
            out_ref[:, 0, 2 * f + octet] = turned[:, :HALF]
            out_ref[:, 1, 2 * f + octet] = turned[:, HALF:]
    copies[n_f].wait()
    copies[n_f + 1].wait()
    part_x = lax.axis_index("gy")
    part_y = lax.rem(lax.axis_index("gx"), block_y // HALF)
    own_x = x_ref[pl.ds(part_x * HALF, HALF), :]
    own_y = y_ref[pl.ds(part_y * HALF, HALF), :]
    factors = jnp.concatenate([own_x, own_y, own_y, own_y], axis=1)
    out_ref[:, :, 2 * n_f] = jnp.broadcast_to(factors[None, None], (tiles, 2, HALF, LANES))


def split(value):
    high = value.astype(jnp.bfloat16)
    low = (value - high.astype(jnp.float32)).astype(jnp.bfloat16)
    return high, low


def mul(a, b, dims=((1,), (0,))):
    return lax.dot_general(a, b, (dims, ((), ())), preferred_element_type=jnp.float32)


def mul_split(a, b, dims=((1,), (0,))):
    return mul(a[0], b[0], dims) + (mul(a[0], b[1], dims) + mul(a[1], b[0], dims))


def main_kernel(
    n_f, count_x, count_y, rank, rescale, in_ref, sent_hbm, spread_ref, *refs
):
    column_refs = refs[:count_y]
    ext_a, ext_b, ext_c, adv, staged, sent_ref, sent_sem = refs[count_y:]
    margin = 3
    inner = pl.ds(margin, SUBLANES)
    lower = lax.broadcasted_iota(jnp.int32, (margin, SUBLANES, LANES), 1) < HALF

    def each(body):
        def step(s, carry):
            body(s)
            return carry

        lax.fori_loop(0, count_y, step, 0, unroll=True)

    def fill_margins(ext):
        def one(s):
            before = lax.rem(s + count_y - 1, count_y)
            after = lax.rem(s + 1, count_y)
            for f in range(n_f):
                old = ext[before, f, pl.ds(SUBLANES, margin)]
                own = ext[s, f, pl.ds(SUBLANES, margin)]
                ext[s, f, 0:margin] = pltpu.roll(jnp.where(lower, own, old), HALF, 1)
                own = ext[s, f, pl.ds(margin, margin)]
                new = ext[after, f, pl.ds(margin, margin)]
                ext[s, f, pl.ds(SUBLANES + margin, margin)] = pltpu.roll(
                    jnp.where(lower, new, own), HALF, 1
                )

        each(one)

    row = lax.broadcasted_iota(jnp.int32, (LANES, LANES), 0)
    col = lax.broadcasted_iota(jnp.int32, (LANES, LANES), 1)
    ahead = (row - col) & (LANES - 1)
    taps = jnp.zeros((LANES, LANES), jnp.float32)
    for shift, weight in ((1, 45.0), (2, -9.0), (3, 1.0)):
        taps = jnp.where(ahead == shift, weight, taps)
        taps = jnp.where(ahead == LANES - shift, -weight, taps)
    taps = taps.astype(jnp.bfloat16)
    taps = jnp.concatenate([taps, taps], axis=0)

    def section(ext, step, store):
        def one(s):
            padded = [ext[s, f] for f in range(n_f)]
            center = [p[margin : margin + SUBLANES] for p in padded]
            flux_x = [center[0] * c for c in center]
            flux_x[0] = flux_x[0] + 0.5 * center[3]
            flat = jnp.concatenate(flux_x, axis=0).reshape(n_f * SUBLANES * SUBLANES, LANES)
            along_x = mul(jnp.concatenate(split(flat), axis=1), taps)
            along_x = along_x.reshape(n_f, SUBLANES, SUBLANES, LANES)
            react = (step * REACT_RATE) * center[2] * (1.0 + jnp.tanh(center[3]))
            for f in range(n_f):
                flux_y = padded[1] * padded[f]
                if f == 1:
                    flux_y = flux_y + 0.5 * padded[3]

                def along_y(k):
                    after = flux_y[margin + k : margin + k + SUBLANES]
                    return after - flux_y[margin - k : margin - k + SUBLANES]

                change = (
                    (-45.0 * step / 60.0) * along_y(1)
                    + (9.0 * step / 60.0) * along_y(2)
                    + (-step / 60.0) * (along_y(3) + along_x[f])
                )
                if f == 2:
                    change = change - react
                if f == 3:
                    change = change + HEAT_RELEASE * react
                store(s, f, center[f], change)

        each(one)

    def arrive(s):
        for f in range(n_f):
            got = [
                in_ref[i, s, 2 * f : 2 * f + 2].reshape(SUBLANES, LANES) for i in range(count_x)
            ]
            for y, block in enumerate(exchange(got, LANES // SUBLANES)):
                ext_a[s, f, margin + y] = block

    def first(s, f, center, change):
        ext_b[s, f, inner] = center + change

    def second(s, f, center, change):
        ext_c[s, f, inner] = 0.75 * ext_a[s, f, inner] + (0.25 * center + change)

    def third(s, f, center, change):
        done = (1.0 / 3.0) * ext_a[s, f, inner] + ((2.0 / 3.0) * center + change)
        adv[f, s] = done
        parts = exchange([done[y] for y in range(SUBLANES)], LANES // SUBLANES)
        for i, part in enumerate(parts):
            sent_ref[i, s, 2 * f : 2 * f + 2] = part.reshape(2, HALF, LANES)

    each(arrive)
    fill_margins(ext_a)
    section(ext_a, TIME_STEP, first)
    fill_margins(ext_b)
    section(ext_b, 0.25 * TIME_STEP, second)
    fill_margins(ext_c)
    section(ext_c, 2.0 / 3.0 * TIME_STEP, third)
    sent = pltpu.make_async_copy(sent_ref, sent_hbm, sent_sem)
    sent.start()

    @pl.when(lax.axis_index("gy") >= 0)
    def tucker():
        plane = count_y * SUBLANES * SUBLANES
        held = in_ref[:, :, 2 * n_f].reshape(LANES, LANES)
        held_x = split(held)
        held_y = split(jnp.where(col < rank, pltpu.roll(held, LANES - rank, 1), held))
        picks = (row == col // n_f).astype(jnp.bfloat16)
        spread_x = [mul(part, picks) for part in held_x]
        weights_x = [
            jnp.concatenate(
                [jnp.where(col % n_f == f, part, 0.0).astype(jnp.bfloat16) for f in range(n_f)], axis=0
            )
            for part in spread_x
        ]
        r = lax.broadcasted_iota(jnp.int32, (plane, LANES), 0)
        c = lax.broadcasted_iota(jnp.int32, (plane, LANES), 1)
        from_s, from_y = r // (SUBLANES * SUBLANES), (r // HALF) % 2 * SUBLANES + (r // SUBLANES) % SUBLANES
        block_x = LANES // count_x
        held_at = from_y // HALF * block_x + from_s * HALF + from_y % HALF
        picks = (held_at == c).astype(jnp.bfloat16)
        same_z = r % HALF == c // rank
        weights_y = [jnp.where(same_z, mul(picks, part), 0.0).astype(jnp.bfloat16) for part in held_y]

        def by_x(value):
            return jnp.concatenate([value[f].reshape(plane, LANES) for f in range(n_f)], axis=1)

        partial = mul_split(split(by_x(adv)), weights_x)
        core = mul_split(weights_y, split(partial), ((0,), (0,)))
        columns = rescale * mul_split(weights_y, split(core))
        for part in range(2):
            spread_ref[part] = weights_x[part]

        block = plane // count_y
        for s in range(count_y):
            staged[s, 0:block] = columns[s * block : (s + 1) * block]
            for z in range(HALF):
                at = z * rank + s * SUBLANES
                staged[s, block + z * SUBLANES : block + (z + 1) * SUBLANES] = core[at : at + SUBLANES]
        own = lax.axis_index("gy")
        for k, ref in enumerate(column_refs):
            ref[...] = staged[lax.rem(own + k, count_y)]

    sent.wait()


def expand_kernel(n_f, count_x, count_y, spread_ref, *refs):
    in_refs, out_refs = refs[:count_y], refs[count_y : count_y + count_x]
    held, staged = refs[count_y + count_x :]
    own = lax.axis_index("gy")
    for k, ref in enumerate(in_refs):
        held[lax.rem(own + count_y - k, count_y)] = ref[...]
    block = SUBLANES * SUBLANES
    plane = count_y * block
    columns = split(jnp.concatenate([held[s, 0:block] for s in range(count_y)], axis=0))
    for f in range(n_f):
        weights = [spread_ref[part, f * LANES : (f + 1) * LANES] for part in range(2)]
        rebuilt = mul_split(columns, weights, ((1,), (1,)))
        rebuilt = rebuilt.reshape(count_y, SUBLANES, SUBLANES, LANES)
        for s in range(count_y):
            parts = exchange([rebuilt[s, y] for y in range(SUBLANES)], LANES // SUBLANES)
            for i, part in enumerate(parts):
                at = (f * count_y + s) * SUBLANES
                staged[i, at : at + SUBLANES] = part
    by_f = [
        exchange([held[s, block + z * SUBLANES : block + (z + 1) * SUBLANES] for z in range(HALF)], 1)
        for s in range(count_y)
    ]
    left = lax.broadcasted_iota(jnp.int32, (SUBLANES, LANES), 1) < LANES // 2
    by_i = []
    for f in range(n_f):
        tiles = exchange([by_f[s][f] for s in range(count_y)], HALF)
        by_i.append(exchange(tiles, LANES // SUBLANES))
    for i in range(count_x):
        for pair in range(n_f // 2):
            low, high = by_i[2 * pair][i % HALF], by_i[2 * pair + 1][i % HALF]
            if i < HALF:
                tile = jnp.where(left, low, pltpu.roll(high, LANES // 2, 1))
            else:
                tile = jnp.where(left, pltpu.roll(low, LANES // 2, 1), high)
            at = (n_f * count_y + pair) * SUBLANES
            staged[i, at : at + SUBLANES] = tile
    own = lax.axis_index("gx")
    for k, ref in enumerate(out_refs):
        ref[...] = staged[lax.rem(own + k, count_x)]


def leave_fields(ref, hbm, sems):
    return [
        pltpu.make_async_copy(ref.at[f], hbm.at[f], sems.at[f]) for f in range(ref.shape[0])
    ]


def scatter_rows(turned, octet, block_x, block_y, target, f):
    for y in range(SUBLANES):
        rows = pl.ds(octet * SUBLANES + y, block_x, stride=block_y)
        target[f, rows, :] = turned[y * block_x : (y + 1) * block_x]


def advanced_kernel(block_x, block_y, in_ref, advanced_hbm, advanced_ref, sems):
    leaving = leave_fields(advanced_ref, advanced_hbm, sems)
    for f in range(advanced_ref.shape[0]):
        for octet in range(2):
            place = 2 * f + octet
            matrix = jnp.concatenate([in_ref[:, 0, place], in_ref[:, 1, place]], axis=1)
            turned = matrix.reshape(LANES, LANES).T
            scatter_rows(turned, octet, block_x, block_y, advanced_ref, f)
        leaving[f].start()
    for copy in leaving:
        copy.wait()


def rebuilt_kernel(block_x, block_y, count_x, count_y, *refs):
    in_refs, (rebuilt_hbm, core_hbm, held, rebuilt_ref, core_ref, sems) = refs[:count_x], refs[count_x:]
    n_f = rebuilt_ref.shape[0]
    leaving = leave_fields(rebuilt_ref, rebuilt_hbm, sems)
    leaving.append(pltpu.make_async_copy(core_ref, core_hbm, sems.at[n_f]))
    own = lax.axis_index("gx")
    for k, ref in enumerate(in_refs):
        held[lax.rem(own + count_x - k, count_x)] = ref[...]
    a_count = core_ref.shape[1]
    for pair in range(n_f // 2):
        at = (n_f * count_y + pair) * SUBLANES
        tiles = exchange([held[i, at : at + SUBLANES] for i in range(count_x)], LANES // SUBLANES)
        for place, tile in enumerate(tiles):
            core_ref[2 * pair + place // a_count, place % a_count] = tile
    leaving[n_f].start()
    pairs = count_y // 2
    lower = lax.broadcasted_iota(jnp.int32, (count_x, pairs, SUBLANES, LANES), 2) < HALF
    for f in range(n_f):
        at = pl.ds(f * count_y * SUBLANES, count_y * SUBLANES)
        tiles = held[:, at, :].reshape(count_x, pairs, 2, SUBLANES, LANES)
        even, odd = tiles[:, :, 0], tiles[:, :, 1]
        first = jnp.where(lower, even, pltpu.roll(odd, HALF, 2))
        second = jnp.where(lower, pltpu.roll(even, HALF, 2), odd)
        for octet, part in enumerate((first, second)):
            turned = part.reshape(LANES, LANES).T
            scatter_rows(turned, octet, block_x, block_y, rebuilt_ref, f)
        leaving[f].start()
    for copy in leaving:
        copy.wait()


def z_plan(fields, factor_x, factor_y):
    n_f, block_x, block_y, n_z = fields.shape
    rank = factor_x.shape[1]
    count_x = lax.axis_size("gx")
    count_y = lax.axis_size("gy")
    devices = count_x * count_y
    pairs = devices // 2
    rescale = math.sqrt(float(block_x * count_x) * float(block_y * count_y)) / rank
    vmem = pl.BlockSpec(memory_space=pltpu.VMEM)
    hbm = pl.BlockSpec(memory_space=pltpu.HBM)
    f32 = jnp.float32

    def array(shape, dtype=f32):
        return jax.ShapeDtypeStruct(shape, dtype)

    def call(
        kernel, name, outs, scratch, operands, space=vmem, out_spaces=None, limit=32 * 1024 * 1024, cost=10**9
    ):
        return pl.pallas_call(
            kernel,
            out_shape=tuple(outs),
            in_specs=[space] * len(operands),
            out_specs=out_spaces or (vmem,) * len(outs),
            scratch_shapes=scratch,
            compiler_params=pltpu.CompilerParams(vmem_limit_bytes=limit),
            cost_estimate=pl.CostEstimate(flops=cost, bytes_accessed=0, transcendentals=0),
            name=name,
        )(*operands)

    def swap(blocks, tiles):
        blocks = blocks.reshape(devices, tiles, HALF, n_z)
        return lax.all_to_all(blocks, ("gx", "gy"), 0, 0, tiled=True)

    def pass_on(blocks, axis):
        count = len(blocks)
        moved = [
            lax.ppermute(block, axis, [(i, (i + k) % count) for i in range(count)])
            for k, block in enumerate(blocks)
            if k
        ]
        return [blocks[0]] + moved

    flat = (n_f, block_x * block_y, n_z)
    (packed,) = call(
        pack_kernel,
        "pack",
        [array((pairs, 2, 2 * n_f + 1, HALF, n_z))],
        [
            pltpu.VMEM(flat, f32),
            pltpu.VMEM(factor_x.shape, f32),
            pltpu.VMEM(factor_y.shape, f32),
            pltpu.SemaphoreType.DMA((n_f + 2,)),
        ],
        tuple(
            pltpu.with_memory_space_constraint(v, pltpu.HBM)
            for v in (fields.reshape(flat), factor_x, factor_y)
        ),
        space=hbm,
    )
    planes = swap(packed, 2 * n_f + 1).reshape(count_x, count_y, 2 * n_f + 1, HALF, n_z)
    extended = pltpu.VMEM((count_y, n_f, SUBLANES + 6, SUBLANES, LANES), f32)
    rows = SUBLANES * SUBLANES + HALF * SUBLANES
    sent, spread, *columns = call(
        functools.partial(main_kernel, n_f, count_x, count_y, rank, rescale),
        "sections",
        [
            array((count_x, count_y, 2 * n_f, HALF, n_z)),
            array((2, n_f * LANES, LANES), jnp.bfloat16),
        ]
        + [array((rows, LANES))] * count_y,
        [extended] * 3
        + [
            pltpu.VMEM((n_f, count_y, SUBLANES, SUBLANES, LANES), f32),
            pltpu.VMEM((count_y, rows, LANES), f32),
            pltpu.VMEM((count_x, count_y, 2 * n_f, HALF, n_z), f32),
            pltpu.SemaphoreType.DMA,
        ],
        (planes,),
        out_spaces=(hbm,) + (vmem,) * (1 + count_y),
    )
    columns = pass_on(columns, "gy")
    sent = swap(sent, 2 * n_f).reshape(pairs, 2, 2 * n_f, HALF, n_z)
    rows = (n_f * count_y + n_f // 2) * SUBLANES
    blocks = call(
        functools.partial(expand_kernel, n_f, count_x, count_y),
        "expand",
        [array((rows, LANES))] * count_x,
        [
            pltpu.VMEM((count_y,) + columns[0].shape, f32),
            pltpu.VMEM((count_x, rows, LANES), f32),
        ],
        (spread, *columns),
        cost=20000000000,
    )
    blocks = pass_on(blocks, "gx")
    (advanced,) = call(
        functools.partial(advanced_kernel, block_x, block_y),
        "advanced",
        [array(flat)],
        [pltpu.VMEM(flat, f32), pltpu.SemaphoreType.DMA((n_f,))],
        (sent,),
        out_spaces=(hbm,),
    )
    rebuilt, core = call(
        functools.partial(rebuilt_kernel, block_x, block_y, count_x, count_y),
        "rebuilt",
        [array(flat), array((n_f, rank // count_x, rank // count_y, n_z))],
        [
            pltpu.VMEM((count_x, rows, LANES), f32),
            pltpu.VMEM(flat, f32),
            pltpu.VMEM((n_f, rank // count_x, rank // count_y, n_z), f32),
            pltpu.SemaphoreType.DMA((n_f + 1,)),
        ],
        tuple(blocks),
        out_spaces=(hbm, hbm),
        cost=1000000000,
    )
    return advanced.reshape(fields.shape), core, rebuilt.reshape(fields.shape)


def extended(block, sides, width):
    for axis, dim in sides:
        count = lax.axis_size(axis)
        forward = [(i, i + 1) for i in range(count - 1)]
        forward.append((count - 1, 0))
        backward = [(target, source) for source, target in forward]
        low = lax.ppermute(
            lax.slice_in_dim(block, block.shape[dim] - width, None, axis=dim), axis, forward
        )
        high = lax.ppermute(lax.slice_in_dim(block, 0, width, axis=dim), axis, backward)
        block = jnp.concatenate([low, block, high], axis=dim)
    return block


def inner_part(array, margin):
    return array[:, margin : array.shape[1] - margin, margin : array.shape[2] - margin]


def tendency(padded):
    n_x = padded.shape[1]
    n_y = padded.shape[2]
    pressure = 0.5 * padded[3]
    flux_x = padded[0][None] * padded
    flux_x = flux_x.at[0].add(pressure)
    flux_y = padded[1][None] * padded
    flux_y = flux_y.at[1].add(pressure)

    def along_x(shift):
        return (
            flux_x[:, 3 + shift : n_x - 3 + shift, 3 : n_y - 3]
            - flux_x[:, 3 - shift : n_x - 3 - shift, 3 : n_y - 3]
        )

    def along_y(shift):
        return (
            flux_y[:, 3 : n_x - 3, 3 + shift : n_y - 3 + shift]
            - flux_y[:, 3 : n_x - 3, 3 - shift : n_y - 3 - shift]
        )

    deriv_x = (45.0 * along_x(1) - 9.0 * along_x(2) + along_x(3)) / 60.0
    deriv_y = (45.0 * along_y(1) - 9.0 * along_y(2) + along_y(3)) / 60.0
    center = inner_part(padded, 3)
    react = REACT_RATE * center[2] * (1.0 + jnp.tanh(center[3]))
    zeros = jnp.zeros_like(react)
    source = jnp.stack([zeros, zeros, -react, HEAT_RELEASE * react])
    return source - deriv_x - deriv_y


def section_tendency(state):
    padded = extended(state, (("gx", 1), ("gy", 2)), 3)
    return tendency(padded)


def per_device(fields, factor_x, factor_y):
    high = lax.Precision.HIGHEST
    section_one = fields + TIME_STEP * section_tendency(fields)
    section_two = 0.75 * fields + 0.25 * (section_one + TIME_STEP * section_tendency(section_one))
    advanced = 1.0 / 3.0 * fields + 2.0 / 3.0 * (
        section_two + TIME_STEP * section_tendency(section_two)
    )
    rank_full = factor_x.shape[1]
    count_x = lax.axis_size("gx")
    count_y = lax.axis_size("gy")
    partial_x = jnp.einsum("fxyz,xa->fayz", advanced, factor_x, precision=high)
    partial_value = lax.psum_scatter(partial_x, "gx", scatter_dimension=1, tiled=True)
    local_core = jnp.einsum("fayz,yb->fabz", partial_value, factor_y, precision=high)
    core_tensor = lax.psum_scatter(local_core, "gy", scatter_dimension=2, tiled=True)
    weights = factor_y
    columns = jnp.einsum(
        "fabz,yb->fayz",
        lax.all_gather(core_tensor, "gy", axis=2, tiled=True),
        weights,
        precision=high,
    )
    weights = factor_x
    expanded = jnp.einsum(
        "fayz,xa->fxyz", lax.all_gather(columns, "gx", axis=1, tiled=True), weights, precision=high
    )
    total_x = factor_x.shape[0] * count_x
    total_y = factor_y.shape[0] * count_y
    rescale = math.sqrt(float(total_x) * float(total_y)) / rank_full
    rebuilt = rescale * expanded
    return (advanced, core_tensor, rebuilt)


def solution(mesh):
    placed = (P(None, "gx", "gy", None), P("gx", None), P("gy", None))
    out = P(None, "gx", "gy", None)

    def whole(fields, factor_x, factor_y):
        plan = z_plan if fits(mesh, fields, factor_x, factor_y) else per_device
        return jax.shard_map(
            plan, mesh=mesh, in_specs=placed, out_specs=(out, out, out), check_vma=False
        )(fields, factor_x, factor_y)

    return whole
```

```python
import functools
import math

import jax
import jax.numpy as jnp
from jax import lax
from jax.experimental import pallas as pl
from jax.experimental.pallas import tpu as pltpu
from jax.sharding import PartitionSpec as P

TIME_STEP = 0.2
REACT_RATE = 0.5
HEAT_RELEASE = 1.0
SUBLANES = 8
LANES = 128
HALF = SUBLANES // 2


def fits(mesh, fields, factor_x, factor_y):
    n_f, n_x, n_y, n_z = fields.shape
    count_x, count_y = mesh.shape["gx"], mesh.shape["gy"]
    devices = count_x * count_y
    rank = factor_x.shape[1]
    if n_x % count_x or n_y % count_y or n_z % devices:
        return False
    block_x, block_y, block_z = n_x // count_x, n_y // count_y, n_z // devices
    return (
        n_x == LANES
        and n_z == LANES
        and n_f == HALF
        and block_z == HALF
        and block_x == 2 * SUBLANES
        and block_y == 2 * SUBLANES
        and count_x == SUBLANES
        and count_y == HALF
        and rank == count_y * SUBLANES
        and factor_y.shape[1] == rank
        and n_f * rank == LANES
    )


def exchange(blocks, stride):
    count = len(blocks)
    period = stride * count
    group = lax.broadcasted_iota(jnp.int32, (SUBLANES, LANES), 1) // stride % count
    if period == LANES:
        blocks = [pltpu.roll(b, i * stride, 1) if i else b for i, b in enumerate(blocks)]
        step = 1
        while step < count:
            taken = (group & step) != 0
            blocks = [
                jnp.where(taken, blocks[(i + step) % count], blocks[i]) for i in range(count)
            ]
            step *= 2
        blocks = [blocks[-j % count] for j in range(count)]
        return [pltpu.roll(b, LANES - j * stride, 1) if j else b for j, b in enumerate(blocks)]
    blocks = list(blocks)
    step = 1
    while step < count:
        upper = (group & step) != 0
        for i in range(count):
            if i & step:
                continue
            low, high = blocks[i], blocks[i + step]
            blocks[i] = jnp.where(upper, pltpu.roll(high, stride * step, 1), low)
            blocks[i + step] = jnp.where(upper, high, pltpu.roll(low, LANES - stride * step, 1))
        step *= 2
    return blocks


def pack_kernel(fields_hbm, factor_x_hbm, factor_y_hbm, out_ref, fields_ref, x_ref, y_ref, sems):
    n_f, rows, _ = fields_ref.shape
    block_x = x_ref.shape[0]
    block_y = rows // block_x
    tiles = LANES // SUBLANES
    copies = [
        pltpu.make_async_copy(fields_hbm.at[f], fields_ref.at[f], sems.at[f]) for f in range(n_f)
    ]
    copies.append(pltpu.make_async_copy(factor_x_hbm, x_ref, sems.at[n_f]))
    copies.append(pltpu.make_async_copy(factor_y_hbm, y_ref, sems.at[n_f + 1]))
    for copy in copies:
        copy.start()
    for f in range(n_f):
        copies[f].wait()
        for octet in range(2):
            matrix = jnp.concatenate(
                [
                    fields_ref[f, pl.ds(octet * SUBLANES + y, block_x, stride=block_y), :]
                    for y in range(SUBLANES)
                ],
                axis=0,
            )
            turned = matrix.T.reshape(tiles, SUBLANES, LANES)
            for part in range(2):
                at = 2 * (2 * f + octet) + part
                out_ref[:, 0, at] = turned[:, 2 * part : 2 * part + 2]
                out_ref[:, 1, at] = turned[:, HALF + 2 * part : HALF + 2 * part + 2]
    copies[n_f].wait()
    copies[n_f + 1].wait()
    own_x = x_ref[pl.ds(lax.axis_index("gy") * HALF, HALF), :]
    own_y = y_ref[pl.ds(lax.axis_index("gx") * 2, 2), :]
    row_x = jnp.concatenate([own_x[j : j + 1] for j in range(HALF)], axis=1)
    row_y = jnp.concatenate([own_y[j % 2 : j % 2 + 1] for j in range(HALF)], axis=1)
    factors = jnp.concatenate([row_x, row_y], axis=0)
    out_ref[:, :, 4 * n_f] = jnp.broadcast_to(factors[None, None], (tiles, 2, 2, LANES))


def split(value):
    high = value.astype(jnp.bfloat16)
    low = (value - high.astype(jnp.float32)).astype(jnp.bfloat16)
    return high, low


def mul(a, b, dims=((1,), (0,))):
    return lax.dot_general(a, b, (dims, ((), ())), preferred_element_type=jnp.float32)


def mul_split(a, b, dims=((1,), (0,))):
    return mul(a[0], b[0], dims) + (mul(a[0], b[1], dims) + mul(a[1], b[0], dims))


def main_kernel(
    n_f, count_x, count_y, rank, rescale, in_ref, sent_hbm, spread_ref, *refs
):
    column_refs = refs[:count_y]
    ext_a, ext_b, ext_c, adv, staged, sent_ref, sent_sem = refs[count_y : count_y + 7]
    to_core_ref, project_ref = refs[count_y + 7 :]
    margin = 3
    inner = pl.ds(margin, SUBLANES)
    lower = lax.broadcasted_iota(jnp.int32, (margin, SUBLANES, LANES), 1) < HALF

    def each(body):
        def step(s, carry):
            body(s)
            return carry

        lax.fori_loop(0, count_y, step, 0, unroll=True)

    def fill_margins(ext):
        def one(s):
            before = lax.rem(s + count_y - 1, count_y)
            after = lax.rem(s + 1, count_y)
            for f in range(n_f):
                old = ext[before, f, pl.ds(SUBLANES, margin)]
                own = ext[s, f, pl.ds(SUBLANES, margin)]
                ext[s, f, 0:margin] = pltpu.roll(jnp.where(lower, own, old), HALF, 1)
                own = ext[s, f, pl.ds(margin, margin)]
                new = ext[after, f, pl.ds(margin, margin)]
                ext[s, f, pl.ds(SUBLANES + margin, margin)] = pltpu.roll(
                    jnp.where(lower, new, own), HALF, 1
                )

        each(one)

    row = lax.broadcasted_iota(jnp.int32, (LANES, LANES), 0)
    col = lax.broadcasted_iota(jnp.int32, (LANES, LANES), 1)
    ahead = (row - col) & (LANES - 1)
    taps = jnp.zeros((LANES, LANES), jnp.float32)
    for shift, weight in ((1, 45.0), (2, -9.0), (3, 1.0)):
        taps = jnp.where(ahead == shift, weight, taps)
        taps = jnp.where(ahead == LANES - shift, -weight, taps)
    taps = taps.astype(jnp.bfloat16)
    taps = jnp.concatenate([taps, taps], axis=0)

    def section(ext, step, store):
        def one(s):
            padded = [ext[s, f] for f in range(n_f)]
            center = [p[margin : margin + SUBLANES] for p in padded]
            flux_x = [center[0] * c for c in center]
            flux_x[0] = flux_x[0] + 0.5 * center[3]
            flat = jnp.concatenate(flux_x, axis=0).reshape(n_f * SUBLANES * SUBLANES, LANES)
            along_x = mul(jnp.concatenate(split(flat), axis=1), taps)
            along_x = along_x.reshape(n_f, SUBLANES, SUBLANES, LANES)
            react = (step * REACT_RATE) * center[2] * (1.0 + jnp.tanh(center[3]))
            for f in range(n_f):
                flux_y = padded[1] * padded[f]
                if f == 1:
                    flux_y = flux_y + 0.5 * padded[3]

                def along_y(k):
                    after = flux_y[margin + k : margin + k + SUBLANES]
                    return after - flux_y[margin - k : margin - k + SUBLANES]

                change = (
                    (-45.0 * step / 60.0) * along_y(1)
                    + (9.0 * step / 60.0) * along_y(2)
                    + (-step / 60.0) * (along_y(3) + along_x[f])
                )
                if f == 2:
                    change = change - react
                if f == 3:
                    change = change + HEAT_RELEASE * react
                store(s, f, center[f], change)

        each(one)

    def arrive(s):
        for f in range(n_f):
            got = [
                in_ref[i, s, 4 * f : 4 * f + 4].reshape(SUBLANES, LANES) for i in range(count_x)
            ]
            for y, block in enumerate(exchange(got, LANES // SUBLANES)):
                ext_a[s, f, margin + y] = block

    def first(s, f, center, change):
        ext_b[s, f, inner] = center + change

    def second(s, f, center, change):
        ext_c[s, f, inner] = 0.75 * ext_a[s, f, inner] + (0.25 * center + change)

    def third(s, f, center, change):
        done = (1.0 / 3.0) * ext_a[s, f, inner] + ((2.0 / 3.0) * center + change)
        adv[f, s] = done
        parts = exchange([done[y] for y in range(SUBLANES)], LANES // SUBLANES)
        for i, part in enumerate(parts):
            sent_ref[i, s, 2 * f : 2 * f + 2] = part.reshape(2, HALF, LANES)

    plane = count_y * SUBLANES * SUBLANES
    count = count_x * count_y
    held = in_ref[:, :, 4 * n_f].reshape(2 * count, LANES)
    held_at = lax.broadcasted_iota(jnp.int32, (LANES, 2 * count), 1)
    source = lax.broadcasted_iota(jnp.int32, (LANES, 2 * count), 0) // HALF
    rows_of = (held_at == 2 * source).astype(jnp.bfloat16)
    spread_x = [jnp.where(row % HALF == col // rank, mul(rows_of, part), 0.0) for part in split(held)]
    picks = (row % rank == col // n_f).astype(jnp.bfloat16)
    spread_x = [mul(part.astype(jnp.bfloat16), picks) for part in spread_x]
    weights_x = [
        jnp.concatenate(
            [jnp.where(col % n_f == f, part, 0.0).astype(jnp.bfloat16) for f in range(n_f)], axis=0
        )
        for part in spread_x
    ]
    r = lax.broadcasted_iota(jnp.int32, (plane, LANES), 0)
    c = lax.broadcasted_iota(jnp.int32, (plane, LANES), 1)
    from_s, from_y = r // (SUBLANES * SUBLANES), (r // HALF) % 2 * SUBLANES + (r // SUBLANES) % SUBLANES
    held_at = lax.broadcasted_iota(jnp.int32, (plane, 2 * count), 1)
    source = (from_y // 2 * count_y + from_s)[:, : 2 * count]
    rows_of = (held_at == 2 * source + 1).astype(jnp.bfloat16)
    spread_y = [jnp.where(from_y % 2 == c // rank % 2, mul(rows_of, part), 0.0) for part in split(held)]
    spread_y = [part + pltpu.roll(part, rank, 1) for part in spread_y]
    same_z = r % HALF == c // rank
    weights_y = [jnp.where(same_z, part, 0.0).astype(jnp.bfloat16) for part in spread_y]
    for part in range(2):
        spread_ref[part] = weights_x[part]
        to_core_ref[part] = weights_y[part].astype(jnp.float32).T.astype(jnp.bfloat16)
    projector = split(rescale * mul_split(weights_y, weights_y, ((1,), (1,))))
    for part in range(2):
        project_ref[part] = projector[part]

    each(arrive)
    fill_margins(ext_a)
    section(ext_a, TIME_STEP, first)
    fill_margins(ext_b)
    section(ext_b, 0.25 * TIME_STEP, second)
    fill_margins(ext_c)
    section(ext_c, 2.0 / 3.0 * TIME_STEP, third)
    sent = pltpu.make_async_copy(sent_ref, sent_hbm, sent_sem)
    sent.start()

    @pl.when(lax.axis_index("gy") >= 0)
    def tucker():
        def by_x(value):
            return jnp.concatenate([value[f].reshape(plane, LANES) for f in range(n_f)], axis=1)

        weights_x = [spread_ref[part] for part in range(2)]
        partial = split(mul_split(split(by_x(adv)), weights_x))
        core = mul_split([to_core_ref[part] for part in range(2)], partial)
        columns = mul_split([project_ref[part] for part in range(2)], partial)

        block = plane // count_y
        for s in range(count_y):
            staged[s, 0:block] = columns[s * block : (s + 1) * block]
            for z in range(HALF):
                at = z * rank + s * SUBLANES
                staged[s, block + z * SUBLANES : block + (z + 1) * SUBLANES] = core[at : at + SUBLANES]
        own = lax.axis_index("gy")
        for k, ref in enumerate(column_refs):
            ref[...] = staged[lax.rem(own + k, count_y)]

    sent.wait()


def expand_kernel(n_f, count_x, count_y, spread_ref, *refs):
    in_refs, out_refs = refs[:count_y], refs[count_y : count_y + count_x]
    held, staged = refs[count_y + count_x :]
    own = lax.axis_index("gy")
    for k, ref in enumerate(in_refs):
        held[lax.rem(own + count_y - k, count_y)] = ref[...]
    block = SUBLANES * SUBLANES
    plane = count_y * block
    columns = split(jnp.concatenate([held[s, 0:block] for s in range(count_y)], axis=0))
    for f in range(n_f):
        weights = [spread_ref[part, f * LANES : (f + 1) * LANES] for part in range(2)]
        rebuilt = mul_split(columns, weights, ((1,), (1,)))
        rebuilt = rebuilt.reshape(count_y, SUBLANES, SUBLANES, LANES)
        for s in range(count_y):
            parts = exchange([rebuilt[s, y] for y in range(SUBLANES)], LANES // SUBLANES)
            for i, part in enumerate(parts):
                at = (f * count_y + s) * SUBLANES
                staged[i, at : at + SUBLANES] = part
    by_f = [
        exchange([held[s, block + z * SUBLANES : block + (z + 1) * SUBLANES] for z in range(HALF)], 1)
        for s in range(count_y)
    ]
    left = lax.broadcasted_iota(jnp.int32, (SUBLANES, LANES), 1) < LANES // 2
    by_i = []
    for f in range(n_f):
        tiles = exchange([by_f[s][f] for s in range(count_y)], HALF)
        by_i.append(exchange(tiles, LANES // SUBLANES))
    for i in range(count_x):
        for pair in range(n_f // 2):
            low, high = by_i[2 * pair][i % HALF], by_i[2 * pair + 1][i % HALF]
            if i < HALF:
                tile = jnp.where(left, low, pltpu.roll(high, LANES // 2, 1))
            else:
                tile = jnp.where(left, pltpu.roll(low, LANES // 2, 1), high)
            at = (n_f * count_y + pair) * SUBLANES
            staged[i, at : at + SUBLANES] = tile
    own = lax.axis_index("gx")
    for k, ref in enumerate(out_refs):
        ref[...] = staged[lax.rem(own + k, count_x)]


def leave_fields(ref, hbm, sems):
    return [
        pltpu.make_async_copy(ref.at[f], hbm.at[f], sems.at[f]) for f in range(ref.shape[0])
    ]


def scatter_rows(turned, octet, block_x, block_y, target, f):
    for y in range(SUBLANES):
        rows = pl.ds(octet * SUBLANES + y, block_x, stride=block_y)
        target[f, rows, :] = turned[y * block_x : (y + 1) * block_x]


def advanced_kernel(block_x, block_y, in_ref, advanced_hbm, advanced_ref, sems):
    leaving = leave_fields(advanced_ref, advanced_hbm, sems)
    for f in range(advanced_ref.shape[0]):
        for octet in range(2):
            place = 2 * f + octet
            matrix = jnp.concatenate([in_ref[:, 0, place], in_ref[:, 1, place]], axis=1)
            turned = matrix.reshape(LANES, LANES).T
            scatter_rows(turned, octet, block_x, block_y, advanced_ref, f)
        leaving[f].start()
    for copy in leaving:
        copy.wait()


def rebuilt_kernel(block_x, block_y, count_x, count_y, *refs):
    in_refs, (rebuilt_hbm, core_hbm, held, rebuilt_ref, core_ref, sems) = refs[:count_x], refs[count_x:]
    n_f = rebuilt_ref.shape[0]
    leaving = leave_fields(rebuilt_ref, rebuilt_hbm, sems)
    leaving.append(pltpu.make_async_copy(core_ref, core_hbm, sems.at[n_f]))
    own = lax.axis_index("gx")
    for k, ref in enumerate(in_refs):
        held[lax.rem(own + count_x - k, count_x)] = ref[...]
    a_count = core_ref.shape[1]
    for pair in range(n_f // 2):
        at = (n_f * count_y + pair) * SUBLANES
        tiles = exchange([held[i, at : at + SUBLANES] for i in range(count_x)], LANES // SUBLANES)
        for place, tile in enumerate(tiles):
            core_ref[2 * pair + place // a_count, place % a_count] = tile
    leaving[n_f].start()
    pairs = count_y // 2
    lower = lax.broadcasted_iota(jnp.int32, (count_x, pairs, SUBLANES, LANES), 2) < HALF
    for f in range(n_f):
        at = pl.ds(f * count_y * SUBLANES, count_y * SUBLANES)
        tiles = held[:, at, :].reshape(count_x, pairs, 2, SUBLANES, LANES)
        even, odd = tiles[:, :, 0], tiles[:, :, 1]
        first = jnp.where(lower, even, pltpu.roll(odd, HALF, 2))
        second = jnp.where(lower, pltpu.roll(even, HALF, 2), odd)
        for octet, part in enumerate((first, second)):
            turned = part.reshape(LANES, LANES).T
            scatter_rows(turned, octet, block_x, block_y, rebuilt_ref, f)
        leaving[f].start()
    for copy in leaving:
        copy.wait()


def z_plan(fields, factor_x, factor_y):
    n_f, block_x, block_y, n_z = fields.shape
    rank = factor_x.shape[1]
    count_x = lax.axis_size("gx")
    count_y = lax.axis_size("gy")
    devices = count_x * count_y
    pairs = devices // 2
    rescale = math.sqrt(float(block_x * count_x) * float(block_y * count_y)) / rank
    vmem = pl.BlockSpec(memory_space=pltpu.VMEM)
    hbm = pl.BlockSpec(memory_space=pltpu.HBM)
    f32 = jnp.float32

    def array(shape, dtype=f32):
        return jax.ShapeDtypeStruct(shape, dtype)

    def call(
        kernel, name, outs, scratch, operands, space=vmem, out_spaces=None, limit=32 * 1024 * 1024, cost=10**9
    ):
        return pl.pallas_call(
            kernel,
            out_shape=tuple(outs),
            in_specs=[space] * len(operands),
            out_specs=out_spaces or (vmem,) * len(outs),
            scratch_shapes=scratch,
            compiler_params=pltpu.CompilerParams(vmem_limit_bytes=limit),
            cost_estimate=pl.CostEstimate(flops=cost, bytes_accessed=0, transcendentals=0),
            name=name,
        )(*operands)

    def swap(blocks):
        blocks = blocks.reshape((devices,) + blocks.shape[2:])
        return lax.all_to_all(blocks, ("gx", "gy"), 0, 0, tiled=True)

    def pass_on(blocks, axis):
        count = len(blocks)
        moved = [
            lax.ppermute(block, axis, [(i, (i + k) % count) for i in range(count)])
            for k, block in enumerate(blocks)
            if k
        ]
        return [blocks[0]] + moved

    flat = (n_f, block_x * block_y, n_z)
    (packed,) = call(
        pack_kernel,
        "pack",
        [array((pairs, 2, 4 * n_f + 1, 2, n_z))],
        [
            pltpu.VMEM(flat, f32),
            pltpu.VMEM(factor_x.shape, f32),
            pltpu.VMEM(factor_y.shape, f32),
            pltpu.SemaphoreType.DMA((n_f + 2,)),
        ],
        tuple(
            pltpu.with_memory_space_constraint(v, pltpu.HBM)
            for v in (fields.reshape(flat), factor_x, factor_y)
        ),
        space=hbm,
    )
    planes = swap(packed).reshape(count_x, count_y, 4 * n_f + 1, 2, n_z)
    extended = pltpu.VMEM((count_y, n_f, SUBLANES + 6, SUBLANES, LANES), f32)
    rows = SUBLANES * SUBLANES + HALF * SUBLANES
    plane = count_y * SUBLANES * SUBLANES
    sent, spread, *columns = call(
        functools.partial(main_kernel, n_f, count_x, count_y, rank, rescale),
        "sections",
        [
            array((count_x, count_y, 2 * n_f, HALF, n_z)),
            array((2, n_f * LANES, LANES), jnp.bfloat16),
        ]
        + [array((rows, LANES))] * count_y,
        [extended] * 3
        + [
            pltpu.VMEM((n_f, count_y, SUBLANES, SUBLANES, LANES), f32),
            pltpu.VMEM((count_y, rows, LANES), f32),
            pltpu.VMEM((count_x, count_y, 2 * n_f, HALF, n_z), f32),
            pltpu.SemaphoreType.DMA,
            pltpu.VMEM((2, LANES, plane), jnp.bfloat16),
            pltpu.VMEM((2, plane, plane), jnp.bfloat16),
        ],
        (planes,),
        out_spaces=(hbm,) + (vmem,) * (1 + count_y),
    )
    columns = pass_on(columns, "gy")
    sent = swap(sent).reshape(pairs, 2, 2 * n_f, HALF, n_z)
    rows = (n_f * count_y + n_f // 2) * SUBLANES
    blocks = call(
        functools.partial(expand_kernel, n_f, count_x, count_y),
        "expand",
        [array((rows, LANES))] * count_x,
        [
            pltpu.VMEM((count_y,) + columns[0].shape, f32),
            pltpu.VMEM((count_x, rows, LANES), f32),
        ],
        (spread, *columns),
        cost=20000000000,
    )
    blocks = pass_on(blocks, "gx")
    (advanced,) = call(
        functools.partial(advanced_kernel, block_x, block_y),
        "advanced",
        [array(flat)],
        [pltpu.VMEM(flat, f32), pltpu.SemaphoreType.DMA((n_f,))],
        (sent,),
        out_spaces=(hbm,),
    )
    rebuilt, core = call(
        functools.partial(rebuilt_kernel, block_x, block_y, count_x, count_y),
        "rebuilt",
        [array(flat), array((n_f, rank // count_x, rank // count_y, n_z))],
        [
            pltpu.VMEM((count_x, rows, LANES), f32),
            pltpu.VMEM(flat, f32),
            pltpu.VMEM((n_f, rank // count_x, rank // count_y, n_z), f32),
            pltpu.SemaphoreType.DMA((n_f + 1,)),
        ],
        tuple(blocks),
        out_spaces=(hbm, hbm),
        cost=1000000000,
    )
    return advanced.reshape(fields.shape), core, rebuilt.reshape(fields.shape)


def extended(block, sides, width):
    for axis, dim in sides:
        count = lax.axis_size(axis)
        forward = [(i, i + 1) for i in range(count - 1)]
        forward.append((count - 1, 0))
        backward = [(target, source) for source, target in forward]
        low = lax.ppermute(
            lax.slice_in_dim(block, block.shape[dim] - width, None, axis=dim), axis, forward
        )
        high = lax.ppermute(lax.slice_in_dim(block, 0, width, axis=dim), axis, backward)
        block = jnp.concatenate([low, block, high], axis=dim)
    return block


def inner_part(array, margin):
    return array[:, margin : array.shape[1] - margin, margin : array.shape[2] - margin]


def tendency(padded):
    n_x = padded.shape[1]
    n_y = padded.shape[2]
    pressure = 0.5 * padded[3]
    flux_x = padded[0][None] * padded
    flux_x = flux_x.at[0].add(pressure)
    flux_y = padded[1][None] * padded
    flux_y = flux_y.at[1].add(pressure)

    def along_x(shift):
        return (
            flux_x[:, 3 + shift : n_x - 3 + shift, 3 : n_y - 3]
            - flux_x[:, 3 - shift : n_x - 3 - shift, 3 : n_y - 3]
        )

    def along_y(shift):
        return (
            flux_y[:, 3 : n_x - 3, 3 + shift : n_y - 3 + shift]
            - flux_y[:, 3 : n_x - 3, 3 - shift : n_y - 3 - shift]
        )

    deriv_x = (45.0 * along_x(1) - 9.0 * along_x(2) + along_x(3)) / 60.0
    deriv_y = (45.0 * along_y(1) - 9.0 * along_y(2) + along_y(3)) / 60.0
    center = inner_part(padded, 3)
    react = REACT_RATE * center[2] * (1.0 + jnp.tanh(center[3]))
    zeros = jnp.zeros_like(react)
    source = jnp.stack([zeros, zeros, -react, HEAT_RELEASE * react])
    return source - deriv_x - deriv_y


def section_tendency(state):
    padded = extended(state, (("gx", 1), ("gy", 2)), 3)
    return tendency(padded)


def per_device(fields, factor_x, factor_y):
    high = lax.Precision.HIGHEST
    section_one = fields + TIME_STEP * section_tendency(fields)
    section_two = 0.75 * fields + 0.25 * (section_one + TIME_STEP * section_tendency(section_one))
    advanced = 1.0 / 3.0 * fields + 2.0 / 3.0 * (
        section_two + TIME_STEP * section_tendency(section_two)
    )
    rank_full = factor_x.shape[1]
    count_x = lax.axis_size("gx")
    count_y = lax.axis_size("gy")
    partial_x = jnp.einsum("fxyz,xa->fayz", advanced, factor_x, precision=high)
    partial_value = lax.psum_scatter(partial_x, "gx", scatter_dimension=1, tiled=True)
    local_core = jnp.einsum("fayz,yb->fabz", partial_value, factor_y, precision=high)
    core_tensor = lax.psum_scatter(local_core, "gy", scatter_dimension=2, tiled=True)
    weights = factor_y
    columns = jnp.einsum(
        "fabz,yb->fayz",
        lax.all_gather(core_tensor, "gy", axis=2, tiled=True),
        weights,
        precision=high,
    )
    weights = factor_x
    expanded = jnp.einsum(
        "fayz,xa->fxyz", lax.all_gather(columns, "gx", axis=1, tiled=True), weights, precision=high
    )
    total_x = factor_x.shape[0] * count_x
    total_y = factor_y.shape[0] * count_y
    rescale = math.sqrt(float(total_x) * float(total_y)) / rank_full
    rebuilt = rescale * expanded
    return (advanced, core_tensor, rebuilt)


def solution(mesh):
    placed = (P(None, "gx", "gy", None), P("gx", None), P("gy", None))
    out = P(None, "gx", "gy", None)

    def whole(fields, factor_x, factor_y):
        plan = z_plan if fits(mesh, fields, factor_x, factor_y) else per_device
        return jax.shard_map(
            plan, mesh=mesh, in_specs=placed, out_specs=(out, out, out), check_vma=False
        )(fields, factor_x, factor_y)

    return whole
```

```python
import functools
import math

import jax
import jax.numpy as jnp
from jax import lax
from jax.experimental import pallas as pl
from jax.experimental.pallas import tpu as pltpu
from jax.sharding import PartitionSpec as P

TIME_STEP = 0.2
REACT_RATE = 0.5
HEAT_RELEASE = 1.0
SUBLANES = 8
LANES = 128
HALF = SUBLANES // 2


def fits(mesh, fields, factor_x, factor_y):
    n_f, n_x, n_y, n_z = fields.shape
    count_x, count_y = mesh.shape["gx"], mesh.shape["gy"]
    devices = count_x * count_y
    rank = factor_x.shape[1]
    if n_x % count_x or n_y % count_y or n_z % devices:
        return False
    block_x, block_y, block_z = n_x // count_x, n_y // count_y, n_z // devices
    return (
        n_x == LANES
        and n_z == LANES
        and n_f == HALF
        and block_z == HALF
        and block_x == 2 * SUBLANES
        and block_y == 2 * SUBLANES
        and count_x == SUBLANES
        and count_y == HALF
        and rank == count_y * SUBLANES
        and factor_y.shape[1] == rank
        and n_f * rank == LANES
    )


def exchange(blocks, stride):
    count = len(blocks)
    period = stride * count
    group = lax.broadcasted_iota(jnp.int32, (SUBLANES, LANES), 1) // stride % count
    if period == LANES:
        blocks = [pltpu.roll(b, i * stride, 1) if i else b for i, b in enumerate(blocks)]
        step = 1
        while step < count:
            taken = (group & step) != 0
            blocks = [
                jnp.where(taken, blocks[(i + step) % count], blocks[i]) for i in range(count)
            ]
            step *= 2
        blocks = [blocks[-j % count] for j in range(count)]
        return [pltpu.roll(b, LANES - j * stride, 1) if j else b for j, b in enumerate(blocks)]
    blocks = list(blocks)
    step = 1
    while step < count:
        upper = (group & step) != 0
        for i in range(count):
            if i & step:
                continue
            low, high = blocks[i], blocks[i + step]
            blocks[i] = jnp.where(upper, pltpu.roll(high, stride * step, 1), low)
            blocks[i + step] = jnp.where(upper, high, pltpu.roll(low, LANES - stride * step, 1))
        step *= 2
    return blocks


def pack_kernel(fields_hbm, factor_x_hbm, factor_y_hbm, out_ref, fields_ref, x_ref, y_ref, sems):
    n_f, rows, _ = fields_ref.shape
    block_x = x_ref.shape[0]
    block_y = rows // block_x
    tiles = LANES // SUBLANES
    copies = [
        pltpu.make_async_copy(fields_hbm.at[f], fields_ref.at[f], sems.at[f]) for f in range(n_f)
    ]
    copies.append(pltpu.make_async_copy(factor_x_hbm, x_ref, sems.at[n_f]))
    copies.append(pltpu.make_async_copy(factor_y_hbm, y_ref, sems.at[n_f + 1]))
    for copy in copies:
        copy.start()
    for f in range(n_f):
        copies[f].wait()
        for octet in range(2):
            matrix = jnp.concatenate(
                [
                    fields_ref[f, pl.ds(octet * SUBLANES + y, block_x, stride=block_y), :]
                    for y in range(SUBLANES)
                ],
                axis=0,
            )
            turned = matrix.T.reshape(tiles, SUBLANES, LANES)
            for part in range(2):
                at = 2 * (2 * f + octet) + part
                out_ref[:, 0, at] = turned[:, 2 * part : 2 * part + 2]
                out_ref[:, 1, at] = turned[:, HALF + 2 * part : HALF + 2 * part + 2]
    copies[n_f].wait()
    copies[n_f + 1].wait()
    own_x = x_ref[pl.ds(lax.axis_index("gy") * HALF, HALF), :]
    own_y = y_ref[pl.ds(lax.axis_index("gx") * 2, 2), :]
    row_x = jnp.concatenate([own_x[j : j + 1] for j in range(HALF)], axis=1)
    row_y = jnp.concatenate([own_y[j % 2 : j % 2 + 1] for j in range(HALF)], axis=1)
    factors = jnp.concatenate([row_x, row_y], axis=0)
    out_ref[:, :, 4 * n_f] = jnp.broadcast_to(factors[None, None], (tiles, 2, 2, LANES))


def split(value):
    high = value.astype(jnp.bfloat16)
    low = (value - high.astype(jnp.float32)).astype(jnp.bfloat16)
    return high, low


def mul(a, b, dims=((1,), (0,))):
    return lax.dot_general(a, b, (dims, ((), ())), preferred_element_type=jnp.float32)


def mul_split(a, b, dims=((1,), (0,))):
    return mul(a[0], b[0], dims) + (mul(a[0], b[1], dims) + mul(a[1], b[0], dims))


def main_kernel(
    n_f, count_x, count_y, rank, rescale, in_ref, sent_hbm, spread_ref, *refs
):
    column_refs = refs[:count_y]
    ext_a, ext_b, ext_c, adv, staged, sent_ref, sent_sem = refs[count_y : count_y + 7]
    to_core_ref, project_ref = refs[count_y + 7 :]
    margin = 3
    inner = pl.ds(margin, SUBLANES)
    lower = lax.broadcasted_iota(jnp.int32, (margin, SUBLANES, LANES), 1) < HALF

    def each(body):
        def step(s, carry):
            body(s)
            return carry

        lax.fori_loop(0, count_y, step, 0, unroll=True)

    def fill_margins(ext):
        def one(s):
            before = lax.rem(s + count_y - 1, count_y)
            after = lax.rem(s + 1, count_y)
            for f in range(n_f):
                old = ext[before, f, pl.ds(SUBLANES, margin)]
                own = ext[s, f, pl.ds(SUBLANES, margin)]
                ext[s, f, 0:margin] = pltpu.roll(jnp.where(lower, own, old), HALF, 1)
                own = ext[s, f, pl.ds(margin, margin)]
                new = ext[after, f, pl.ds(margin, margin)]
                ext[s, f, pl.ds(SUBLANES + margin, margin)] = pltpu.roll(
                    jnp.where(lower, new, own), HALF, 1
                )

        each(one)

    row = lax.broadcasted_iota(jnp.int32, (LANES, LANES), 0)
    col = lax.broadcasted_iota(jnp.int32, (LANES, LANES), 1)
    ahead = (row - col) & (LANES - 1)
    taps = jnp.zeros((LANES, LANES), jnp.float32)
    for shift, weight in ((1, 45.0), (2, -9.0), (3, 1.0)):
        taps = jnp.where(ahead == shift, weight, taps)
        taps = jnp.where(ahead == LANES - shift, -weight, taps)
    taps = taps.astype(jnp.bfloat16)
    taps = jnp.concatenate([taps, taps], axis=0)

    def section(ext, step, store):
        def one(s):
            padded = [ext[s, f] for f in range(n_f)]
            center = [p[margin : margin + SUBLANES] for p in padded]
            flux_x = [center[0] * c for c in center]
            flux_x[0] = flux_x[0] + 0.5 * center[3]
            flat = jnp.concatenate(flux_x, axis=0).reshape(n_f * SUBLANES * SUBLANES, LANES)
            along_x = mul(jnp.concatenate(split(flat), axis=1), taps)
            along_x = along_x.reshape(n_f, SUBLANES, SUBLANES, LANES)
            react = (step * REACT_RATE) * center[2] * (1.0 + jnp.tanh(center[3]))
            for f in range(n_f):
                flux_y = padded[1] * padded[f]
                if f == 1:
                    flux_y = flux_y + 0.5 * padded[3]

                def along_y(k):
                    after = flux_y[margin + k : margin + k + SUBLANES]
                    return after - flux_y[margin - k : margin - k + SUBLANES]

                change = (
                    (-45.0 * step / 60.0) * along_y(1)
                    + (9.0 * step / 60.0) * along_y(2)
                    + (-step / 60.0) * (along_y(3) + along_x[f])
                )
                if f == 2:
                    change = change - react
                if f == 3:
                    change = change + HEAT_RELEASE * react
                store(s, f, center[f], change)

        each(one)

    def arrive(s):
        for f in range(n_f):
            got = [
                in_ref[i, s, 4 * f : 4 * f + 4].reshape(SUBLANES, LANES) for i in range(count_x)
            ]
            for y, block in enumerate(exchange(got, LANES // SUBLANES)):
                ext_a[s, f, margin + y] = block

    def first(s, f, center, change):
        ext_b[s, f, inner] = center + change

    def second(s, f, center, change):
        ext_c[s, f, inner] = 0.75 * ext_a[s, f, inner] + (0.25 * center + change)

    def third(s, f, center, change):
        done = (1.0 / 3.0) * ext_a[s, f, inner] + ((2.0 / 3.0) * center + change)
        adv[f, s] = done
        parts = exchange([done[y] for y in range(SUBLANES)], LANES // SUBLANES)
        for i, part in enumerate(parts):
            sent_ref[i, s, 2 * f : 2 * f + 2] = part.reshape(2, HALF, LANES)

    plane = count_y * SUBLANES * SUBLANES
    count = count_x * count_y
    held = in_ref[:, :, 4 * n_f].reshape(2 * count, LANES)
    held_at = lax.broadcasted_iota(jnp.int32, (LANES, 2 * count), 1)
    source = lax.broadcasted_iota(jnp.int32, (LANES, 2 * count), 0) // HALF
    rows_of = (held_at == 2 * source).astype(jnp.bfloat16)
    spread_x = [jnp.where(row % HALF == col // rank, mul(rows_of, part), 0.0) for part in split(held)]
    picks = (row % rank == col // n_f).astype(jnp.bfloat16)
    spread_x = [mul(part.astype(jnp.bfloat16), picks) for part in spread_x]
    weights_x = [
        jnp.concatenate(
            [jnp.where(col % n_f == f, part, 0.0).astype(jnp.bfloat16) for f in range(n_f)], axis=0
        )
        for part in spread_x
    ]
    r = lax.broadcasted_iota(jnp.int32, (plane, LANES), 0)
    c = lax.broadcasted_iota(jnp.int32, (plane, LANES), 1)
    from_s, from_y = r // (SUBLANES * SUBLANES), (r // HALF) % 2 * SUBLANES + (r // SUBLANES) % SUBLANES
    held_at = lax.broadcasted_iota(jnp.int32, (plane, 2 * count), 1)
    source = (from_y // 2 * count_y + from_s)[:, : 2 * count]
    rows_of = (held_at == 2 * source + 1).astype(jnp.bfloat16)
    spread_y = [jnp.where(from_y % 2 == c // rank % 2, mul(rows_of, part), 0.0) for part in split(held)]
    spread_y = [part + pltpu.roll(part, rank, 1) for part in spread_y]
    same_z = r % HALF == c // rank
    weights_y = [jnp.where(same_z, part, 0.0).astype(jnp.bfloat16) for part in spread_y]
    for part in range(2):
        spread_ref[part] = weights_x[part]
        to_core_ref[part] = weights_y[part].astype(jnp.float32).T.astype(jnp.bfloat16)
    projector = split(rescale * mul_split(weights_y, weights_y, ((1,), (1,))))
    for part in range(2):
        project_ref[part] = projector[part]

    each(arrive)
    fill_margins(ext_a)
    section(ext_a, TIME_STEP, first)
    fill_margins(ext_b)
    section(ext_b, 0.25 * TIME_STEP, second)
    fill_margins(ext_c)
    section(ext_c, 2.0 / 3.0 * TIME_STEP, third)
    sent = pltpu.make_async_copy(sent_ref, sent_hbm, sent_sem)
    sent.start()

    @pl.when(lax.axis_index("gy") >= 0)
    def tucker():
        def by_x(value):
            return jnp.concatenate([value[f].reshape(plane, LANES) for f in range(n_f)], axis=1)

        weights_x = [spread_ref[part] for part in range(2)]
        partial = split(mul_split(split(by_x(adv)), weights_x))
        core = mul_split([to_core_ref[part] for part in range(2)], partial)
        columns = mul_split([project_ref[part] for part in range(2)], partial)

        block = plane // count_y
        for s in range(count_y):
            staged[s, 0:block] = columns[s * block : (s + 1) * block]
            for z in range(HALF):
                at = z * rank + s * SUBLANES
                staged[s, block + z * SUBLANES : block + (z + 1) * SUBLANES] = core[at : at + SUBLANES]
        own = lax.axis_index("gy")
        for k, ref in enumerate(column_refs):
            ref[...] = staged[lax.rem(own + k, count_y)]

    sent.wait()


def expand_kernel(n_f, count_x, count_y, spread_ref, *refs):
    in_refs, out_refs = refs[:count_y], refs[count_y : count_y + count_x]
    held, staged = refs[count_y + count_x :]
    own = lax.axis_index("gy")
    for k, ref in enumerate(in_refs):
        held[lax.rem(own + count_y - k, count_y)] = ref[...]
    block = SUBLANES * SUBLANES
    plane = count_y * block
    columns = split(jnp.concatenate([held[s, 0:block] for s in range(count_y)], axis=0))
    for f in range(n_f):
        weights = [spread_ref[part, f * LANES : (f + 1) * LANES] for part in range(2)]
        rebuilt = mul_split(columns, weights, ((1,), (1,)))
        rebuilt = rebuilt.reshape(count_y, SUBLANES, SUBLANES, LANES)
        for s in range(count_y):
            parts = exchange([rebuilt[s, y] for y in range(SUBLANES)], LANES // SUBLANES)
            for i, part in enumerate(parts):
                at = (f * count_y + s) * SUBLANES
                staged[i, at : at + SUBLANES] = part
    by_f = [
        exchange([held[s, block + z * SUBLANES : block + (z + 1) * SUBLANES] for z in range(HALF)], 1)
        for s in range(count_y)
    ]
    left = lax.broadcasted_iota(jnp.int32, (SUBLANES, LANES), 1) < LANES // 2
    by_i = []
    for f in range(n_f):
        tiles = exchange([by_f[s][f] for s in range(count_y)], HALF)
        by_i.append(exchange(tiles, LANES // SUBLANES))
    for i in range(count_x):
        for pair in range(n_f // 2):
            low, high = by_i[2 * pair][i % HALF], by_i[2 * pair + 1][i % HALF]
            if i < HALF:
                tile = jnp.where(left, low, pltpu.roll(high, LANES // 2, 1))
            else:
                tile = jnp.where(left, pltpu.roll(low, LANES // 2, 1), high)
            at = (n_f * count_y + pair) * SUBLANES
            staged[i, at : at + SUBLANES] = tile
    own = lax.axis_index("gx")
    for k, ref in enumerate(out_refs):
        ref[...] = staged[lax.rem(own + k, count_x)]


def scatter_rows(turned, octet, block_x, block_y, target, f):
    for y in range(SUBLANES):
        rows = pl.ds(octet * SUBLANES + y, block_x, stride=block_y)
        target[f, rows, :] = turned[y * block_x : (y + 1) * block_x]


def results_kernel(
    block_x, block_y, in_ref, rebuilt_ref, core_ref, advanced_hbm, rebuilt_hbm, core_hbm, advanced_ref, sems
):
    n_f = advanced_ref.shape[0]
    leaving = [
        pltpu.make_async_copy(advanced_ref.at[f], advanced_hbm.at[f], sems.at[f]) for f in range(n_f)
    ]
    leaving.append(pltpu.make_async_copy(rebuilt_ref, rebuilt_hbm, sems.at[n_f]))
    leaving.append(pltpu.make_async_copy(core_ref, core_hbm, sems.at[n_f + 1]))
    leaving[n_f].start()
    leaving[n_f + 1].start()
    for f in range(n_f):
        for octet in range(2):
            place = 2 * f + octet
            matrix = jnp.concatenate([in_ref[:, 0, place], in_ref[:, 1, place]], axis=1)
            turned = matrix.reshape(LANES, LANES).T
            scatter_rows(turned, octet, block_x, block_y, advanced_ref, f)
        leaving[f].start()
    for copy in leaving:
        copy.wait()


def rebuilt_kernel(block_x, block_y, count_x, count_y, *refs):
    in_refs, (rebuilt_ref, core_ref, held) = refs[:count_x], refs[count_x:]
    n_f = rebuilt_ref.shape[0]
    own = lax.axis_index("gx")
    for k, ref in enumerate(in_refs):
        held[lax.rem(own + count_x - k, count_x)] = ref[...]
    a_count = core_ref.shape[1]
    for pair in range(n_f // 2):
        at = (n_f * count_y + pair) * SUBLANES
        tiles = exchange([held[i, at : at + SUBLANES] for i in range(count_x)], LANES // SUBLANES)
        for place, tile in enumerate(tiles):
            core_ref[2 * pair + place // a_count, place % a_count] = tile
    pairs = count_y // 2
    lower = lax.broadcasted_iota(jnp.int32, (count_x, pairs, SUBLANES, LANES), 2) < HALF
    for f in range(n_f):
        at = pl.ds(f * count_y * SUBLANES, count_y * SUBLANES)
        tiles = held[:, at, :].reshape(count_x, pairs, 2, SUBLANES, LANES)
        even, odd = tiles[:, :, 0], tiles[:, :, 1]
        first = jnp.where(lower, even, pltpu.roll(odd, HALF, 2))
        second = jnp.where(lower, pltpu.roll(even, HALF, 2), odd)
        for octet, part in enumerate((first, second)):
            turned = part.reshape(LANES, LANES).T
            scatter_rows(turned, octet, block_x, block_y, rebuilt_ref, f)


def z_plan(fields, factor_x, factor_y):
    n_f, block_x, block_y, n_z = fields.shape
    rank = factor_x.shape[1]
    count_x = lax.axis_size("gx")
    count_y = lax.axis_size("gy")
    devices = count_x * count_y
    pairs = devices // 2
    rescale = math.sqrt(float(block_x * count_x) * float(block_y * count_y)) / rank
    vmem = pl.BlockSpec(memory_space=pltpu.VMEM)
    hbm = pl.BlockSpec(memory_space=pltpu.HBM)
    f32 = jnp.float32

    def array(shape, dtype=f32):
        return jax.ShapeDtypeStruct(shape, dtype)

    def call(
        kernel, name, outs, scratch, operands, space=vmem, out_spaces=None, limit=32 * 1024 * 1024, cost=10**9
    ):
        return pl.pallas_call(
            kernel,
            out_shape=tuple(outs),
            in_specs=[space] * len(operands),
            out_specs=out_spaces or (vmem,) * len(outs),
            scratch_shapes=scratch,
            compiler_params=pltpu.CompilerParams(vmem_limit_bytes=limit),
            cost_estimate=pl.CostEstimate(flops=cost, bytes_accessed=0, transcendentals=0),
            name=name,
        )(*operands)

    def swap(blocks):
        blocks = blocks.reshape((devices,) + blocks.shape[2:])
        return lax.all_to_all(blocks, ("gx", "gy"), 0, 0, tiled=True)

    def pass_on(blocks, axis):
        count = len(blocks)
        moved = [
            lax.ppermute(block, axis, [(i, (i + k) % count) for i in range(count)])
            for k, block in enumerate(blocks)
            if k
        ]
        return [blocks[0]] + moved

    flat = (n_f, block_x * block_y, n_z)
    (packed,) = call(
        pack_kernel,
        "pack",
        [array((pairs, 2, 4 * n_f + 1, 2, n_z))],
        [
            pltpu.VMEM(flat, f32),
            pltpu.VMEM(factor_x.shape, f32),
            pltpu.VMEM(factor_y.shape, f32),
            pltpu.SemaphoreType.DMA((n_f + 2,)),
        ],
        tuple(
            pltpu.with_memory_space_constraint(v, pltpu.HBM)
            for v in (fields.reshape(flat), factor_x, factor_y)
        ),
        space=hbm,
    )
    planes = swap(packed).reshape(count_x, count_y, 4 * n_f + 1, 2, n_z)
    extended = pltpu.VMEM((count_y, n_f, SUBLANES + 6, SUBLANES, LANES), f32)
    rows = SUBLANES * SUBLANES + HALF * SUBLANES
    plane = count_y * SUBLANES * SUBLANES
    sent, spread, *columns = call(
        functools.partial(main_kernel, n_f, count_x, count_y, rank, rescale),
        "sections",
        [
            array((count_x, count_y, 2 * n_f, HALF, n_z)),
            array((2, n_f * LANES, LANES), jnp.bfloat16),
        ]
        + [array((rows, LANES))] * count_y,
        [extended] * 3
        + [
            pltpu.VMEM((n_f, count_y, SUBLANES, SUBLANES, LANES), f32),
            pltpu.VMEM((count_y, rows, LANES), f32),
            pltpu.VMEM((count_x, count_y, 2 * n_f, HALF, n_z), f32),
            pltpu.SemaphoreType.DMA,
            pltpu.VMEM((2, LANES, plane), jnp.bfloat16),
            pltpu.VMEM((2, plane, plane), jnp.bfloat16),
        ],
        (planes,),
        out_spaces=(hbm,) + (vmem,) * (1 + count_y),
    )
    columns = pass_on(columns, "gy")
    sent = swap(sent).reshape(pairs, 2, 2 * n_f, HALF, n_z)
    rows = (n_f * count_y + n_f // 2) * SUBLANES
    blocks = call(
        functools.partial(expand_kernel, n_f, count_x, count_y),
        "expand",
        [array((rows, LANES))] * count_x,
        [
            pltpu.VMEM((count_y,) + columns[0].shape, f32),
            pltpu.VMEM((count_x, rows, LANES), f32),
        ],
        (spread, *columns),
        cost=20000000000,
    )
    blocks = pass_on(blocks, "gx")
    core_shape = (n_f, rank // count_x, rank // count_y, n_z)
    rebuilt, core = call(
        functools.partial(rebuilt_kernel, block_x, block_y, count_x, count_y),
        "rebuilt",
        [array(flat), array(core_shape)],
        [pltpu.VMEM((count_x, rows, LANES), f32)],
        tuple(blocks),
    )
    advanced, rebuilt, core = call(
        functools.partial(results_kernel, block_x, block_y),
        "results",
        [array(flat), array(flat), array(core_shape)],
        [pltpu.VMEM(flat, f32), pltpu.SemaphoreType.DMA((n_f + 2,))],
        (sent, rebuilt, core),
        out_spaces=(hbm,) * 3,
    )
    return advanced.reshape(fields.shape), core, rebuilt.reshape(fields.shape)


def extended(block, sides, width):
    for axis, dim in sides:
        count = lax.axis_size(axis)
        forward = [(i, i + 1) for i in range(count - 1)]
        forward.append((count - 1, 0))
        backward = [(target, source) for source, target in forward]
        low = lax.ppermute(
            lax.slice_in_dim(block, block.shape[dim] - width, None, axis=dim), axis, forward
        )
        high = lax.ppermute(lax.slice_in_dim(block, 0, width, axis=dim), axis, backward)
        block = jnp.concatenate([low, block, high], axis=dim)
    return block


def inner_part(array, margin):
    return array[:, margin : array.shape[1] - margin, margin : array.shape[2] - margin]


def tendency(padded):
    n_x = padded.shape[1]
    n_y = padded.shape[2]
    pressure = 0.5 * padded[3]
    flux_x = padded[0][None] * padded
    flux_x = flux_x.at[0].add(pressure)
    flux_y = padded[1][None] * padded
    flux_y = flux_y.at[1].add(pressure)

    def along_x(shift):
        return (
            flux_x[:, 3 + shift : n_x - 3 + shift, 3 : n_y - 3]
            - flux_x[:, 3 - shift : n_x - 3 - shift, 3 : n_y - 3]
        )

    def along_y(shift):
        return (
            flux_y[:, 3 : n_x - 3, 3 + shift : n_y - 3 + shift]
            - flux_y[:, 3 : n_x - 3, 3 - shift : n_y - 3 - shift]
        )

    deriv_x = (45.0 * along_x(1) - 9.0 * along_x(2) + along_x(3)) / 60.0
    deriv_y = (45.0 * along_y(1) - 9.0 * along_y(2) + along_y(3)) / 60.0
    center = inner_part(padded, 3)
    react = REACT_RATE * center[2] * (1.0 + jnp.tanh(center[3]))
    zeros = jnp.zeros_like(react)
    source = jnp.stack([zeros, zeros, -react, HEAT_RELEASE * react])
    return source - deriv_x - deriv_y


def section_tendency(state):
    padded = extended(state, (("gx", 1), ("gy", 2)), 3)
    return tendency(padded)


def per_device(fields, factor_x, factor_y):
    high = lax.Precision.HIGHEST
    section_one = fields + TIME_STEP * section_tendency(fields)
    section_two = 0.75 * fields + 0.25 * (section_one + TIME_STEP * section_tendency(section_one))
    advanced = 1.0 / 3.0 * fields + 2.0 / 3.0 * (
        section_two + TIME_STEP * section_tendency(section_two)
    )
    rank_full = factor_x.shape[1]
    count_x = lax.axis_size("gx")
    count_y = lax.axis_size("gy")
    partial_x = jnp.einsum("fxyz,xa->fayz", advanced, factor_x, precision=high)
    partial_value = lax.psum_scatter(partial_x, "gx", scatter_dimension=1, tiled=True)
    local_core = jnp.einsum("fayz,yb->fabz", partial_value, factor_y, precision=high)
    core_tensor = lax.psum_scatter(local_core, "gy", scatter_dimension=2, tiled=True)
    weights = factor_y
    columns = jnp.einsum(
        "fabz,yb->fayz",
        lax.all_gather(core_tensor, "gy", axis=2, tiled=True),
        weights,
        precision=high,
    )
    weights = factor_x
    expanded = jnp.einsum(
        "fayz,xa->fxyz", lax.all_gather(columns, "gx", axis=1, tiled=True), weights, precision=high
    )
    total_x = factor_x.shape[0] * count_x
    total_y = factor_y.shape[0] * count_y
    rescale = math.sqrt(float(total_x) * float(total_y)) / rank_full
    rebuilt = rescale * expanded
    return (advanced, core_tensor, rebuilt)


def solution(mesh):
    placed = (P(None, "gx", "gy", None), P("gx", None), P("gy", None))
    out = P(None, "gx", "gy", None)

    def whole(fields, factor_x, factor_y):
        plan = z_plan if fits(mesh, fields, factor_x, factor_y) else per_device
        return jax.shard_map(
            plan, mesh=mesh, in_specs=placed, out_specs=(out, out, out), check_vma=False
        )(fields, factor_x, factor_y)

    return whole
```

```python
import functools
import math

import jax
import jax.numpy as jnp
from jax import lax
from jax.experimental import pallas as pl
from jax.experimental.pallas import tpu as pltpu
from jax.sharding import PartitionSpec as P

TIME_STEP = 0.2
REACT_RATE = 0.5
HEAT_RELEASE = 1.0
SUBLANES = 8
LANES = 128
HALF = SUBLANES // 2


def fits(mesh, fields, factor_x, factor_y):
    n_f, n_x, n_y, n_z = fields.shape
    count_x, count_y = mesh.shape["gx"], mesh.shape["gy"]
    devices = count_x * count_y
    rank = factor_x.shape[1]
    if n_x % count_x or n_y % count_y or n_z % devices:
        return False
    block_x, block_y, block_z = n_x // count_x, n_y // count_y, n_z // devices
    return (
        n_x == LANES
        and n_z == LANES
        and n_f == HALF
        and block_z == HALF
        and block_x == 2 * SUBLANES
        and block_y == 2 * SUBLANES
        and count_x == SUBLANES
        and count_y == HALF
        and rank == count_y * SUBLANES
        and factor_y.shape[1] == rank
        and n_f * rank == LANES
    )


def digit(index, size, count):
    return lax.shift_right_logical(index, size.bit_length() - 1) & (count - 1)


def exchange(blocks, stride):
    count = len(blocks)
    period = stride * count
    group = digit(lax.broadcasted_iota(jnp.int32, (SUBLANES, LANES), 1), stride, count)
    if period == LANES:
        blocks = [pltpu.roll(b, i * stride, 1) if i else b for i, b in enumerate(blocks)]
        step = 1
        while step < count:
            taken = (group & step) != 0
            blocks = [
                jnp.where(taken, blocks[(i + step) % count], blocks[i]) for i in range(count)
            ]
            step *= 2
        blocks = [blocks[-j % count] for j in range(count)]
        return [pltpu.roll(b, LANES - j * stride, 1) if j else b for j, b in enumerate(blocks)]
    blocks = list(blocks)
    step = 1
    while step < count:
        upper = (group & step) != 0
        for i in range(count):
            if i & step:
                continue
            low, high = blocks[i], blocks[i + step]
            blocks[i] = jnp.where(upper, pltpu.roll(high, stride * step, 1), low)
            blocks[i + step] = jnp.where(upper, high, pltpu.roll(low, LANES - stride * step, 1))
        step *= 2
    return blocks


def pack_kernel(fields_hbm, factor_x_hbm, factor_y_hbm, out_ref, fields_ref, x_ref, y_ref, sems):
    n_f, rows, _ = fields_ref.shape
    block_x = x_ref.shape[0]
    block_y = rows // block_x
    tiles = LANES // SUBLANES
    copies = [
        pltpu.make_async_copy(fields_hbm.at[f], fields_ref.at[f], sems.at[f]) for f in range(n_f)
    ]
    copies.append(pltpu.make_async_copy(factor_x_hbm, x_ref, sems.at[n_f]))
    copies.append(pltpu.make_async_copy(factor_y_hbm, y_ref, sems.at[n_f + 1]))
    for copy in copies:
        copy.start()
    for f in range(n_f):
        if f % 2 == 0:
            copies[f].wait()
            copies[f + 1].wait()
        for octet in range(2):
            matrix = jnp.concatenate(
                [
                    fields_ref[f, pl.ds(octet * SUBLANES + y, block_x, stride=block_y), :]
                    for y in range(SUBLANES)
                ],
                axis=0,
            )
            turned = matrix.T.reshape(tiles, SUBLANES, LANES)
            for part in range(2):
                at = 2 * (2 * f + octet) + part
                out_ref[:, 0, at] = turned[:, 2 * part : 2 * part + 2]
                out_ref[:, 1, at] = turned[:, HALF + 2 * part : HALF + 2 * part + 2]
    copies[n_f].wait()
    copies[n_f + 1].wait()
    own_x = x_ref[pl.ds(lax.axis_index("gy") * HALF, HALF), :]
    own_y = y_ref[pl.ds(lax.axis_index("gx") * 2, 2), :]
    row_x = jnp.concatenate([own_x[j : j + 1] for j in range(HALF)], axis=1)
    row_y = jnp.concatenate([own_y[j % 2 : j % 2 + 1] for j in range(HALF)], axis=1)
    factors = jnp.concatenate([row_x, row_y], axis=0)
    out_ref[:, :, 4 * n_f] = jnp.broadcast_to(factors[None, None], (tiles, 2, 2, LANES))


def split(value):
    high = value.astype(jnp.bfloat16)
    low = (value - high.astype(jnp.float32)).astype(jnp.bfloat16)
    return high, low


def mul(a, b, dims=((1,), (0,))):
    return lax.dot_general(a, b, (dims, ((), ())), preferred_element_type=jnp.float32)


def mul_split(a, b, dims=((1,), (0,))):
    return mul(a[0], b[0], dims) + (mul(a[0], b[1], dims) + mul(a[1], b[0], dims))


def main_kernel(
    n_f, count_x, count_y, rank, rescale, in_ref, sent_hbm, spread_ref, *refs
):
    column_refs = refs[:count_y]
    ext_a, ext_b, ext_c, adv, staged, sent_ref, sent_sem = refs[count_y : count_y + 7]
    to_core_ref, from_core_ref = refs[count_y + 7 :]
    margin = 3
    inner = pl.ds(margin, SUBLANES)
    lower = lax.broadcasted_iota(jnp.int32, (margin, SUBLANES, LANES), 1) < HALF

    def each(body):
        for s in range(count_y):
            body(s)

    def fill_margins(ext):
        def one(s):
            before, after = (s - 1) % count_y, (s + 1) % count_y
            for f in range(n_f):
                old = ext[before, f, pl.ds(SUBLANES, margin)]
                own = ext[s, f, pl.ds(SUBLANES, margin)]
                ext[s, f, 0:margin] = pltpu.roll(jnp.where(lower, own, old), HALF, 1)
                own = ext[s, f, pl.ds(margin, margin)]
                new = ext[after, f, pl.ds(margin, margin)]
                ext[s, f, pl.ds(SUBLANES + margin, margin)] = pltpu.roll(
                    jnp.where(lower, new, own), HALF, 1
                )

        each(one)

    row = lax.broadcasted_iota(jnp.int32, (LANES, LANES), 0)
    col = lax.broadcasted_iota(jnp.int32, (LANES, LANES), 1)
    ahead = (row - col) & (LANES - 1)
    taps = jnp.zeros((LANES, LANES), jnp.float32)
    for shift, weight in ((1, 45.0), (2, -9.0), (3, 1.0)):
        taps = jnp.where(ahead == shift, weight, taps)
        taps = jnp.where(ahead == LANES - shift, -weight, taps)
    taps = taps.astype(jnp.bfloat16)
    taps = jnp.concatenate([taps, taps], axis=0)

    def section(ext, step, store):
        def one(s):
            padded = [ext[s, f] for f in range(n_f)]
            center = [p[margin : margin + SUBLANES] for p in padded]
            flux_x = [center[0] * c for c in center]
            flux_x[0] = flux_x[0] + 0.5 * center[3]
            flat = jnp.concatenate(flux_x, axis=0).reshape(n_f * SUBLANES * SUBLANES, LANES)
            along_x = mul(jnp.concatenate(split(flat), axis=1), taps)
            along_x = along_x.reshape(n_f, SUBLANES, SUBLANES, LANES)
            react = (step * REACT_RATE) * center[2] * (1.0 + jnp.tanh(center[3]))
            for f in range(n_f):
                flux_y = padded[1] * padded[f]
                if f == 1:
                    flux_y = flux_y + 0.5 * padded[3]

                def along_y(k):
                    after = flux_y[margin + k : margin + k + SUBLANES]
                    return after - flux_y[margin - k : margin - k + SUBLANES]

                change = (
                    (-45.0 * step / 60.0) * along_y(1)
                    + (9.0 * step / 60.0) * along_y(2)
                    + (-step / 60.0) * (along_y(3) + along_x[f])
                )
                if f == 2:
                    change = change - react
                if f == 3:
                    change = change + HEAT_RELEASE * react
                store(s, f, center[f], change)

        each(one)

    def arrive(s):
        for f in range(n_f):
            got = [
                in_ref[i, s, 4 * f : 4 * f + 4].reshape(SUBLANES, LANES) for i in range(count_x)
            ]
            for y, block in enumerate(exchange(got, LANES // SUBLANES)):
                ext_a[s, f, margin + y] = block

    def first(s, f, center, change):
        ext_b[s, f, inner] = center + change

    def second(s, f, center, change):
        ext_c[s, f, inner] = 0.75 * ext_a[s, f, inner] + (0.25 * center + change)

    def third(s, f, center, change):
        done = (1.0 / 3.0) * ext_a[s, f, inner] + ((2.0 / 3.0) * center + change)
        adv[f, s] = done
        parts = exchange([done[y] for y in range(SUBLANES)], LANES // SUBLANES)
        for i, part in enumerate(parts):
            sent_ref[i, s, 2 * f : 2 * f + 2] = part.reshape(2, HALF, LANES)

    plane = count_y * SUBLANES * SUBLANES
    count = count_x * count_y
    held = in_ref[:, :, 4 * n_f].reshape(2 * count, LANES)
    held_at = lax.broadcasted_iota(jnp.int32, (LANES, 2 * count), 1)
    source = digit(lax.broadcasted_iota(jnp.int32, (LANES, 2 * count), 0), HALF, count)
    rows_of = (held_at == 2 * source).astype(jnp.bfloat16)
    spread_x = [jnp.where(digit(row, 1, HALF) == digit(col, rank, HALF), mul(rows_of, part), 0.0) for part in split(held)]
    picks = (digit(row, 1, rank) == digit(col, n_f, rank)).astype(jnp.bfloat16)
    spread_x = [mul(part.astype(jnp.bfloat16), picks) for part in spread_x]
    weights_x = [
        jnp.concatenate(
            [jnp.where(digit(col, 1, n_f) == f, part, 0.0).astype(jnp.bfloat16) for f in range(n_f)], axis=0
        )
        for part in spread_x
    ]
    r = lax.broadcasted_iota(jnp.int32, (plane, LANES), 0)
    c = lax.broadcasted_iota(jnp.int32, (plane, LANES), 1)
    from_s = digit(r, SUBLANES * SUBLANES, count_y)
    octet, from_y = digit(r, HALF, 2), digit(r, SUBLANES, SUBLANES)
    held_at = lax.broadcasted_iota(jnp.int32, (plane, 2 * count), 1)
    source = ((octet * HALF + digit(from_y, 2, HALF)) * count_y + from_s)[:, : 2 * count]
    rows_of = (held_at == 2 * source + 1).astype(jnp.bfloat16)
    spread_y = [jnp.where(digit(from_y, 1, 2) == digit(c, rank, 2), mul(rows_of, part), 0.0) for part in split(held)]
    spread_y = [part + pltpu.roll(part, rank, 1) for part in spread_y]
    same_z = digit(r, 1, HALF) == digit(c, rank, HALF)
    weights_y = [jnp.where(same_z, part, 0.0).astype(jnp.bfloat16) for part in spread_y]
    for part in range(2):
        spread_ref[part] = weights_x[part]
        to_core_ref[part] = weights_y[part].astype(jnp.float32).T.astype(jnp.bfloat16)
    for part in range(2):
        from_core_ref[part] = weights_y[part]

    each(arrive)
    fill_margins(ext_a)
    section(ext_a, TIME_STEP, first)
    fill_margins(ext_b)
    section(ext_b, 0.25 * TIME_STEP, second)
    fill_margins(ext_c)
    section(ext_c, 2.0 / 3.0 * TIME_STEP, third)
    sent = pltpu.make_async_copy(sent_ref, sent_hbm, sent_sem)
    sent.start()

    @pl.when(lax.axis_index("gy") >= 0)
    def tucker():
        def by_x(value):
            return jnp.concatenate([value[f].reshape(plane, LANES) for f in range(n_f)], axis=1)

        weights_x = [spread_ref[part] for part in range(2)]
        partial = split(mul_split(split(by_x(adv)), weights_x))
        core = mul_split([to_core_ref[part] for part in range(2)], partial)
        columns = rescale * mul_split([from_core_ref[part] for part in range(2)], split(core))

        block = plane // count_y
        for s in range(count_y):
            staged[s, 0:block] = columns[s * block : (s + 1) * block]
            for z in range(HALF):
                at = z * rank + s * SUBLANES
                staged[s, block + z * SUBLANES : block + (z + 1) * SUBLANES] = core[at : at + SUBLANES]
        own = lax.axis_index("gy")
        for k, ref in enumerate(column_refs):
            ref[...] = staged[lax.rem(own + k, count_y)]

    sent.wait()


def expand_kernel(n_f, count_x, count_y, spread_ref, *refs):
    in_refs, out_refs = refs[:count_y], refs[count_y : count_y + count_x]
    held, staged = refs[count_y + count_x :]
    own = lax.axis_index("gy")
    for k, ref in enumerate(in_refs):
        held[lax.rem(own + count_y - k, count_y)] = ref[...]
    block = SUBLANES * SUBLANES
    plane = count_y * block
    columns = split(jnp.concatenate([held[s, 0:block] for s in range(count_y)], axis=0))
    for f in range(n_f):
        weights = [spread_ref[part, f * LANES : (f + 1) * LANES] for part in range(2)]
        rebuilt = mul_split(columns, weights, ((1,), (1,)))
        rebuilt = rebuilt.reshape(count_y, SUBLANES, SUBLANES, LANES)
        for s in range(count_y):
            parts = exchange([rebuilt[s, y] for y in range(SUBLANES)], LANES // SUBLANES)
            for i, part in enumerate(parts):
                at = (f * count_y + s) * SUBLANES
                staged[i, at : at + SUBLANES] = part
    by_f = [
        exchange([held[s, block + z * SUBLANES : block + (z + 1) * SUBLANES] for z in range(HALF)], 1)
        for s in range(count_y)
    ]
    left = lax.broadcasted_iota(jnp.int32, (SUBLANES, LANES), 1) < LANES // 2
    by_i = []
    for f in range(n_f):
        tiles = exchange([by_f[s][f] for s in range(count_y)], HALF)
        by_i.append(exchange(tiles, LANES // SUBLANES))
    for i in range(count_x):
        for pair in range(n_f // 2):
            low, high = by_i[2 * pair][i % HALF], by_i[2 * pair + 1][i % HALF]
            if i < HALF:
                tile = jnp.where(left, low, pltpu.roll(high, LANES // 2, 1))
            else:
                tile = jnp.where(left, pltpu.roll(low, LANES // 2, 1), high)
            at = (n_f * count_y + pair) * SUBLANES
            staged[i, at : at + SUBLANES] = tile
    own = lax.axis_index("gx")
    for k, ref in enumerate(out_refs):
        ref[...] = staged[lax.rem(own + k, count_x)]


def scatter_rows(turned, octet, block_x, block_y, target, f):
    for y in range(SUBLANES):
        rows = pl.ds(octet * SUBLANES + y, block_x, stride=block_y)
        target[f, rows, :] = turned[y * block_x : (y + 1) * block_x]


def results_kernel(
    block_x, block_y, in_ref, rebuilt_ref, core_ref, advanced_hbm, rebuilt_hbm, core_hbm, advanced_ref, sems
):
    n_f = advanced_ref.shape[0]
    leaving = [
        pltpu.make_async_copy(advanced_ref.at[f], advanced_hbm.at[f], sems.at[f]) for f in range(n_f)
    ]
    leaving.append(pltpu.make_async_copy(rebuilt_ref, rebuilt_hbm, sems.at[n_f]))
    leaving.append(pltpu.make_async_copy(core_ref, core_hbm, sems.at[n_f + 1]))
    leaving[n_f].start()
    leaving[n_f + 1].start()
    for f in range(n_f):
        for octet in range(2):
            place = 2 * f + octet
            matrix = jnp.concatenate([in_ref[:, 0, place], in_ref[:, 1, place]], axis=1)
            turned = matrix.reshape(LANES, LANES).T
            scatter_rows(turned, octet, block_x, block_y, advanced_ref, f)
        leaving[f].start()
    for copy in leaving:
        copy.wait()


def rebuilt_kernel(block_x, block_y, count_x, count_y, *refs):
    in_refs, (rebuilt_ref, core_ref, held) = refs[:count_x], refs[count_x:]
    n_f = rebuilt_ref.shape[0]
    own = lax.axis_index("gx")
    for k, ref in enumerate(in_refs):
        held[lax.rem(own + count_x - k, count_x)] = ref[...]
    a_count = core_ref.shape[1]
    for pair in range(n_f // 2):
        at = (n_f * count_y + pair) * SUBLANES
        tiles = exchange([held[i, at : at + SUBLANES] for i in range(count_x)], LANES // SUBLANES)
        for place, tile in enumerate(tiles):
            core_ref[2 * pair + place // a_count, place % a_count] = tile
    pairs = count_y // 2
    lower = lax.broadcasted_iota(jnp.int32, (count_x, pairs, SUBLANES, LANES), 2) < HALF
    for f in range(n_f):
        at = pl.ds(f * count_y * SUBLANES, count_y * SUBLANES)
        tiles = held[:, at, :].reshape(count_x, pairs, 2, SUBLANES, LANES)
        even, odd = tiles[:, :, 0], tiles[:, :, 1]
        first = jnp.where(lower, even, pltpu.roll(odd, HALF, 2))
        second = jnp.where(lower, pltpu.roll(even, HALF, 2), odd)
        for octet, part in enumerate((first, second)):
            turned = part.reshape(LANES, LANES).T
            scatter_rows(turned, octet, block_x, block_y, rebuilt_ref, f)


def z_plan(fields, factor_x, factor_y):
    n_f, block_x, block_y, n_z = fields.shape
    rank = factor_x.shape[1]
    count_x = lax.axis_size("gx")
    count_y = lax.axis_size("gy")
    devices = count_x * count_y
    pairs = devices // 2
    rescale = math.sqrt(float(block_x * count_x) * float(block_y * count_y)) / rank
    vmem = pl.BlockSpec(memory_space=pltpu.VMEM)
    hbm = pl.BlockSpec(memory_space=pltpu.HBM)
    f32 = jnp.float32

    def array(shape, dtype=f32):
        return jax.ShapeDtypeStruct(shape, dtype)

    def call(
        kernel, name, outs, scratch, operands, space=vmem, out_spaces=None, limit=32 * 1024 * 1024, cost=10**9
    ):
        return pl.pallas_call(
            kernel,
            out_shape=tuple(outs),
            in_specs=[space] * len(operands),
            out_specs=out_spaces or (vmem,) * len(outs),
            scratch_shapes=scratch,
            compiler_params=pltpu.CompilerParams(vmem_limit_bytes=limit),
            cost_estimate=pl.CostEstimate(flops=cost, bytes_accessed=0, transcendentals=0),
            name=name,
        )(*operands)

    def swap(blocks):
        blocks = blocks.reshape((devices,) + blocks.shape[2:])
        return lax.all_to_all(blocks, ("gx", "gy"), 0, 0, tiled=True)

    def pass_on(blocks, axis):
        count = len(blocks)
        moved = [
            lax.ppermute(block, axis, [(i, (i + k) % count) for i in range(count)])
            for k, block in enumerate(blocks)
            if k
        ]
        return [blocks[0]] + moved

    flat = (n_f, block_x * block_y, n_z)
    (packed,) = call(
        pack_kernel,
        "pack",
        [array((pairs, 2, 4 * n_f + 1, 2, n_z))],
        [
            pltpu.VMEM(flat, f32),
            pltpu.VMEM(factor_x.shape, f32),
            pltpu.VMEM(factor_y.shape, f32),
            pltpu.SemaphoreType.DMA((n_f + 2,)),
        ],
        tuple(
            pltpu.with_memory_space_constraint(v, pltpu.HBM)
            for v in (fields.reshape(flat), factor_x, factor_y)
        ),
        space=hbm,
    )
    planes = swap(packed).reshape(count_x, count_y, 4 * n_f + 1, 2, n_z)
    extended = pltpu.VMEM((count_y, n_f, SUBLANES + 6, SUBLANES, LANES), f32)
    rows = SUBLANES * SUBLANES + HALF * SUBLANES
    plane = count_y * SUBLANES * SUBLANES
    sent, spread, *columns = call(
        functools.partial(main_kernel, n_f, count_x, count_y, rank, rescale),
        "sections",
        [
            array((count_x, count_y, 2 * n_f, HALF, n_z)),
            array((2, n_f * LANES, LANES), jnp.bfloat16),
        ]
        + [array((rows, LANES))] * count_y,
        [extended] * 3
        + [
            pltpu.VMEM((n_f, count_y, SUBLANES, SUBLANES, LANES), f32),
            pltpu.VMEM((count_y, rows, LANES), f32),
            pltpu.VMEM((count_x, count_y, 2 * n_f, HALF, n_z), f32),
            pltpu.SemaphoreType.DMA,
            pltpu.VMEM((2, LANES, plane), jnp.bfloat16),
            pltpu.VMEM((2, plane, LANES), jnp.bfloat16),
        ],
        (planes,),
        out_spaces=(hbm,) + (vmem,) * (1 + count_y),
    )
    columns = pass_on(columns, "gy")
    sent = swap(sent).reshape(pairs, 2, 2 * n_f, HALF, n_z)
    rows = (n_f * count_y + n_f // 2) * SUBLANES
    blocks = call(
        functools.partial(expand_kernel, n_f, count_x, count_y),
        "expand",
        [array((rows, LANES))] * count_x,
        [
            pltpu.VMEM((count_y,) + columns[0].shape, f32),
            pltpu.VMEM((count_x, rows, LANES), f32),
        ],
        (spread, *columns),
        cost=20000000000,
    )
    blocks = pass_on(blocks, "gx")
    core_shape = (n_f, rank // count_x, rank // count_y, n_z)
    rebuilt, core = call(
        functools.partial(rebuilt_kernel, block_x, block_y, count_x, count_y),
        "rebuilt",
        [array(flat), array(core_shape)],
        [pltpu.VMEM((count_x, rows, LANES), f32)],
        tuple(blocks),
    )
    advanced, rebuilt, core = call(
        functools.partial(results_kernel, block_x, block_y),
        "results",
        [array(flat), array(flat), array(core_shape)],
        [pltpu.VMEM(flat, f32), pltpu.SemaphoreType.DMA((n_f + 2,))],
        (sent, rebuilt, core),
        out_spaces=(hbm,) * 3,
    )
    return advanced.reshape(fields.shape), core, rebuilt.reshape(fields.shape)


def extended(block, sides, width):
    for axis, dim in sides:
        count = lax.axis_size(axis)
        forward = [(i, i + 1) for i in range(count - 1)]
        forward.append((count - 1, 0))
        backward = [(target, source) for source, target in forward]
        low = lax.ppermute(
            lax.slice_in_dim(block, block.shape[dim] - width, None, axis=dim), axis, forward
        )
        high = lax.ppermute(lax.slice_in_dim(block, 0, width, axis=dim), axis, backward)
        block = jnp.concatenate([low, block, high], axis=dim)
    return block


def inner_part(array, margin):
    return array[:, margin : array.shape[1] - margin, margin : array.shape[2] - margin]


def tendency(padded):
    n_x = padded.shape[1]
    n_y = padded.shape[2]
    pressure = 0.5 * padded[3]
    flux_x = padded[0][None] * padded
    flux_x = flux_x.at[0].add(pressure)
    flux_y = padded[1][None] * padded
    flux_y = flux_y.at[1].add(pressure)

    def along_x(shift):
        return (
            flux_x[:, 3 + shift : n_x - 3 + shift, 3 : n_y - 3]
            - flux_x[:, 3 - shift : n_x - 3 - shift, 3 : n_y - 3]
        )

    def along_y(shift):
        return (
            flux_y[:, 3 : n_x - 3, 3 + shift : n_y - 3 + shift]
            - flux_y[:, 3 : n_x - 3, 3 - shift : n_y - 3 - shift]
        )

    deriv_x = (45.0 * along_x(1) - 9.0 * along_x(2) + along_x(3)) / 60.0
    deriv_y = (45.0 * along_y(1) - 9.0 * along_y(2) + along_y(3)) / 60.0
    center = inner_part(padded, 3)
    react = REACT_RATE * center[2] * (1.0 + jnp.tanh(center[3]))
    zeros = jnp.zeros_like(react)
    source = jnp.stack([zeros, zeros, -react, HEAT_RELEASE * react])
    return source - deriv_x - deriv_y


def section_tendency(state):
    padded = extended(state, (("gx", 1), ("gy", 2)), 3)
    return tendency(padded)


def per_device(fields, factor_x, factor_y):
    high = lax.Precision.HIGHEST
    section_one = fields + TIME_STEP * section_tendency(fields)
    section_two = 0.75 * fields + 0.25 * (section_one + TIME_STEP * section_tendency(section_one))
    advanced = 1.0 / 3.0 * fields + 2.0 / 3.0 * (
        section_two + TIME_STEP * section_tendency(section_two)
    )
    rank_full = factor_x.shape[1]
    count_x = lax.axis_size("gx")
    count_y = lax.axis_size("gy")
    partial_x = jnp.einsum("fxyz,xa->fayz", advanced, factor_x, precision=high)
    partial_value = lax.psum_scatter(partial_x, "gx", scatter_dimension=1, tiled=True)
    local_core = jnp.einsum("fayz,yb->fabz", partial_value, factor_y, precision=high)
    core_tensor = lax.psum_scatter(local_core, "gy", scatter_dimension=2, tiled=True)
    weights = factor_y
    columns = jnp.einsum(
        "fabz,yb->fayz",
        lax.all_gather(core_tensor, "gy", axis=2, tiled=True),
        weights,
        precision=high,
    )
    weights = factor_x
    expanded = jnp.einsum(
        "fayz,xa->fxyz", lax.all_gather(columns, "gx", axis=1, tiled=True), weights, precision=high
    )
    total_x = factor_x.shape[0] * count_x
    total_y = factor_y.shape[0] * count_y
    rescale = math.sqrt(float(total_x) * float(total_y)) / rank_full
    rebuilt = rescale * expanded
    return (advanced, core_tensor, rebuilt)


def solution(mesh):
    placed = (P(None, "gx", "gy", None), P("gx", None), P("gy", None))
    out = P(None, "gx", "gy", None)

    def whole(fields, factor_x, factor_y):
        plan = z_plan if fits(mesh, fields, factor_x, factor_y) else per_device
        return jax.shard_map(
            plan, mesh=mesh, in_specs=placed, out_specs=(out, out, out), check_vma=False
        )(fields, factor_x, factor_y)

    return whole
```

```python
import functools
import math

import jax
import jax.numpy as jnp
from jax import lax
from jax.experimental import pallas as pl
from jax.experimental.pallas import tpu as pltpu
from jax.sharding import PartitionSpec as P

TIME_STEP = 0.2
REACT_RATE = 0.5
HEAT_RELEASE = 1.0
SUBLANES = 8
LANES = 128
HALF = SUBLANES // 2


def fits(mesh, fields, factor_x, factor_y):
    n_f, n_x, n_y, n_z = fields.shape
    count_x, count_y = mesh.shape["gx"], mesh.shape["gy"]
    devices = count_x * count_y
    rank = factor_x.shape[1]
    if n_x % count_x or n_y % count_y or n_z % devices:
        return False
    block_x, block_y, block_z = n_x // count_x, n_y // count_y, n_z // devices
    return (
        n_x == LANES
        and n_z == LANES
        and n_f == HALF
        and block_z == HALF
        and block_x == 2 * SUBLANES
        and block_y == 2 * SUBLANES
        and count_x == SUBLANES
        and count_y == HALF
        and rank == count_y * SUBLANES
        and factor_y.shape[1] == rank
        and n_f * rank == LANES
    )


def digit(index, size, count):
    return lax.shift_right_logical(index, size.bit_length() - 1) & (count - 1)


def exchange(blocks, stride):
    count = len(blocks)
    period = stride * count
    group = digit(lax.broadcasted_iota(jnp.int32, (SUBLANES, LANES), 1), stride, count)
    if period == LANES:
        blocks = [pltpu.roll(b, i * stride, 1) if i else b for i, b in enumerate(blocks)]
        step = 1
        while step < count:
            taken = (group & step) != 0
            blocks = [
                jnp.where(taken, blocks[(i + step) % count], blocks[i]) for i in range(count)
            ]
            step *= 2
        blocks = [blocks[-j % count] for j in range(count)]
        return [pltpu.roll(b, LANES - j * stride, 1) if j else b for j, b in enumerate(blocks)]
    blocks = list(blocks)
    step = 1
    while step < count:
        upper = (group & step) != 0
        for i in range(count):
            if i & step:
                continue
            low, high = blocks[i], blocks[i + step]
            blocks[i] = jnp.where(upper, pltpu.roll(high, stride * step, 1), low)
            blocks[i + step] = jnp.where(upper, high, pltpu.roll(low, LANES - stride * step, 1))
        step *= 2
    return blocks


def pack_kernel(constants, fields_hbm, factor_x_hbm, factor_y_hbm, out_ref, *refs):
    *constant_refs, fields_ref, x_ref, y_ref, sems = refs
    n_f, rows, _ = fields_ref.shape
    block_x = x_ref.shape[0]
    block_y = rows // block_x
    tiles = LANES // SUBLANES
    copies = [
        pltpu.make_async_copy(fields_hbm.at[f], fields_ref.at[f], sems.at[f]) for f in range(n_f)
    ]
    copies.append(pltpu.make_async_copy(factor_x_hbm, x_ref, sems.at[n_f]))
    copies.append(pltpu.make_async_copy(factor_y_hbm, y_ref, sems.at[n_f + 1]))
    for copy in copies:
        copy.start()
    constants(*constant_refs)
    for f in range(n_f):
        if f % 2 == 0:
            copies[f].wait()
            copies[f + 1].wait()
        for octet in range(2):
            matrix = jnp.concatenate(
                [
                    fields_ref[f, pl.ds(octet * SUBLANES + y, block_x, stride=block_y), :]
                    for y in range(SUBLANES)
                ],
                axis=0,
            )
            turned = matrix.T.reshape(tiles, SUBLANES, LANES)
            for part in range(2):
                at = 2 * (2 * f + octet) + part
                out_ref[:, 0, at] = turned[:, 2 * part : 2 * part + 2]
                out_ref[:, 1, at] = turned[:, HALF + 2 * part : HALF + 2 * part + 2]
    copies[n_f].wait()
    copies[n_f + 1].wait()
    own_x = x_ref[pl.ds(lax.axis_index("gy") * HALF, HALF), :]
    own_y = y_ref[pl.ds(lax.axis_index("gx") * 2, 2), :]
    row_x = jnp.concatenate([own_x[j : j + 1] for j in range(HALF)], axis=1)
    row_y = jnp.concatenate([own_y[j % 2 : j % 2 + 1] for j in range(HALF)], axis=1)
    factors = jnp.concatenate([row_x, row_y], axis=0)
    out_ref[:, :, 4 * n_f] = jnp.broadcast_to(factors[None, None], (tiles, 2, 2, LANES))


def split(value):
    high = value.astype(jnp.bfloat16)
    low = (value - high.astype(jnp.float32)).astype(jnp.bfloat16)
    return high, low


def mul(a, b, dims=((1,), (0,))):
    return lax.dot_general(a, b, (dims, ((), ())), preferred_element_type=jnp.float32)


def mul_split(a, b, dims=((1,), (0,))):
    return mul(a[0], b[0], dims) + (mul(a[0], b[1], dims) + mul(a[1], b[0], dims))


def constants_kernel(
    n_f, count_x, count_y, rank, taps_ref, rows_x_ref, lanes_x_ref, picks_ref, rows_y_ref, lanes_y_ref
):
    row = lax.broadcasted_iota(jnp.int32, (LANES, LANES), 0)
    col = lax.broadcasted_iota(jnp.int32, (LANES, LANES), 1)
    ahead = (row - col) & (LANES - 1)
    taps = jnp.zeros((LANES, LANES), jnp.float32)
    for shift, weight in ((1, 45.0), (2, -9.0), (3, 1.0)):
        taps = jnp.where(ahead == shift, weight, taps)
        taps = jnp.where(ahead == LANES - shift, -weight, taps)
    taps = taps.astype(jnp.bfloat16)
    taps = jnp.concatenate([taps, taps], axis=0)
    taps_ref[...] = taps
    count = count_x * count_y
    plane = count_y * SUBLANES * SUBLANES
    held_at = lax.broadcasted_iota(jnp.int32, (LANES, 2 * count), 1)
    source = digit(lax.broadcasted_iota(jnp.int32, (LANES, 2 * count), 0), HALF, count)
    rows_x_ref[...] = (held_at == 2 * source).astype(jnp.bfloat16)
    lanes_x_ref[...] = (digit(row, 1, HALF) == digit(col, rank, HALF)).astype(jnp.float32)
    picks_ref[...] = (digit(row, 1, rank) == digit(col, n_f, rank)).astype(jnp.bfloat16)
    r = lax.broadcasted_iota(jnp.int32, (plane, LANES), 0)
    c = lax.broadcasted_iota(jnp.int32, (plane, LANES), 1)
    from_s = digit(r, SUBLANES * SUBLANES, count_y)
    octet, from_y = digit(r, HALF, 2), digit(r, SUBLANES, SUBLANES)
    held_at = lax.broadcasted_iota(jnp.int32, (plane, 2 * count), 1)
    source = ((octet * HALF + digit(from_y, 2, HALF)) * count_y + from_s)[:, : 2 * count]
    rows_y_ref[...] = (held_at == 2 * source + 1).astype(jnp.bfloat16)
    lanes_y_ref[0] = (digit(from_y, 1, 2) == digit(c, rank, 2)).astype(jnp.float32)
    lanes_y_ref[1] = (digit(r, 1, HALF) == digit(c, rank, HALF)).astype(jnp.float32)


def main_kernel(
    n_f, count_x, count_y, rank, rescale, in_ref,
    taps_ref, rows_x_ref, lanes_x_ref, picks_ref, rows_y_ref, lanes_y_ref, sent_hbm, spread_ref, *refs
):
    column_refs = refs[:count_y]
    ext_a, ext_b, ext_c, adv, staged, sent_ref, sent_sem = refs[count_y : count_y + 7]
    to_core_ref, from_core_ref = refs[count_y + 7 :]
    margin = 3
    inner = pl.ds(margin, SUBLANES)
    lower = lax.broadcasted_iota(jnp.int32, (margin, SUBLANES, LANES), 1) < HALF

    def each(body):
        for s in range(count_y):
            body(s)

    def fill_margins(ext):
        def one(s):
            before, after = (s - 1) % count_y, (s + 1) % count_y
            for f in range(n_f):
                old = ext[before, f, pl.ds(SUBLANES, margin)]
                own = ext[s, f, pl.ds(SUBLANES, margin)]
                ext[s, f, 0:margin] = pltpu.roll(jnp.where(lower, own, old), HALF, 1)
                own = ext[s, f, pl.ds(margin, margin)]
                new = ext[after, f, pl.ds(margin, margin)]
                ext[s, f, pl.ds(SUBLANES + margin, margin)] = pltpu.roll(
                    jnp.where(lower, new, own), HALF, 1
                )

        each(one)

    taps = taps_ref[...]

    def section(ext, step, store):
        def one(s):
            padded = [ext[s, f] for f in range(n_f)]
            center = [p[margin : margin + SUBLANES] for p in padded]
            flux_x = [center[0] * c for c in center]
            flux_x[0] = flux_x[0] + 0.5 * center[3]
            flat = jnp.concatenate(flux_x, axis=0).reshape(n_f * SUBLANES * SUBLANES, LANES)
            along_x = mul(jnp.concatenate(split(flat), axis=1), taps)
            along_x = along_x.reshape(n_f, SUBLANES, SUBLANES, LANES)
            react = (step * REACT_RATE) * center[2] * (1.0 + jnp.tanh(center[3]))
            for f in range(n_f):
                flux_y = padded[1] * padded[f]
                if f == 1:
                    flux_y = flux_y + 0.5 * padded[3]

                def along_y(k):
                    after = flux_y[margin + k : margin + k + SUBLANES]
                    return after - flux_y[margin - k : margin - k + SUBLANES]

                change = (
                    (-45.0 * step / 60.0) * along_y(1)
                    + (9.0 * step / 60.0) * along_y(2)
                    + (-step / 60.0) * (along_y(3) + along_x[f])
                )
                if f == 2:
                    change = change - react
                if f == 3:
                    change = change + HEAT_RELEASE * react
                store(s, f, center[f], change)

        each(one)

    def arrive(s):
        for f in range(n_f):
            got = [
                in_ref[i, s, 4 * f : 4 * f + 4].reshape(SUBLANES, LANES) for i in range(count_x)
            ]
            for y, block in enumerate(exchange(got, LANES // SUBLANES)):
                ext_a[s, f, margin + y] = block

    def first(s, f, center, change):
        ext_b[s, f, inner] = center + change

    def second(s, f, center, change):
        ext_c[s, f, inner] = 0.75 * ext_a[s, f, inner] + (0.25 * center + change)

    def third(s, f, center, change):
        done = (1.0 / 3.0) * ext_a[s, f, inner] + ((2.0 / 3.0) * center + change)
        adv[f, s] = done
        parts = exchange([done[y] for y in range(SUBLANES)], LANES // SUBLANES)
        for i, part in enumerate(parts):
            sent_ref[i, s, 2 * f : 2 * f + 2] = part.reshape(2, HALF, LANES)

    plane = count_y * SUBLANES * SUBLANES
    held = in_ref[:, :, 4 * n_f].reshape(2 * count_x * count_y, LANES)
    held = split(held)
    spread_x = [mul(rows_x_ref[...], part) * lanes_x_ref[...] for part in held]
    spread_x = [mul(part.astype(jnp.bfloat16), picks_ref[...]) for part in spread_x]
    col = lax.broadcasted_iota(jnp.int32, (LANES, LANES), 1)
    weights_x = [
        jnp.concatenate(
            [jnp.where(digit(col, 1, n_f) == f, part, 0.0).astype(jnp.bfloat16) for f in range(n_f)], axis=0
        )
        for part in spread_x
    ]
    spread_y = [mul(rows_y_ref[...], part) * lanes_y_ref[0] for part in held]
    spread_y = [part + pltpu.roll(part, rank, 1) for part in spread_y]
    weights_y = [(part * lanes_y_ref[1]).astype(jnp.bfloat16) for part in spread_y]
    for part in range(2):
        spread_ref[part] = weights_x[part]
        to_core_ref[part] = weights_y[part].astype(jnp.float32).T.astype(jnp.bfloat16)
    for part in range(2):
        from_core_ref[part] = weights_y[part]

    each(arrive)
    fill_margins(ext_a)
    section(ext_a, TIME_STEP, first)
    fill_margins(ext_b)
    section(ext_b, 0.25 * TIME_STEP, second)
    fill_margins(ext_c)
    section(ext_c, 2.0 / 3.0 * TIME_STEP, third)
    sent = pltpu.make_async_copy(sent_ref, sent_hbm, sent_sem)
    sent.start()

    @pl.when(lax.axis_index("gy") >= 0)
    def tucker():
        def by_x(value):
            return jnp.concatenate([value[f].reshape(plane, LANES) for f in range(n_f)], axis=1)

        weights_x = [spread_ref[part] for part in range(2)]
        partial = split(mul_split(split(by_x(adv)), weights_x))
        core = mul_split([to_core_ref[part] for part in range(2)], partial)
        columns = rescale * mul_split([from_core_ref[part] for part in range(2)], split(core))

        block = plane // count_y
        for s in range(count_y):
            staged[s, 0:block] = columns[s * block : (s + 1) * block]
            for z in range(HALF):
                at = z * rank + s * SUBLANES
                staged[s, block + z * SUBLANES : block + (z + 1) * SUBLANES] = core[at : at + SUBLANES]
        own = lax.axis_index("gy")
        for k, ref in enumerate(column_refs):
            ref[...] = staged[lax.rem(own + k, count_y)]

    sent.wait()


def expand_kernel(n_f, count_x, count_y, spread_ref, *refs):
    in_refs, out_refs = refs[:count_y], refs[count_y : count_y + count_x]
    held, staged = refs[count_y + count_x :]
    own = lax.axis_index("gy")
    for k, ref in enumerate(in_refs):
        held[lax.rem(own + count_y - k, count_y)] = ref[...]
    block = SUBLANES * SUBLANES
    plane = count_y * block
    columns = split(jnp.concatenate([held[s, 0:block] for s in range(count_y)], axis=0))
    for f in range(n_f):
        weights = [spread_ref[part, f * LANES : (f + 1) * LANES] for part in range(2)]
        rebuilt = mul_split(columns, weights, ((1,), (1,)))
        rebuilt = rebuilt.reshape(count_y, SUBLANES, SUBLANES, LANES)
        for s in range(count_y):
            parts = exchange([rebuilt[s, y] for y in range(SUBLANES)], LANES // SUBLANES)
            for i, part in enumerate(parts):
                at = (f * count_y + s) * SUBLANES
                staged[i, at : at + SUBLANES] = part
    by_f = [
        exchange([held[s, block + z * SUBLANES : block + (z + 1) * SUBLANES] for z in range(HALF)], 1)
        for s in range(count_y)
    ]
    left = lax.broadcasted_iota(jnp.int32, (SUBLANES, LANES), 1) < LANES // 2
    by_i = []
    for f in range(n_f):
        tiles = exchange([by_f[s][f] for s in range(count_y)], HALF)
        by_i.append(exchange(tiles, LANES // SUBLANES))
    for i in range(count_x):
        for pair in range(n_f // 2):
            low, high = by_i[2 * pair][i % HALF], by_i[2 * pair + 1][i % HALF]
            if i < HALF:
                tile = jnp.where(left, low, pltpu.roll(high, LANES // 2, 1))
            else:
                tile = jnp.where(left, pltpu.roll(low, LANES // 2, 1), high)
            at = (n_f * count_y + pair) * SUBLANES
            staged[i, at : at + SUBLANES] = tile
    own = lax.axis_index("gx")
    for k, ref in enumerate(out_refs):
        ref[...] = staged[lax.rem(own + k, count_x)]


def scatter_rows(turned, octet, block_x, block_y, target, f):
    for y in range(SUBLANES):
        rows = pl.ds(octet * SUBLANES + y, block_x, stride=block_y)
        target[f, rows, :] = turned[y * block_x : (y + 1) * block_x]


def results_kernel(
    block_x, block_y, in_ref, rebuilt_ref, core_ref, advanced_hbm, rebuilt_hbm, core_hbm, advanced_ref, sems
):
    n_f = advanced_ref.shape[0]
    leaving = [
        pltpu.make_async_copy(advanced_ref.at[f], advanced_hbm.at[f], sems.at[f]) for f in range(n_f)
    ]
    leaving.append(pltpu.make_async_copy(rebuilt_ref, rebuilt_hbm, sems.at[n_f]))
    leaving.append(pltpu.make_async_copy(core_ref, core_hbm, sems.at[n_f + 1]))
    leaving[n_f].start()
    leaving[n_f + 1].start()
    for f in range(n_f):
        for octet in range(2):
            place = 2 * f + octet
            matrix = jnp.concatenate([in_ref[:, 0, place], in_ref[:, 1, place]], axis=1)
            turned = matrix.reshape(LANES, LANES).T
            scatter_rows(turned, octet, block_x, block_y, advanced_ref, f)
        leaving[f].start()
    for copy in leaving:
        copy.wait()


def rebuilt_kernel(block_x, block_y, count_x, count_y, *refs):
    in_refs, (rebuilt_ref, core_ref, held) = refs[:count_x], refs[count_x:]
    n_f = rebuilt_ref.shape[0]
    own = lax.axis_index("gx")
    for k, ref in enumerate(in_refs):
        held[lax.rem(own + count_x - k, count_x)] = ref[...]
    a_count = core_ref.shape[1]
    for pair in range(n_f // 2):
        at = (n_f * count_y + pair) * SUBLANES
        tiles = exchange([held[i, at : at + SUBLANES] for i in range(count_x)], LANES // SUBLANES)
        for place, tile in enumerate(tiles):
            core_ref[2 * pair + place // a_count, place % a_count] = tile
    pairs = count_y // 2
    lower = lax.broadcasted_iota(jnp.int32, (count_x, pairs, SUBLANES, LANES), 2) < HALF
    for f in range(n_f):
        at = pl.ds(f * count_y * SUBLANES, count_y * SUBLANES)
        tiles = held[:, at, :].reshape(count_x, pairs, 2, SUBLANES, LANES)
        even, odd = tiles[:, :, 0], tiles[:, :, 1]
        first = jnp.where(lower, even, pltpu.roll(odd, HALF, 2))
        second = jnp.where(lower, pltpu.roll(even, HALF, 2), odd)
        for octet, part in enumerate((first, second)):
            turned = part.reshape(LANES, LANES).T
            scatter_rows(turned, octet, block_x, block_y, rebuilt_ref, f)


def z_plan(fields, factor_x, factor_y):
    n_f, block_x, block_y, n_z = fields.shape
    rank = factor_x.shape[1]
    count_x = lax.axis_size("gx")
    count_y = lax.axis_size("gy")
    devices = count_x * count_y
    pairs = devices // 2
    rescale = math.sqrt(float(block_x * count_x) * float(block_y * count_y)) / rank
    vmem = pl.BlockSpec(memory_space=pltpu.VMEM)
    hbm = pl.BlockSpec(memory_space=pltpu.HBM)
    f32 = jnp.float32

    def array(shape, dtype=f32):
        return jax.ShapeDtypeStruct(shape, dtype)

    def call(
        kernel, name, outs, scratch, operands, space=vmem, out_spaces=None, limit=32 * 1024 * 1024, cost=10**9
    ):
        return pl.pallas_call(
            kernel,
            out_shape=tuple(outs),
            in_specs=[space] * len(operands),
            out_specs=out_spaces or (vmem,) * len(outs),
            scratch_shapes=scratch,
            compiler_params=pltpu.CompilerParams(vmem_limit_bytes=limit),
            cost_estimate=pl.CostEstimate(flops=cost, bytes_accessed=0, transcendentals=0),
            name=name,
        )(*operands)

    def swap(blocks):
        blocks = blocks.reshape((devices,) + blocks.shape[2:])
        return lax.all_to_all(blocks, ("gx", "gy"), 0, 0, tiled=True)

    def pass_on(blocks, axis):
        count = len(blocks)
        moved = [
            lax.ppermute(block, axis, [(i, (i + k) % count) for i in range(count)])
            for k, block in enumerate(blocks)
            if k
        ]
        return [blocks[0]] + moved

    flat = (n_f, block_x * block_y, n_z)
    plane = count_y * SUBLANES * SUBLANES
    packed, *constants = call(
        functools.partial(
            pack_kernel, functools.partial(constants_kernel, n_f, count_x, count_y, rank)
        ),
        "pack",
        [
            array((pairs, 2, 4 * n_f + 1, 2, n_z)),
            array((2 * LANES, LANES), jnp.bfloat16),
            array((LANES, 2 * devices), jnp.bfloat16),
            array((LANES, LANES)),
            array((LANES, LANES), jnp.bfloat16),
            array((plane, 2 * devices), jnp.bfloat16),
            array((2, plane, LANES)),
        ],
        [
            pltpu.VMEM(flat, f32),
            pltpu.VMEM(factor_x.shape, f32),
            pltpu.VMEM(factor_y.shape, f32),
            pltpu.SemaphoreType.DMA((n_f + 2,)),
        ],
        tuple(
            pltpu.with_memory_space_constraint(v, pltpu.HBM)
            for v in (fields.reshape(flat), factor_x, factor_y)
        ),
        space=hbm,
    )
    planes = swap(packed).reshape(count_x, count_y, 4 * n_f + 1, 2, n_z)
    extended = pltpu.VMEM((count_y, n_f, SUBLANES + 6, SUBLANES, LANES), f32)
    rows = SUBLANES * SUBLANES + HALF * SUBLANES
    plane = count_y * SUBLANES * SUBLANES
    sent, spread, *columns = call(
        functools.partial(main_kernel, n_f, count_x, count_y, rank, rescale),
        "sections",
        [
            array((count_x, count_y, 2 * n_f, HALF, n_z)),
            array((2, n_f * LANES, LANES), jnp.bfloat16),
        ]
        + [array((rows, LANES))] * count_y,
        [extended] * 3
        + [
            pltpu.VMEM((n_f, count_y, SUBLANES, SUBLANES, LANES), f32),
            pltpu.VMEM((count_y, rows, LANES), f32),
            pltpu.VMEM((count_x, count_y, 2 * n_f, HALF, n_z), f32),
            pltpu.SemaphoreType.DMA,
            pltpu.VMEM((2, LANES, plane), jnp.bfloat16),
            pltpu.VMEM((2, plane, LANES), jnp.bfloat16),
        ],
        (planes, *constants),
        out_spaces=(hbm,) + (vmem,) * (1 + count_y),
    )
    columns = pass_on(columns, "gy")
    sent = swap(sent).reshape(pairs, 2, 2 * n_f, HALF, n_z)
    rows = (n_f * count_y + n_f // 2) * SUBLANES
    blocks = call(
        functools.partial(expand_kernel, n_f, count_x, count_y),
        "expand",
        [array((rows, LANES))] * count_x,
        [
            pltpu.VMEM((count_y,) + columns[0].shape, f32),
            pltpu.VMEM((count_x, rows, LANES), f32),
        ],
        (spread, *columns),
        cost=20000000000,
    )
    blocks = pass_on(blocks, "gx")
    core_shape = (n_f, rank // count_x, rank // count_y, n_z)
    rebuilt, core = call(
        functools.partial(rebuilt_kernel, block_x, block_y, count_x, count_y),
        "rebuilt",
        [array(flat), array(core_shape)],
        [pltpu.VMEM((count_x, rows, LANES), f32)],
        tuple(blocks),
    )
    advanced, rebuilt, core = call(
        functools.partial(results_kernel, block_x, block_y),
        "results",
        [array(flat), array(flat), array(core_shape)],
        [pltpu.VMEM(flat, f32), pltpu.SemaphoreType.DMA((n_f + 2,))],
        (sent, rebuilt, core),
        out_spaces=(hbm,) * 3,
    )
    return advanced.reshape(fields.shape), core, rebuilt.reshape(fields.shape)


def extended(block, sides, width):
    for axis, dim in sides:
        count = lax.axis_size(axis)
        forward = [(i, i + 1) for i in range(count - 1)]
        forward.append((count - 1, 0))
        backward = [(target, source) for source, target in forward]
        low = lax.ppermute(
            lax.slice_in_dim(block, block.shape[dim] - width, None, axis=dim), axis, forward
        )
        high = lax.ppermute(lax.slice_in_dim(block, 0, width, axis=dim), axis, backward)
        block = jnp.concatenate([low, block, high], axis=dim)
    return block


def inner_part(array, margin):
    return array[:, margin : array.shape[1] - margin, margin : array.shape[2] - margin]


def tendency(padded):
    n_x = padded.shape[1]
    n_y = padded.shape[2]
    pressure = 0.5 * padded[3]
    flux_x = padded[0][None] * padded
    flux_x = flux_x.at[0].add(pressure)
    flux_y = padded[1][None] * padded
    flux_y = flux_y.at[1].add(pressure)

    def along_x(shift):
        return (
            flux_x[:, 3 + shift : n_x - 3 + shift, 3 : n_y - 3]
            - flux_x[:, 3 - shift : n_x - 3 - shift, 3 : n_y - 3]
        )

    def along_y(shift):
        return (
            flux_y[:, 3 : n_x - 3, 3 + shift : n_y - 3 + shift]
            - flux_y[:, 3 : n_x - 3, 3 - shift : n_y - 3 - shift]
        )

    deriv_x = (45.0 * along_x(1) - 9.0 * along_x(2) + along_x(3)) / 60.0
    deriv_y = (45.0 * along_y(1) - 9.0 * along_y(2) + along_y(3)) / 60.0
    center = inner_part(padded, 3)
    react = REACT_RATE * center[2] * (1.0 + jnp.tanh(center[3]))
    zeros = jnp.zeros_like(react)
    source = jnp.stack([zeros, zeros, -react, HEAT_RELEASE * react])
    return source - deriv_x - deriv_y


def section_tendency(state):
    padded = extended(state, (("gx", 1), ("gy", 2)), 3)
    return tendency(padded)


def per_device(fields, factor_x, factor_y):
    high = lax.Precision.HIGHEST
    section_one = fields + TIME_STEP * section_tendency(fields)
    section_two = 0.75 * fields + 0.25 * (section_one + TIME_STEP * section_tendency(section_one))
    advanced = 1.0 / 3.0 * fields + 2.0 / 3.0 * (
        section_two + TIME_STEP * section_tendency(section_two)
    )
    rank_full = factor_x.shape[1]
    count_x = lax.axis_size("gx")
    count_y = lax.axis_size("gy")
    partial_x = jnp.einsum("fxyz,xa->fayz", advanced, factor_x, precision=high)
    partial_value = lax.psum_scatter(partial_x, "gx", scatter_dimension=1, tiled=True)
    local_core = jnp.einsum("fayz,yb->fabz", partial_value, factor_y, precision=high)
    core_tensor = lax.psum_scatter(local_core, "gy", scatter_dimension=2, tiled=True)
    weights = factor_y
    columns = jnp.einsum(
        "fabz,yb->fayz",
        lax.all_gather(core_tensor, "gy", axis=2, tiled=True),
        weights,
        precision=high,
    )
    weights = factor_x
    expanded = jnp.einsum(
        "fayz,xa->fxyz", lax.all_gather(columns, "gx", axis=1, tiled=True), weights, precision=high
    )
    total_x = factor_x.shape[0] * count_x
    total_y = factor_y.shape[0] * count_y
    rescale = math.sqrt(float(total_x) * float(total_y)) / rank_full
    rebuilt = rescale * expanded
    return (advanced, core_tensor, rebuilt)


def solution(mesh):
    placed = (P(None, "gx", "gy", None), P("gx", None), P("gy", None))
    out = P(None, "gx", "gy", None)

    def whole(fields, factor_x, factor_y):
        plan = z_plan if fits(mesh, fields, factor_x, factor_y) else per_device
        return jax.shard_map(
            plan, mesh=mesh, in_specs=placed, out_specs=(out, out, out), check_vma=False
        )(fields, factor_x, factor_y)

    return whole
```

```python
import functools
import math

import jax
import jax.numpy as jnp
from jax import lax
from jax.experimental import pallas as pl
from jax.experimental.pallas import tpu as pltpu
from jax.sharding import PartitionSpec as P

TIME_STEP = 0.2
REACT_RATE = 0.5
HEAT_RELEASE = 1.0
SUBLANES = 8
LANES = 128
HALF = SUBLANES // 2


def fits(mesh, fields, factor_x, factor_y):
    n_f, n_x, n_y, n_z = fields.shape
    count_x, count_y = mesh.shape["gx"], mesh.shape["gy"]
    devices = count_x * count_y
    rank = factor_x.shape[1]
    if n_x % count_x or n_y % count_y or n_z % devices:
        return False
    block_x, block_y, block_z = n_x // count_x, n_y // count_y, n_z // devices
    return (
        n_x == LANES
        and n_z == LANES
        and n_f == HALF
        and block_z == HALF
        and block_x == 2 * SUBLANES
        and block_y == 2 * SUBLANES
        and count_x == SUBLANES
        and count_y == HALF
        and rank == count_y * SUBLANES
        and factor_y.shape[1] == rank
        and n_f * rank == LANES
    )


def digit(index, size, count):
    return lax.shift_right_logical(index, size.bit_length() - 1) & (count - 1)


def exchange(blocks, stride):
    count = len(blocks)
    period = stride * count
    group = digit(lax.broadcasted_iota(jnp.int32, (SUBLANES, LANES), 1), stride, count)
    if period == LANES:
        blocks = [pltpu.roll(b, i * stride, 1) if i else b for i, b in enumerate(blocks)]
        step = 1
        while step < count:
            taken = (group & step) != 0
            blocks = [
                jnp.where(taken, blocks[(i + step) % count], blocks[i]) for i in range(count)
            ]
            step *= 2
        blocks = [blocks[-j % count] for j in range(count)]
        return [pltpu.roll(b, LANES - j * stride, 1) if j else b for j, b in enumerate(blocks)]
    blocks = list(blocks)
    step = 1
    while step < count:
        upper = (group & step) != 0
        for i in range(count):
            if i & step:
                continue
            low, high = blocks[i], blocks[i + step]
            blocks[i] = jnp.where(upper, pltpu.roll(high, stride * step, 1), low)
            blocks[i + step] = jnp.where(upper, high, pltpu.roll(low, LANES - stride * step, 1))
        step *= 2
    return blocks


def pack_kernel(constants, fields_hbm, factor_x_hbm, factor_y_hbm, out_ref, *refs):
    *constant_refs, fields_ref, x_ref, y_ref, sems = refs
    n_f, rows, _ = fields_ref.shape
    block_x = x_ref.shape[0]
    block_y = rows // block_x
    tiles = LANES // SUBLANES
    copies = [
        pltpu.make_async_copy(fields_hbm.at[f], fields_ref.at[f], sems.at[f]) for f in range(n_f)
    ]
    copies.append(pltpu.make_async_copy(factor_x_hbm, x_ref, sems.at[n_f]))
    copies.append(pltpu.make_async_copy(factor_y_hbm, y_ref, sems.at[n_f + 1]))
    for copy in copies:
        copy.start()
    constants(*constant_refs)
    for f in range(n_f):
        if f % 2 == 0:
            copies[f].wait()
            copies[f + 1].wait()
        for octet in range(2):
            matrix = jnp.concatenate(
                [
                    fields_ref[f, pl.ds(octet * SUBLANES + y, block_x, stride=block_y), :]
                    for y in range(SUBLANES)
                ],
                axis=0,
            )
            turned = matrix.T.reshape(tiles, SUBLANES, LANES)
            for part in range(2):
                at = 2 * (2 * f + octet) + part
                out_ref[:, 0, at] = turned[:, 2 * part : 2 * part + 2]
                out_ref[:, 1, at] = turned[:, HALF + 2 * part : HALF + 2 * part + 2]
    copies[n_f].wait()
    copies[n_f + 1].wait()
    own_x = x_ref[pl.ds(lax.axis_index("gy") * HALF, HALF), :]
    own_y = y_ref[pl.ds(lax.axis_index("gx") * 2, 2), :]
    row_x = jnp.concatenate([own_x[j : j + 1] for j in range(HALF)], axis=1)
    row_y = jnp.concatenate([own_y[j % 2 : j % 2 + 1] for j in range(HALF)], axis=1)
    factors = jnp.concatenate([row_x, row_y], axis=0)
    out_ref[:, :, 4 * n_f] = jnp.broadcast_to(factors[None, None], (tiles, 2, 2, LANES))


def split(value):
    high = value.astype(jnp.bfloat16)
    low = (value - high.astype(jnp.float32)).astype(jnp.bfloat16)
    return high, low


def mul(a, b, dims=((1,), (0,))):
    return lax.dot_general(a, b, (dims, ((), ())), preferred_element_type=jnp.float32)


def mul_split(a, b, dims=((1,), (0,))):
    return mul(a[0], b[0], dims) + (mul(a[0], b[1], dims) + mul(a[1], b[0], dims))


def constants_kernel(
    n_f, count_x, count_y, rank, taps_ref, rows_x_ref, lanes_x_ref, picks_ref, rows_y_ref, lanes_y_ref
):
    row = lax.broadcasted_iota(jnp.int32, (LANES, LANES), 0)
    col = lax.broadcasted_iota(jnp.int32, (LANES, LANES), 1)
    ahead = (row - col) & (LANES - 1)
    taps = jnp.zeros((LANES, LANES), jnp.float32)
    for shift, weight in ((1, 45.0), (2, -9.0), (3, 1.0)):
        taps = jnp.where(ahead == shift, weight, taps)
        taps = jnp.where(ahead == LANES - shift, -weight, taps)
    taps = taps.astype(jnp.bfloat16)
    taps = jnp.concatenate([taps, taps], axis=0)
    taps_ref[...] = taps
    count = count_x * count_y
    plane = count_y * SUBLANES * SUBLANES
    held_at = lax.broadcasted_iota(jnp.int32, (LANES, 2 * count), 1)
    source = digit(lax.broadcasted_iota(jnp.int32, (LANES, 2 * count), 0), HALF, count)
    rows_x_ref[...] = (held_at == 2 * source).astype(jnp.bfloat16)
    lanes_x_ref[...] = (digit(row, 1, HALF) == digit(col, rank, HALF)).astype(jnp.float32)
    picks_ref[...] = (digit(row, 1, rank) == digit(col, n_f, rank)).astype(jnp.bfloat16)
    r = lax.broadcasted_iota(jnp.int32, (plane, LANES), 0)
    c = lax.broadcasted_iota(jnp.int32, (plane, LANES), 1)
    from_s = digit(r, SUBLANES * SUBLANES, count_y)
    octet, from_y = digit(r, HALF, 2), digit(r, SUBLANES, SUBLANES)
    held_at = lax.broadcasted_iota(jnp.int32, (plane, 2 * count), 1)
    source = ((octet * HALF + digit(from_y, 2, HALF)) * count_y + from_s)[:, : 2 * count]
    rows_y_ref[...] = (held_at == 2 * source + 1).astype(jnp.bfloat16)
    lanes_y_ref[0] = (digit(from_y, 1, 2) == digit(c, rank, 2)).astype(jnp.float32)
    lanes_y_ref[1] = (digit(r, 1, HALF) == digit(c, rank, HALF)).astype(jnp.float32)


def main_kernel(
    n_f, count_x, count_y, rank, rescale, in_ref,
    taps_ref, rows_x_ref, lanes_x_ref, picks_ref, rows_y_ref, lanes_y_ref, sent_hbm, spread_ref, *refs
):
    column_refs = refs[:count_y]
    ext_a, ext_b, ext_c, adv, staged, sent_ref, sent_sem = refs[count_y : count_y + 7]
    to_core_ref, from_core_ref = refs[count_y + 7 :]
    margin = 3
    inner = pl.ds(margin, SUBLANES)
    lower = lax.broadcasted_iota(jnp.int32, (margin, SUBLANES, LANES), 1) < HALF

    def each(body):
        for s in range(count_y):
            body(s)

    def fill_margins(ext):
        def one(s):
            before, after = (s - 1) % count_y, (s + 1) % count_y
            for f in range(n_f):
                old = ext[before, f, pl.ds(SUBLANES, margin)]
                own = ext[s, f, pl.ds(SUBLANES, margin)]
                ext[s, f, 0:margin] = pltpu.roll(jnp.where(lower, own, old), HALF, 1)
                own = ext[s, f, pl.ds(margin, margin)]
                new = ext[after, f, pl.ds(margin, margin)]
                ext[s, f, pl.ds(SUBLANES + margin, margin)] = pltpu.roll(
                    jnp.where(lower, new, own), HALF, 1
                )

        each(one)

    taps = taps_ref[...]

    def section(ext, step, store):
        def one(s):
            padded = [ext[s, f] for f in range(n_f)]
            center = [p[margin : margin + SUBLANES] for p in padded]
            flux_x = [center[0] * c for c in center]
            flux_x[0] = flux_x[0] + 0.5 * center[3]
            flat = jnp.concatenate(flux_x, axis=0).reshape(n_f * SUBLANES * SUBLANES, LANES)
            along_x = mul(jnp.concatenate(split(flat), axis=1), taps)
            along_x = along_x.reshape(n_f, SUBLANES, SUBLANES, LANES)
            react = (step * REACT_RATE) * center[2] * (1.0 + jnp.tanh(center[3]))
            for f in range(n_f):
                flux_y = padded[1] * padded[f]
                if f == 1:
                    flux_y = flux_y + 0.5 * padded[3]

                def along_y(k):
                    after = flux_y[margin + k : margin + k + SUBLANES]
                    return after - flux_y[margin - k : margin - k + SUBLANES]

                change = (
                    (-45.0 * step / 60.0) * along_y(1)
                    + (9.0 * step / 60.0) * along_y(2)
                    + (-step / 60.0) * (along_y(3) + along_x[f])
                )
                if f == 2:
                    change = change - react
                if f == 3:
                    change = change + HEAT_RELEASE * react
                store(s, f, center[f], change)

        each(one)

    def arrive(s):
        for f in range(n_f):
            got = [
                in_ref[i, s, 4 * f : 4 * f + 4].reshape(SUBLANES, LANES) for i in range(count_x)
            ]
            for y, block in enumerate(exchange(got, LANES // SUBLANES)):
                ext_a[s, f, margin + y] = block

    def first(s, f, center, change):
        ext_b[s, f, inner] = center + change

    def second(s, f, center, change):
        ext_c[s, f, inner] = 0.75 * ext_a[s, f, inner] + (0.25 * center + change)

    def third(s, f, center, change):
        done = (1.0 / 3.0) * ext_a[s, f, inner] + ((2.0 / 3.0) * center + change)
        adv[f, s] = done
        parts = exchange([done[y] for y in range(SUBLANES)], LANES // SUBLANES)
        for i, part in enumerate(parts):
            sent_ref[i, s, f * SUBLANES : (f + 1) * SUBLANES] = part

    plane = count_y * SUBLANES * SUBLANES
    held = in_ref[:, :, 4 * n_f].reshape(2 * count_x * count_y, LANES)
    held = split(held)
    spread_x = [mul(rows_x_ref[...], part) * lanes_x_ref[...] for part in held]
    spread_x = [mul(part.astype(jnp.bfloat16), picks_ref[...]) for part in spread_x]
    col = lax.broadcasted_iota(jnp.int32, (LANES, LANES), 1)
    weights_x = [
        jnp.concatenate(
            [jnp.where(digit(col, 1, n_f) == f, part, 0.0).astype(jnp.bfloat16) for f in range(n_f)], axis=0
        )
        for part in spread_x
    ]
    spread_y = [mul(rows_y_ref[...], part) * lanes_y_ref[0] for part in held]
    spread_y = [part + pltpu.roll(part, rank, 1) for part in spread_y]
    weights_y = [(part * lanes_y_ref[1]).astype(jnp.bfloat16) for part in spread_y]
    for part in range(2):
        spread_ref[part] = weights_x[part]
        to_core_ref[part] = weights_y[part].astype(jnp.float32).T.astype(jnp.bfloat16)
    for part in range(2):
        from_core_ref[part] = weights_y[part]

    each(arrive)
    fill_margins(ext_a)
    section(ext_a, TIME_STEP, first)
    fill_margins(ext_b)
    section(ext_b, 0.25 * TIME_STEP, second)
    fill_margins(ext_c)
    section(ext_c, 2.0 / 3.0 * TIME_STEP, third)
    sent = pltpu.make_async_copy(sent_ref, sent_hbm, sent_sem)
    sent.start()

    @pl.when(lax.axis_index("gy") >= 0)
    def tucker():
        def by_x(value):
            return jnp.concatenate([value[f].reshape(plane, LANES) for f in range(n_f)], axis=1)

        weights_x = [spread_ref[part] for part in range(2)]
        partial = split(mul_split(split(by_x(adv)), weights_x))
        core = mul_split([to_core_ref[part] for part in range(2)], partial)
        columns = rescale * mul_split([from_core_ref[part] for part in range(2)], split(core))

        block = plane // count_y
        for s in range(count_y):
            staged[s, 0:block] = columns[s * block : (s + 1) * block]
            for z in range(HALF):
                at = z * rank + s * SUBLANES
                staged[s, block + z * SUBLANES : block + (z + 1) * SUBLANES] = core[at : at + SUBLANES]
        own = lax.axis_index("gy")
        for k, ref in enumerate(column_refs):
            ref[...] = staged[lax.rem(own + k, count_y)]

    sent.wait()


def expand_kernel(n_f, count_x, count_y, spread_ref, *refs):
    in_refs, out_refs = refs[:count_y], refs[count_y : count_y + count_x]
    held, staged = refs[count_y + count_x :]
    own = lax.axis_index("gy")
    for k, ref in enumerate(in_refs):
        held[lax.rem(own + count_y - k, count_y)] = ref[...]
    block = SUBLANES * SUBLANES
    plane = count_y * block
    columns = split(jnp.concatenate([held[s, 0:block] for s in range(count_y)], axis=0))
    for f in range(n_f):
        weights = [spread_ref[part, f * LANES : (f + 1) * LANES] for part in range(2)]
        rebuilt = mul_split(columns, weights, ((1,), (1,)))
        rebuilt = rebuilt.reshape(count_y, SUBLANES, SUBLANES, LANES)
        for s in range(count_y):
            parts = exchange([rebuilt[s, y] for y in range(SUBLANES)], LANES // SUBLANES)
            for i, part in enumerate(parts):
                at = (f * count_y + s) * SUBLANES
                staged[i, at : at + SUBLANES] = part
    by_f = [
        exchange([held[s, block + z * SUBLANES : block + (z + 1) * SUBLANES] for z in range(HALF)], 1)
        for s in range(count_y)
    ]
    left = lax.broadcasted_iota(jnp.int32, (SUBLANES, LANES), 1) < LANES // 2
    by_i = []
    for f in range(n_f):
        tiles = exchange([by_f[s][f] for s in range(count_y)], HALF)
        by_i.append(exchange(tiles, LANES // SUBLANES))
    for i in range(count_x):
        for pair in range(n_f // 2):
            low, high = by_i[2 * pair][i % HALF], by_i[2 * pair + 1][i % HALF]
            if i < HALF:
                tile = jnp.where(left, low, pltpu.roll(high, LANES // 2, 1))
            else:
                tile = jnp.where(left, pltpu.roll(low, LANES // 2, 1), high)
            at = (n_f * count_y + pair) * SUBLANES
            staged[i, at : at + SUBLANES] = tile
    own = lax.axis_index("gx")
    for k, ref in enumerate(out_refs):
        ref[...] = staged[lax.rem(own + k, count_x)]


def scatter_rows(turned, octet, block_x, block_y, target, f):
    for y in range(SUBLANES):
        rows = pl.ds(octet * SUBLANES + y, block_x, stride=block_y)
        target[f, rows, :] = turned[y * block_x : (y + 1) * block_x]


def results_kernel(
    block_x, block_y, in_ref, rebuilt_ref, core_ref, advanced_hbm, rebuilt_hbm, core_hbm, advanced_ref, sems
):
    n_f = advanced_ref.shape[0]
    leaving = [
        pltpu.make_async_copy(advanced_ref.at[f], advanced_hbm.at[f], sems.at[f]) for f in range(n_f)
    ]
    leaving.append(pltpu.make_async_copy(rebuilt_ref, rebuilt_hbm, sems.at[n_f]))
    leaving.append(pltpu.make_async_copy(core_ref, core_hbm, sems.at[n_f + 1]))
    leaving[n_f].start()
    leaving[n_f + 1].start()
    for f in range(n_f):
        at = pl.ds(f * SUBLANES, SUBLANES)
        even, odd = in_ref[:, 0, at, :], in_ref[:, 1, at, :]
        lower = lax.broadcasted_iota(jnp.int32, even.shape, 1) < HALF
        first = jnp.where(lower, even, pltpu.roll(odd, HALF, 1))
        second = jnp.where(lower, pltpu.roll(even, HALF, 1), odd)
        for octet, part in enumerate((first, second)):
            turned = part.reshape(LANES, LANES).T
            scatter_rows(turned, octet, block_x, block_y, advanced_ref, f)
        leaving[f].start()
    for copy in leaving:
        copy.wait()


def rebuilt_kernel(block_x, block_y, count_x, count_y, *refs):
    in_refs, (rebuilt_ref, core_ref, held) = refs[:count_x], refs[count_x:]
    n_f = rebuilt_ref.shape[0]
    own = lax.axis_index("gx")
    for k, ref in enumerate(in_refs):
        held[lax.rem(own + count_x - k, count_x)] = ref[...]
    a_count = core_ref.shape[1]
    for pair in range(n_f // 2):
        at = (n_f * count_y + pair) * SUBLANES
        tiles = exchange([held[i, at : at + SUBLANES] for i in range(count_x)], LANES // SUBLANES)
        for place, tile in enumerate(tiles):
            core_ref[2 * pair + place // a_count, place % a_count] = tile
    pairs = count_y // 2
    lower = lax.broadcasted_iota(jnp.int32, (count_x, pairs, SUBLANES, LANES), 2) < HALF
    for f in range(n_f):
        at = pl.ds(f * count_y * SUBLANES, count_y * SUBLANES)
        tiles = held[:, at, :].reshape(count_x, pairs, 2, SUBLANES, LANES)
        even, odd = tiles[:, :, 0], tiles[:, :, 1]
        first = jnp.where(lower, even, pltpu.roll(odd, HALF, 2))
        second = jnp.where(lower, pltpu.roll(even, HALF, 2), odd)
        for octet, part in enumerate((first, second)):
            turned = part.reshape(LANES, LANES).T
            scatter_rows(turned, octet, block_x, block_y, rebuilt_ref, f)


def z_plan(fields, factor_x, factor_y):
    n_f, block_x, block_y, n_z = fields.shape
    rank = factor_x.shape[1]
    count_x = lax.axis_size("gx")
    count_y = lax.axis_size("gy")
    devices = count_x * count_y
    pairs = devices // 2
    rescale = math.sqrt(float(block_x * count_x) * float(block_y * count_y)) / rank
    vmem = pl.BlockSpec(memory_space=pltpu.VMEM)
    hbm = pl.BlockSpec(memory_space=pltpu.HBM)
    f32 = jnp.float32

    def array(shape, dtype=f32):
        return jax.ShapeDtypeStruct(shape, dtype)

    def call(
        kernel, name, outs, scratch, operands, space=vmem, out_spaces=None, limit=32 * 1024 * 1024, cost=10**9
    ):
        return pl.pallas_call(
            kernel,
            out_shape=tuple(outs),
            in_specs=[space] * len(operands),
            out_specs=out_spaces or (vmem,) * len(outs),
            scratch_shapes=scratch,
            compiler_params=pltpu.CompilerParams(vmem_limit_bytes=limit),
            cost_estimate=pl.CostEstimate(flops=cost, bytes_accessed=0, transcendentals=0),
            name=name,
        )(*operands)

    def swap(blocks):
        blocks = blocks.reshape((devices,) + blocks.shape[2:])
        return lax.all_to_all(blocks, ("gx", "gy"), 0, 0, tiled=True)

    def pass_on(blocks, axis):
        count = len(blocks)
        moved = [
            lax.ppermute(block, axis, [(i, (i + k) % count) for i in range(count)])
            for k, block in enumerate(blocks)
            if k
        ]
        return [blocks[0]] + moved

    flat = (n_f, block_x * block_y, n_z)
    plane = count_y * SUBLANES * SUBLANES
    packed, *constants = call(
        functools.partial(
            pack_kernel, functools.partial(constants_kernel, n_f, count_x, count_y, rank)
        ),
        "pack",
        [
            array((pairs, 2, 4 * n_f + 1, 2, n_z)),
            array((2 * LANES, LANES), jnp.bfloat16),
            array((LANES, 2 * devices), jnp.bfloat16),
            array((LANES, LANES)),
            array((LANES, LANES), jnp.bfloat16),
            array((plane, 2 * devices), jnp.bfloat16),
            array((2, plane, LANES)),
        ],
        [
            pltpu.VMEM(flat, f32),
            pltpu.VMEM(factor_x.shape, f32),
            pltpu.VMEM(factor_y.shape, f32),
            pltpu.SemaphoreType.DMA((n_f + 2,)),
        ],
        tuple(
            pltpu.with_memory_space_constraint(v, pltpu.HBM)
            for v in (fields.reshape(flat), factor_x, factor_y)
        ),
        space=hbm,
    )
    planes = swap(packed).reshape(count_x, count_y, 4 * n_f + 1, 2, n_z)
    extended = pltpu.VMEM((count_y, n_f, SUBLANES + 6, SUBLANES, LANES), f32)
    rows = SUBLANES * SUBLANES + HALF * SUBLANES
    plane = count_y * SUBLANES * SUBLANES
    sent, spread, *columns = call(
        functools.partial(main_kernel, n_f, count_x, count_y, rank, rescale),
        "sections",
        [
            array((count_x, count_y, n_f * SUBLANES, n_z)),
            array((2, n_f * LANES, LANES), jnp.bfloat16),
        ]
        + [array((rows, LANES))] * count_y,
        [extended] * 3
        + [
            pltpu.VMEM((n_f, count_y, SUBLANES, SUBLANES, LANES), f32),
            pltpu.VMEM((count_y, rows, LANES), f32),
            pltpu.VMEM((count_x, count_y, n_f * SUBLANES, n_z), f32),
            pltpu.SemaphoreType.DMA,
            pltpu.VMEM((2, LANES, plane), jnp.bfloat16),
            pltpu.VMEM((2, plane, LANES), jnp.bfloat16),
        ],
        (planes, *constants),
        out_spaces=(hbm,) + (vmem,) * (1 + count_y),
    )
    columns = pass_on(columns, "gy")
    sent = swap(sent).reshape(pairs, 2, n_f * SUBLANES, n_z)
    rows = (n_f * count_y + n_f // 2) * SUBLANES
    blocks = call(
        functools.partial(expand_kernel, n_f, count_x, count_y),
        "expand",
        [array((rows, LANES))] * count_x,
        [
            pltpu.VMEM((count_y,) + columns[0].shape, f32),
            pltpu.VMEM((count_x, rows, LANES), f32),
        ],
        (spread, *columns),
        cost=20000000000,
    )
    blocks = pass_on(blocks, "gx")
    core_shape = (n_f, rank // count_x, rank // count_y, n_z)
    rebuilt, core = call(
        functools.partial(rebuilt_kernel, block_x, block_y, count_x, count_y),
        "rebuilt",
        [array(flat), array(core_shape)],
        [pltpu.VMEM((count_x, rows, LANES), f32)],
        tuple(blocks),
    )
    advanced, rebuilt, core = call(
        functools.partial(results_kernel, block_x, block_y),
        "results",
        [array(flat), array(flat), array(core_shape)],
        [pltpu.VMEM(flat, f32), pltpu.SemaphoreType.DMA((n_f + 2,))],
        (sent, rebuilt, core),
        out_spaces=(hbm,) * 3,
    )
    return advanced.reshape(fields.shape), core, rebuilt.reshape(fields.shape)


def extended(block, sides, width):
    for axis, dim in sides:
        count = lax.axis_size(axis)
        forward = [(i, i + 1) for i in range(count - 1)]
        forward.append((count - 1, 0))
        backward = [(target, source) for source, target in forward]
        low = lax.ppermute(
            lax.slice_in_dim(block, block.shape[dim] - width, None, axis=dim), axis, forward
        )
        high = lax.ppermute(lax.slice_in_dim(block, 0, width, axis=dim), axis, backward)
        block = jnp.concatenate([low, block, high], axis=dim)
    return block


def inner_part(array, margin):
    return array[:, margin : array.shape[1] - margin, margin : array.shape[2] - margin]


def tendency(padded):
    n_x = padded.shape[1]
    n_y = padded.shape[2]
    pressure = 0.5 * padded[3]
    flux_x = padded[0][None] * padded
    flux_x = flux_x.at[0].add(pressure)
    flux_y = padded[1][None] * padded
    flux_y = flux_y.at[1].add(pressure)

    def along_x(shift):
        return (
            flux_x[:, 3 + shift : n_x - 3 + shift, 3 : n_y - 3]
            - flux_x[:, 3 - shift : n_x - 3 - shift, 3 : n_y - 3]
        )

    def along_y(shift):
        return (
            flux_y[:, 3 : n_x - 3, 3 + shift : n_y - 3 + shift]
            - flux_y[:, 3 : n_x - 3, 3 - shift : n_y - 3 - shift]
        )

    deriv_x = (45.0 * along_x(1) - 9.0 * along_x(2) + along_x(3)) / 60.0
    deriv_y = (45.0 * along_y(1) - 9.0 * along_y(2) + along_y(3)) / 60.0
    center = inner_part(padded, 3)
    react = REACT_RATE * center[2] * (1.0 + jnp.tanh(center[3]))
    zeros = jnp.zeros_like(react)
    source = jnp.stack([zeros, zeros, -react, HEAT_RELEASE * react])
    return source - deriv_x - deriv_y


def section_tendency(state):
    padded = extended(state, (("gx", 1), ("gy", 2)), 3)
    return tendency(padded)


def per_device(fields, factor_x, factor_y):
    high = lax.Precision.HIGHEST
    section_one = fields + TIME_STEP * section_tendency(fields)
    section_two = 0.75 * fields + 0.25 * (section_one + TIME_STEP * section_tendency(section_one))
    advanced = 1.0 / 3.0 * fields + 2.0 / 3.0 * (
        section_two + TIME_STEP * section_tendency(section_two)
    )
    rank_full = factor_x.shape[1]
    count_x = lax.axis_size("gx")
    count_y = lax.axis_size("gy")
    partial_x = jnp.einsum("fxyz,xa->fayz", advanced, factor_x, precision=high)
    partial_value = lax.psum_scatter(partial_x, "gx", scatter_dimension=1, tiled=True)
    local_core = jnp.einsum("fayz,yb->fabz", partial_value, factor_y, precision=high)
    core_tensor = lax.psum_scatter(local_core, "gy", scatter_dimension=2, tiled=True)
    weights = factor_y
    columns = jnp.einsum(
        "fabz,yb->fayz",
        lax.all_gather(core_tensor, "gy", axis=2, tiled=True),
        weights,
        precision=high,
    )
    weights = factor_x
    expanded = jnp.einsum(
        "fayz,xa->fxyz", lax.all_gather(columns, "gx", axis=1, tiled=True), weights, precision=high
    )
    total_x = factor_x.shape[0] * count_x
    total_y = factor_y.shape[0] * count_y
    rescale = math.sqrt(float(total_x) * float(total_y)) / rank_full
    rebuilt = rescale * expanded
    return (advanced, core_tensor, rebuilt)


def solution(mesh):
    placed = (P(None, "gx", "gy", None), P("gx", None), P("gy", None))
    out = P(None, "gx", "gy", None)

    def whole(fields, factor_x, factor_y):
        plan = z_plan if fits(mesh, fields, factor_x, factor_y) else per_device
        return jax.shard_map(
            plan, mesh=mesh, in_specs=placed, out_specs=(out, out, out), check_vma=False
        )(fields, factor_x, factor_y)

    return whole
```

```python
import functools
import math

import jax
import jax.numpy as jnp
from jax import lax
from jax.experimental import pallas as pl
from jax.experimental.pallas import tpu as pltpu
from jax.sharding import PartitionSpec as P

TIME_STEP = 0.2
REACT_RATE = 0.5
HEAT_RELEASE = 1.0
SUBLANES = 8
LANES = 128
HALF = SUBLANES // 2


def fits(mesh, fields, factor_x, factor_y):
    n_f, n_x, n_y, n_z = fields.shape
    count_x, count_y = mesh.shape["gx"], mesh.shape["gy"]
    devices = count_x * count_y
    rank = factor_x.shape[1]
    if n_x % count_x or n_y % count_y or n_z % devices:
        return False
    block_x, block_y, block_z = n_x // count_x, n_y // count_y, n_z // devices
    return (
        n_x == LANES
        and n_z == LANES
        and n_f == HALF
        and block_z == HALF
        and block_x == 2 * SUBLANES
        and block_y == 2 * SUBLANES
        and count_x == SUBLANES
        and count_y == HALF
        and rank == count_y * SUBLANES
        and factor_y.shape[1] == rank
        and n_f * rank == LANES
    )


def digit(index, size, count):
    return lax.shift_right_logical(index, size.bit_length() - 1) & (count - 1)


def exchange(blocks, stride):
    count = len(blocks)
    period = stride * count
    group = digit(lax.broadcasted_iota(jnp.int32, (SUBLANES, LANES), 1), stride, count)
    if period == LANES:
        blocks = [pltpu.roll(b, i * stride, 1) if i else b for i, b in enumerate(blocks)]
        step = 1
        while step < count:
            taken = (group & step) != 0
            blocks = [
                jnp.where(taken, blocks[(i + step) % count], blocks[i]) for i in range(count)
            ]
            step *= 2
        blocks = [blocks[-j % count] for j in range(count)]
        return [pltpu.roll(b, LANES - j * stride, 1) if j else b for j, b in enumerate(blocks)]
    blocks = list(blocks)
    step = 1
    while step < count:
        upper = (group & step) != 0
        for i in range(count):
            if i & step:
                continue
            low, high = blocks[i], blocks[i + step]
            blocks[i] = jnp.where(upper, pltpu.roll(high, stride * step, 1), low)
            blocks[i + step] = jnp.where(upper, high, pltpu.roll(low, LANES - stride * step, 1))
        step *= 2
    return blocks


def pack_kernel(constants, fields_hbm, factor_x_hbm, factor_y_hbm, out_ref, *refs):
    *constant_refs, fields_ref, x_ref, y_ref, sems = refs
    n_f, rows, _ = fields_ref.shape
    block_x = x_ref.shape[0]
    block_y = rows // block_x
    tiles = LANES // SUBLANES
    copies = [
        pltpu.make_async_copy(fields_hbm.at[f], fields_ref.at[f], sems.at[f]) for f in range(n_f)
    ]
    copies.append(pltpu.make_async_copy(factor_x_hbm, x_ref, sems.at[n_f]))
    copies.append(pltpu.make_async_copy(factor_y_hbm, y_ref, sems.at[n_f + 1]))
    for copy in copies:
        copy.start()
    constants(*constant_refs)
    for f in range(n_f):
        if f % 2 == 0:
            copies[f].wait()
            copies[f + 1].wait()
        for octet in range(2):
            matrix = jnp.concatenate(
                [
                    fields_ref[f, pl.ds(octet * SUBLANES + y, block_x, stride=block_y), :]
                    for y in range(SUBLANES)
                ],
                axis=0,
            )
            turned = matrix.T.reshape(tiles, SUBLANES, LANES)
            for part in range(2):
                at = 2 * (2 * f + octet) + part
                out_ref[:, 0, at] = turned[:, 2 * part : 2 * part + 2]
                out_ref[:, 1, at] = turned[:, HALF + 2 * part : HALF + 2 * part + 2]
    copies[n_f].wait()
    copies[n_f + 1].wait()
    own_x = x_ref[pl.ds(lax.axis_index("gy") * HALF, HALF), :]
    own_y = y_ref[pl.ds(lax.axis_index("gx") * 2, 2), :]
    row_x = jnp.concatenate([own_x[j : j + 1] for j in range(HALF)], axis=1)
    row_y = jnp.concatenate([own_y[j % 2 : j % 2 + 1] for j in range(HALF)], axis=1)
    factors = jnp.concatenate([row_x, row_y], axis=0)
    out_ref[:, :, 4 * n_f] = jnp.broadcast_to(factors[None, None], (tiles, 2, 2, LANES))


def split(value):
    high = value.astype(jnp.bfloat16)
    low = (value - high.astype(jnp.float32)).astype(jnp.bfloat16)
    return high, low


def mul(a, b, dims=((1,), (0,))):
    return lax.dot_general(a, b, (dims, ((), ())), preferred_element_type=jnp.float32)


def mul_split(a, b, dims=((1,), (0,))):
    return mul(a[0], b[0], dims) + (mul(a[0], b[1], dims) + mul(a[1], b[0], dims))


def constants_kernel(
    n_f, count_x, count_y, rank, taps_ref, rows_x_ref, lanes_x_ref, picks_ref, rows_y_ref, lanes_y_ref
):
    row = lax.broadcasted_iota(jnp.int32, (LANES, LANES), 0)
    col = lax.broadcasted_iota(jnp.int32, (LANES, LANES), 1)
    ahead = (row - col) & (LANES - 1)
    taps = jnp.zeros((LANES, LANES), jnp.float32)
    for shift, weight in ((1, 45.0), (2, -9.0), (3, 1.0)):
        taps = jnp.where(ahead == shift, weight, taps)
        taps = jnp.where(ahead == LANES - shift, -weight, taps)
    taps = taps.astype(jnp.bfloat16)
    taps = jnp.concatenate([taps, taps], axis=0)
    taps_ref[...] = taps
    count = count_x * count_y
    plane = count_y * SUBLANES * SUBLANES
    held_at = lax.broadcasted_iota(jnp.int32, (LANES, 2 * count), 1)
    source = digit(lax.broadcasted_iota(jnp.int32, (LANES, 2 * count), 0), HALF, count)
    rows_x_ref[...] = (held_at == 2 * source).astype(jnp.bfloat16)
    lanes_x_ref[...] = (digit(row, 1, HALF) == digit(col, rank, HALF)).astype(jnp.float32)
    picks_ref[...] = (digit(row, 1, rank) == digit(col, n_f, rank)).astype(jnp.bfloat16)
    r = lax.broadcasted_iota(jnp.int32, (plane, LANES), 0)
    c = lax.broadcasted_iota(jnp.int32, (plane, LANES), 1)
    from_s = digit(r, SUBLANES * SUBLANES, count_y)
    octet, from_y = digit(r, HALF, 2), digit(r, SUBLANES, SUBLANES)
    held_at = lax.broadcasted_iota(jnp.int32, (plane, 2 * count), 1)
    source = ((octet * HALF + digit(from_y, 2, HALF)) * count_y + from_s)[:, : 2 * count]
    rows_y_ref[...] = (held_at == 2 * source + 1).astype(jnp.bfloat16)
    lanes_y_ref[0] = (digit(from_y, 1, 2) == digit(c, rank, 2)).astype(jnp.float32)
    lanes_y_ref[1] = (digit(r, 1, HALF) == digit(c, rank, HALF)).astype(jnp.float32)


def main_kernel(
    n_f, count_x, count_y, rank, rescale, in_ref,
    taps_ref, rows_x_ref, lanes_x_ref, picks_ref, rows_y_ref, lanes_y_ref, sent_hbm, spread_ref, *refs
):
    column_refs = refs[:count_y]
    ext_a, ext_b, ext_c, adv, staged, sent_ref, sent_sem = refs[count_y : count_y + 7]
    to_core_ref, from_core_ref = refs[count_y + 7 :]
    margin = 3
    inner = pl.ds(margin, SUBLANES)
    lower = lax.broadcasted_iota(jnp.int32, (margin, SUBLANES, LANES), 1) < HALF

    def each(body):
        for s in range(count_y):
            body(s)

    def fill_margins(ext):
        def one(s):
            before, after = (s - 1) % count_y, (s + 1) % count_y
            for f in range(n_f):
                old = ext[before, f, pl.ds(SUBLANES, margin)]
                own = ext[s, f, pl.ds(SUBLANES, margin)]
                ext[s, f, 0:margin] = pltpu.roll(jnp.where(lower, own, old), HALF, 1)
                own = ext[s, f, pl.ds(margin, margin)]
                new = ext[after, f, pl.ds(margin, margin)]
                ext[s, f, pl.ds(SUBLANES + margin, margin)] = pltpu.roll(
                    jnp.where(lower, new, own), HALF, 1
                )

        each(one)

    taps = taps_ref[...]

    def section(ext, step, store):
        def one(s):
            padded = [ext[s, f] for f in range(n_f)]
            center = [p[margin : margin + SUBLANES] for p in padded]
            flux_x = [center[0] * c for c in center]
            flux_x[0] = flux_x[0] + 0.5 * center[3]
            flat = jnp.concatenate(flux_x, axis=0).reshape(n_f * SUBLANES * SUBLANES, LANES)
            along_x = mul(jnp.concatenate(split(flat), axis=1), taps)
            along_x = along_x.reshape(n_f, SUBLANES, SUBLANES, LANES)
            react = (step * REACT_RATE) * center[2] * (1.0 + jnp.tanh(center[3]))
            for f in range(n_f):
                flux_y = padded[1] * padded[f]
                if f == 1:
                    flux_y = flux_y + 0.5 * padded[3]

                def along_y(k):
                    after = flux_y[margin + k : margin + k + SUBLANES]
                    return after - flux_y[margin - k : margin - k + SUBLANES]

                change = (
                    (-45.0 * step / 60.0) * along_y(1)
                    + (9.0 * step / 60.0) * along_y(2)
                    + (-step / 60.0) * (along_y(3) + along_x[f])
                )
                if f == 2:
                    change = change - react
                if f == 3:
                    change = change + HEAT_RELEASE * react
                store(s, f, center[f], change)

        each(one)

    def arrive(s):
        for f in range(n_f):
            got = [
                in_ref[i, s, 4 * f : 4 * f + 4].reshape(SUBLANES, LANES) for i in range(count_x)
            ]
            for y, block in enumerate(exchange(got, LANES // SUBLANES)):
                ext_a[s, f, margin + y] = block

    def first(s, f, center, change):
        ext_b[s, f, inner] = center + change

    def second(s, f, center, change):
        ext_c[s, f, inner] = 0.75 * ext_a[s, f, inner] + (0.25 * center + change)

    def third(s, f, center, change):
        done = (1.0 / 3.0) * ext_a[s, f, inner] + ((2.0 / 3.0) * center + change)
        adv[f, s] = done
        parts = exchange([done[y] for y in range(SUBLANES)], LANES // SUBLANES)
        for i, part in enumerate(parts):
            sent_ref[i, s, 2 * f : 2 * f + 2] = part.reshape(2, HALF, LANES)

    plane = count_y * SUBLANES * SUBLANES
    held = in_ref[:, :, 4 * n_f].reshape(2 * count_x * count_y, LANES)
    held = split(held)
    spread_x = [mul(rows_x_ref[...], part) * lanes_x_ref[...] for part in held]
    spread_x = [mul(part.astype(jnp.bfloat16), picks_ref[...]) for part in spread_x]
    col = lax.broadcasted_iota(jnp.int32, (LANES, LANES), 1)
    weights_x = [
        jnp.concatenate(
            [jnp.where(digit(col, 1, n_f) == f, part, 0.0).astype(jnp.bfloat16) for f in range(n_f)], axis=0
        )
        for part in spread_x
    ]
    spread_y = [mul(rows_y_ref[...], part) * lanes_y_ref[0] for part in held]
    spread_y = [part + pltpu.roll(part, rank, 1) for part in spread_y]
    weights_y = [(part * lanes_y_ref[1]).astype(jnp.bfloat16) for part in spread_y]
    for part in range(2):
        spread_ref[part] = weights_x[part]
        to_core_ref[part] = weights_y[part].astype(jnp.float32).T.astype(jnp.bfloat16)
    for part in range(2):
        from_core_ref[part] = weights_y[part]

    each(arrive)
    fill_margins(ext_a)
    section(ext_a, TIME_STEP, first)
    fill_margins(ext_b)
    section(ext_b, 0.25 * TIME_STEP, second)
    fill_margins(ext_c)
    section(ext_c, 2.0 / 3.0 * TIME_STEP, third)
    sent = pltpu.make_async_copy(sent_ref, sent_hbm, sent_sem)
    sent.start()

    @pl.when(lax.axis_index("gy") >= 0)
    def tucker():
        def by_x(value):
            return jnp.concatenate([value[f].reshape(plane, LANES) for f in range(n_f)], axis=1)

        weights_x = [spread_ref[part] for part in range(2)]
        partial = split(mul_split(split(by_x(adv)), weights_x))
        core = mul_split([to_core_ref[part] for part in range(2)], partial)
        columns = rescale * mul_split([from_core_ref[part] for part in range(2)], split(core))

        block = plane // count_y
        for s in range(count_y):
            staged[s, 0:block] = columns[s * block : (s + 1) * block]
            for z in range(HALF):
                at = z * rank + s * SUBLANES
                staged[s, block + z * SUBLANES : block + (z + 1) * SUBLANES] = core[at : at + SUBLANES]
        own = lax.axis_index("gy")
        for k, ref in enumerate(column_refs):
            ref[...] = staged[lax.rem(own + k, count_y)]

    sent.wait()


def expand_kernel(n_f, count_x, count_y, spread_ref, *refs):
    in_refs, out_refs = refs[:count_y], refs[count_y : count_y + count_x]
    held, staged = refs[count_y + count_x :]
    own = lax.axis_index("gy")
    for k, ref in enumerate(in_refs):
        held[lax.rem(own + count_y - k, count_y)] = ref[...]
    block = SUBLANES * SUBLANES
    plane = count_y * block
    columns = split(jnp.concatenate([held[s, 0:block] for s in range(count_y)], axis=0))
    for f in range(n_f):
        weights = [spread_ref[part, f * LANES : (f + 1) * LANES] for part in range(2)]
        rebuilt = mul_split(columns, weights, ((1,), (1,)))
        rebuilt = rebuilt.reshape(count_y, SUBLANES, SUBLANES, LANES)
        for s in range(count_y):
            parts = exchange([rebuilt[s, y] for y in range(SUBLANES)], LANES // SUBLANES)
            for i, part in enumerate(parts):
                at = (f * count_y + s) * SUBLANES
                staged[i, at : at + SUBLANES] = part
    by_f = [
        exchange([held[s, block + z * SUBLANES : block + (z + 1) * SUBLANES] for z in range(HALF)], 1)
        for s in range(count_y)
    ]
    left = lax.broadcasted_iota(jnp.int32, (SUBLANES, LANES), 1) < LANES // 2
    by_i = []
    for f in range(n_f):
        tiles = exchange([by_f[s][f] for s in range(count_y)], HALF)
        by_i.append(exchange(tiles, LANES // SUBLANES))
    for i in range(count_x):
        for pair in range(n_f // 2):
            low, high = by_i[2 * pair][i % HALF], by_i[2 * pair + 1][i % HALF]
            if i < HALF:
                tile = jnp.where(left, low, pltpu.roll(high, LANES // 2, 1))
            else:
                tile = jnp.where(left, pltpu.roll(low, LANES // 2, 1), high)
            at = (n_f * count_y + pair) * SUBLANES
            staged[i, at : at + SUBLANES] = tile
    own = lax.axis_index("gx")
    for k, ref in enumerate(out_refs):
        ref[...] = staged[lax.rem(own + k, count_x)]


def scatter_rows(turned, octet, block_x, block_y, target, f):
    for y in range(SUBLANES):
        rows = pl.ds(octet * SUBLANES + y, block_x, stride=block_y)
        target[f, rows, :] = turned[y * block_x : (y + 1) * block_x]


def results_kernel(
    block_x, block_y, in_ref, rebuilt_ref, core_ref, advanced_hbm, rebuilt_hbm, core_hbm, advanced_ref, sems
):
    n_f = advanced_ref.shape[0]
    leaving = [
        pltpu.make_async_copy(advanced_ref.at[f], advanced_hbm.at[f], sems.at[f]) for f in range(n_f)
    ]
    leaving.append(pltpu.make_async_copy(rebuilt_ref, rebuilt_hbm, sems.at[n_f]))
    leaving.append(pltpu.make_async_copy(core_ref, core_hbm, sems.at[n_f + 1]))
    leaving[n_f].start()
    leaving[n_f + 1].start()
    def turn(f):
        for octet in range(2):
            place = 2 * f + octet
            matrix = jnp.concatenate([in_ref[:, 0, place], in_ref[:, 1, place]], axis=1)
            turned = matrix.reshape(LANES, LANES).T
            scatter_rows(turned, octet, block_x, block_y, advanced_ref, f)
        leaving[f].start()

    for f in range(n_f):
        pl.when(lax.axis_index("gy") >= 0)(functools.partial(turn, f))
    for copy in leaving:
        copy.wait()


def rebuilt_kernel(block_x, block_y, count_x, count_y, *refs):
    in_refs, (rebuilt_ref, core_ref, held) = refs[:count_x], refs[count_x:]
    n_f = rebuilt_ref.shape[0]
    own = lax.axis_index("gx")
    for k, ref in enumerate(in_refs):
        held[lax.rem(own + count_x - k, count_x)] = ref[...]
    a_count = core_ref.shape[1]
    for pair in range(n_f // 2):
        at = (n_f * count_y + pair) * SUBLANES
        tiles = exchange([held[i, at : at + SUBLANES] for i in range(count_x)], LANES // SUBLANES)
        for place, tile in enumerate(tiles):
            core_ref[2 * pair + place // a_count, place % a_count] = tile
    pairs = count_y // 2
    lower = lax.broadcasted_iota(jnp.int32, (count_x, pairs, SUBLANES, LANES), 2) < HALF
    for f in range(n_f):
        at = pl.ds(f * count_y * SUBLANES, count_y * SUBLANES)
        tiles = held[:, at, :].reshape(count_x, pairs, 2, SUBLANES, LANES)
        even, odd = tiles[:, :, 0], tiles[:, :, 1]
        first = jnp.where(lower, even, pltpu.roll(odd, HALF, 2))
        second = jnp.where(lower, pltpu.roll(even, HALF, 2), odd)
        for octet, part in enumerate((first, second)):
            turned = part.reshape(LANES, LANES).T
            scatter_rows(turned, octet, block_x, block_y, rebuilt_ref, f)


def z_plan(fields, factor_x, factor_y):
    n_f, block_x, block_y, n_z = fields.shape
    rank = factor_x.shape[1]
    count_x = lax.axis_size("gx")
    count_y = lax.axis_size("gy")
    devices = count_x * count_y
    pairs = devices // 2
    rescale = math.sqrt(float(block_x * count_x) * float(block_y * count_y)) / rank
    vmem = pl.BlockSpec(memory_space=pltpu.VMEM)
    hbm = pl.BlockSpec(memory_space=pltpu.HBM)
    f32 = jnp.float32

    def array(shape, dtype=f32):
        return jax.ShapeDtypeStruct(shape, dtype)

    def call(
        kernel, name, outs, scratch, operands, space=vmem, out_spaces=None, limit=32 * 1024 * 1024, cost=10**9
    ):
        return pl.pallas_call(
            kernel,
            out_shape=tuple(outs),
            in_specs=[space] * len(operands),
            out_specs=out_spaces or (vmem,) * len(outs),
            scratch_shapes=scratch,
            compiler_params=pltpu.CompilerParams(vmem_limit_bytes=limit),
            cost_estimate=pl.CostEstimate(flops=cost, bytes_accessed=0, transcendentals=0),
            name=name,
        )(*operands)

    def swap(blocks):
        blocks = blocks.reshape((devices,) + blocks.shape[2:])
        return lax.all_to_all(blocks, ("gx", "gy"), 0, 0, tiled=True)

    def pass_on(blocks, axis):
        count = len(blocks)
        moved = [
            lax.ppermute(block, axis, [(i, (i + k) % count) for i in range(count)])
            for k, block in enumerate(blocks)
            if k
        ]
        return [blocks[0]] + moved

    flat = (n_f, block_x * block_y, n_z)
    plane = count_y * SUBLANES * SUBLANES
    packed, *constants = call(
        functools.partial(
            pack_kernel, functools.partial(constants_kernel, n_f, count_x, count_y, rank)
        ),
        "pack",
        [
            array((pairs, 2, 4 * n_f + 1, 2, n_z)),
            array((2 * LANES, LANES), jnp.bfloat16),
            array((LANES, 2 * devices), jnp.bfloat16),
            array((LANES, LANES)),
            array((LANES, LANES), jnp.bfloat16),
            array((plane, 2 * devices), jnp.bfloat16),
            array((2, plane, LANES)),
        ],
        [
            pltpu.VMEM(flat, f32),
            pltpu.VMEM(factor_x.shape, f32),
            pltpu.VMEM(factor_y.shape, f32),
            pltpu.SemaphoreType.DMA((n_f + 2,)),
        ],
        tuple(
            pltpu.with_memory_space_constraint(v, pltpu.HBM)
            for v in (fields.reshape(flat), factor_x, factor_y)
        ),
        space=hbm,
    )
    planes = swap(packed).reshape(count_x, count_y, 4 * n_f + 1, 2, n_z)
    extended = pltpu.VMEM((count_y, n_f, SUBLANES + 6, SUBLANES, LANES), f32)
    rows = SUBLANES * SUBLANES + HALF * SUBLANES
    plane = count_y * SUBLANES * SUBLANES
    sent, spread, *columns = call(
        functools.partial(main_kernel, n_f, count_x, count_y, rank, rescale),
        "sections",
        [
            array((count_x, count_y, 2 * n_f, HALF, n_z)),
            array((2, n_f * LANES, LANES), jnp.bfloat16),
        ]
        + [array((rows, LANES))] * count_y,
        [extended] * 3
        + [
            pltpu.VMEM((n_f, count_y, SUBLANES, SUBLANES, LANES), f32),
            pltpu.VMEM((count_y, rows, LANES), f32),
            pltpu.VMEM((count_x, count_y, 2 * n_f, HALF, n_z), f32),
            pltpu.SemaphoreType.DMA,
            pltpu.VMEM((2, LANES, plane), jnp.bfloat16),
            pltpu.VMEM((2, plane, LANES), jnp.bfloat16),
        ],
        (planes, *constants),
        out_spaces=(hbm,) + (vmem,) * (1 + count_y),
    )
    columns = pass_on(columns, "gy")
    sent = swap(sent).reshape(pairs, 2, 2 * n_f, HALF, n_z)
    rows = (n_f * count_y + n_f // 2) * SUBLANES
    blocks = call(
        functools.partial(expand_kernel, n_f, count_x, count_y),
        "expand",
        [array((rows, LANES))] * count_x,
        [
            pltpu.VMEM((count_y,) + columns[0].shape, f32),
            pltpu.VMEM((count_x, rows, LANES), f32),
        ],
        (spread, *columns),
        cost=20000000000,
    )
    blocks = pass_on(blocks, "gx")
    core_shape = (n_f, rank // count_x, rank // count_y, n_z)
    rebuilt, core = call(
        functools.partial(rebuilt_kernel, block_x, block_y, count_x, count_y),
        "rebuilt",
        [array(flat), array(core_shape)],
        [pltpu.VMEM((count_x, rows, LANES), f32)],
        tuple(blocks),
    )
    advanced, rebuilt, core = call(
        functools.partial(results_kernel, block_x, block_y),
        "results",
        [array(flat), array(flat), array(core_shape)],
        [pltpu.VMEM(flat, f32), pltpu.SemaphoreType.DMA((n_f + 2,))],
        (sent, rebuilt, core),
        out_spaces=(hbm,) * 3,
    )
    return advanced.reshape(fields.shape), core, rebuilt.reshape(fields.shape)


def extended(block, sides, width):
    for axis, dim in sides:
        count = lax.axis_size(axis)
        forward = [(i, i + 1) for i in range(count - 1)]
        forward.append((count - 1, 0))
        backward = [(target, source) for source, target in forward]
        low = lax.ppermute(
            lax.slice_in_dim(block, block.shape[dim] - width, None, axis=dim), axis, forward
        )
        high = lax.ppermute(lax.slice_in_dim(block, 0, width, axis=dim), axis, backward)
        block = jnp.concatenate([low, block, high], axis=dim)
    return block


def inner_part(array, margin):
    return array[:, margin : array.shape[1] - margin, margin : array.shape[2] - margin]


def tendency(padded):
    n_x = padded.shape[1]
    n_y = padded.shape[2]
    pressure = 0.5 * padded[3]
    flux_x = padded[0][None] * padded
    flux_x = flux_x.at[0].add(pressure)
    flux_y = padded[1][None] * padded
    flux_y = flux_y.at[1].add(pressure)

    def along_x(shift):
        return (
            flux_x[:, 3 + shift : n_x - 3 + shift, 3 : n_y - 3]
            - flux_x[:, 3 - shift : n_x - 3 - shift, 3 : n_y - 3]
        )

    def along_y(shift):
        return (
            flux_y[:, 3 : n_x - 3, 3 + shift : n_y - 3 + shift]
            - flux_y[:, 3 : n_x - 3, 3 - shift : n_y - 3 - shift]
        )

    deriv_x = (45.0 * along_x(1) - 9.0 * along_x(2) + along_x(3)) / 60.0
    deriv_y = (45.0 * along_y(1) - 9.0 * along_y(2) + along_y(3)) / 60.0
    center = inner_part(padded, 3)
    react = REACT_RATE * center[2] * (1.0 + jnp.tanh(center[3]))
    zeros = jnp.zeros_like(react)
    source = jnp.stack([zeros, zeros, -react, HEAT_RELEASE * react])
    return source - deriv_x - deriv_y


def section_tendency(state):
    padded = extended(state, (("gx", 1), ("gy", 2)), 3)
    return tendency(padded)


def per_device(fields, factor_x, factor_y):
    high = lax.Precision.HIGHEST
    section_one = fields + TIME_STEP * section_tendency(fields)
    section_two = 0.75 * fields + 0.25 * (section_one + TIME_STEP * section_tendency(section_one))
    advanced = 1.0 / 3.0 * fields + 2.0 / 3.0 * (
        section_two + TIME_STEP * section_tendency(section_two)
    )
    rank_full = factor_x.shape[1]
    count_x = lax.axis_size("gx")
    count_y = lax.axis_size("gy")
    partial_x = jnp.einsum("fxyz,xa->fayz", advanced, factor_x, precision=high)
    partial_value = lax.psum_scatter(partial_x, "gx", scatter_dimension=1, tiled=True)
    local_core = jnp.einsum("fayz,yb->fabz", partial_value, factor_y, precision=high)
    core_tensor = lax.psum_scatter(local_core, "gy", scatter_dimension=2, tiled=True)
    weights = factor_y
    columns = jnp.einsum(
        "fabz,yb->fayz",
        lax.all_gather(core_tensor, "gy", axis=2, tiled=True),
        weights,
        precision=high,
    )
    weights = factor_x
    expanded = jnp.einsum(
        "fayz,xa->fxyz", lax.all_gather(columns, "gx", axis=1, tiled=True), weights, precision=high
    )
    total_x = factor_x.shape[0] * count_x
    total_y = factor_y.shape[0] * count_y
    rescale = math.sqrt(float(total_x) * float(total_y)) / rank_full
    rebuilt = rescale * expanded
    return (advanced, core_tensor, rebuilt)


def solution(mesh):
    placed = (P(None, "gx", "gy", None), P("gx", None), P("gy", None))
    out = P(None, "gx", "gy", None)

    def whole(fields, factor_x, factor_y):
        plan = z_plan if fits(mesh, fields, factor_x, factor_y) else per_device
        return jax.shard_map(
            plan, mesh=mesh, in_specs=placed, out_specs=(out, out, out), check_vma=False
        )(fields, factor_x, factor_y)

    return whole
```
